128 devices in a mesh: dp: 32 (over x, z, y_hi), tensor: 4 (over y_lo, core).
Axes of the slice: x: 4, y: 4 (y_hi: 2, y_lo: 2; y = y_hi * 2 + y_lo), z: 4, core: 2. Of those that a mesh axis runs over, the one named last changes fastest.
Arguments:
- tokens: bfloat16 [16384, 2048], P(('dp', 'tensor')), may hold values from -6 to 6
- group_length: int32 [32], P('dp'), may hold values from 385 to 512, as said below
- forget_rate: float32 [8], P('tensor'), may hold values from 0.00048828125 to 0.05
- mixer_gain: float32 [2048], replicated, may hold values from 0.1 to 1.9
- feed_gain: float32 [2048], replicated, may hold values from 0.1 to 1.9
- group_gain: float32 [3456], P('tensor'), may hold values from 0.1 to 1.9
- w_query: bfloat16 [2048, 2048], P('dp', 'tensor'), may hold values from -0.125 to 0.125
- w_key: bfloat16 [2048, 2048], P('dp', 'tensor'), may hold values from -0.125 to 0.125
- w_value: bfloat16 [2048, 3456], P('dp', 'tensor'), may hold values from -0.125 to 0.125
- w_swish: bfloat16 [2048, 3456], P('dp', 'tensor'), may hold values from -0.125 to 0.125
- w_output: bfloat16 [3456, 2048], P('tensor', 'dp'), may hold values from -0.109375 to 0.109375
- w_gelu: bfloat16 [2048, 3456], P('dp', 'tensor'), may hold values from -0.125 to 0.125
- w_linear: bfloat16 [2048, 3456], P('dp', 'tensor'), may hold values from -0.125 to 0.125
- w_down: bfloat16 [3456, 2048], P('tensor', 'dp'), may hold values from -0.109375 to 0.109375
- cotangent: bfloat16 [16384, 2048], P(('dp', 'tensor')), may hold values from -6 to 6
Outputs:
- result: bfloat16 [16384, 2048], P(('dp', 'tensor'))
- grad_tokens: bfloat16 [16384, 2048], P(('dp', 'tensor'))
- grad_mixer_gain: float32 [2048], replicated
- grad_feed_gain: float32 [2048], replicated
- grad_group_gain: float32 [3456], P('tensor')
- grad_query: float32 [2048, 2048], P('dp', 'tensor')
- grad_key: float32 [2048, 2048], P('dp', 'tensor')
- grad_value: float32 [2048, 3456], P('dp', 'tensor')
- grad_swish: float32 [2048, 3456], P('dp', 'tensor')
- grad_output: float32 [3456, 2048], P('tensor', 'dp')
- grad_gelu: float32 [2048, 3456], P('dp', 'tensor')
- grad_linear: float32 [2048, 3456], P('dp', 'tensor')
- grad_down: float32 [3456, 2048], P('tensor', 'dp')
The draws below stay inside these ranges and needn't reach their ends.
Inputs may be any that keep to these rules, and one draw needn't show every extreme that they name: The first group_length[g] rows of data group g form one sequence, the other rows are padding; some group fills all 512 rows.
All inputs are finite; a program needn't handle non-finite values.
Results may differ from the reference program's by a relative error of at most 0.03.
Values may be sent and summed in bfloat16 or wider, within the bound.
No kernel may reach another device: no remote copies, remote signals or barrier semaphores. Data moves between devices by JAX's collectives and lax.ppermute only.
A program may use at most 192 MiB of HBM per device.

```python
import math
import jax
import jax.numpy as jnp
from jax import lax

D = 2048
H = 8
DK = 256
DV = 432
FF = 3456
KD = 2048
VD = 3456
CAP = 512
GROUPS = 32
TOKENS = 16384
QBLK = 512


def draw_group_length(key, part):
    key = jax.random.fold_in(key, 11)
    lengths = jax.random.randint(jax.random.fold_in(key, 1), (GROUPS,), 3 * CAP // 4 + 1, CAP + 1)
    chosen = jax.random.randint(jax.random.fold_in(key, 2), (), 0, GROUPS)
    return jnp.where(jnp.arange(GROUPS, dtype=jnp.int32) == chosen, CAP, lengths).astype(jnp.int32)


def block_levels(key, shape, split, least, largest):
    level = 1.0
    for position, blocks in split:
        draws = jax.random.uniform(jax.random.fold_in(jax.random.fold_in(key, 6), position), (blocks,), jnp.float32, least / len(split), largest / len(split))
        level = level * jnp.repeat(jnp.exp(draws), shape[position] // blocks).reshape((-1,) + (1,) * (len(shape) - 1 - position))
    return level


def scatter_about(key, shape, width, bound, pieces=(), kind=jnp.bfloat16):
    gain = block_levels(key, shape, pieces, -0.22, 0.18) if pieces else 1.0
    entries = jax.random.normal(key, shape, jnp.float32) * width * gain
    return jnp.minimum(jnp.maximum(entries, -bound), bound).astype(kind)


def setup_inputs(seed: int = 0) -> dict:
    keys = jax.random.split(jax.random.key(seed), 16)
    tokens = scatter_about(keys[0], (TOKENS, D), 1.0, 6.0, ((0, 128),))
    group_length = draw_group_length(jax.random.fold_in(keys[15], 71), 0)
    forget_rate = jnp.clip(jnp.exp(math.log(0.05) - 4.6288867 * jax.random.uniform(keys[2], (H,), jnp.float32) ** block_levels(keys[2], (H,), ((0, 4),), -0.2, 0.2)), 0.00048828125, 0.05)
    mixer_gain = jnp.clip(1.0 + 0.18 * jax.random.normal(keys[3], (D,), jnp.float32), 0.1, 1.9)
    feed_gain = jnp.clip(1.0 + 0.18 * jax.random.normal(keys[4], (D,), jnp.float32), 0.1, 1.9)
    group_gain = jnp.clip(1.0 + 0.18 * jax.random.normal(keys[5], (VD,), jnp.float32), 0.1, 1.9)
    w_query = scatter_about(keys[6], (D, KD), D ** -0.5, 0.125, ((0, 32), (1, 4)))
    w_key = scatter_about(keys[7], (D, KD), D ** -0.5, 0.125, ((0, 32), (1, 4)))
    w_value = scatter_about(keys[8], (D, VD), D ** -0.5, 0.125, ((0, 32), (1, 4)))
    w_swish = scatter_about(keys[9], (D, VD), D ** -0.5, 0.125, ((0, 32), (1, 4)))
    w_output = scatter_about(keys[10], (VD, D), VD ** -0.5, 0.109375, ((0, 4), (1, 32)))
    w_gelu = scatter_about(keys[11], (D, FF), D ** -0.5, 0.125, ((0, 32), (1, 4)))
    w_linear = scatter_about(keys[12], (D, FF), D ** -0.5, 0.125, ((0, 32), (1, 4)))
    w_down = scatter_about(keys[13], (FF, D), FF ** -0.5, 0.109375, ((0, 4), (1, 32)))
    cotangent = scatter_about(keys[14], (TOKENS, D), 1.0, 6.0, ((0, 128),))
    return {"tokens": tokens, "group_length": group_length, "forget_rate": forget_rate, "mixer_gain": mixer_gain, "feed_gain": feed_gain, "group_gain": group_gain, "w_query": w_query, "w_key": w_key, "w_value": w_value, "w_swish": w_swish, "w_output": w_output, "w_gelu": w_gelu, "w_linear": w_linear, "w_down": w_down, "cotangent": cotangent}


@jax.custom_vjp
def low(v):
    return lax.optimization_barrier(v.astype(jnp.bfloat16)).astype(jnp.float32)

@jax.custom_vjp
def low_back(v):
    return v

def low_keep(v):
    return (low(v), None)

def low_pass(kept, grad):
    return (grad,)

def back_keep(v):
    return (v, None)

def back_low(kept, grad):
    return (low(grad),)
low.defvjp(low_keep, low_pass)
low_back.defvjp(back_keep, back_low)
norm_eps = 1e-05
group_eps = 1.0
highest = lax.Precision.HIGHEST

def matmul(left_in, right_in):
    return jnp.dot(left_in, right_in, precision=highest, preferred_element_type=jnp.float32)

def rms_scale(row_data, gain_vec):
    return row_data * lax.rsqrt(lax.optimization_barrier(jnp.mean(row_data * row_data, axis=-1, keepdims=True)) + norm_eps) * gain_vec

def decay_mask(log_keep, first_row, query_rows, key_count):
    row_ids = first_row + lax.broadcasted_iota(jnp.int32, (query_rows, key_count), 0)
    col_ids = lax.broadcasted_iota(jnp.int32, (query_rows, key_count), 1)
    offset_rows = row_ids - col_ids
    distance = jnp.maximum(offset_rows, 0).astype(jnp.float32)
    return jnp.where(offset_rows[None] >= 0, jnp.exp(distance[None] * log_keep[:, None, None]), 0.0)

def retention(queries, key_rows, values, log_keep):
    block_count = CAP // QBLK
    blocks = queries.reshape(block_count, QBLK, H, DK)
    starts = jnp.arange(block_count, dtype=jnp.int32) * QBLK

    def one_block(item_pair):
        query_block, first_row = item_pair
        raw_scores = low_back(jnp.einsum('ihd,jhd->hij', query_block, key_rows, precision=highest))
        weighting = decay_mask(log_keep, first_row, QBLK, CAP)
        weights = low(raw_scores * DK ** (-0.5) * weighting)
        return jnp.einsum('hij,jhe->ihe', weights, values, precision=highest)
    outputs = lax.map(jax.checkpoint(one_block), (blocks, starts))
    return outputs.reshape(CAP, H, DV)

def layer(tokens, params, log_keep, valid_rows):
    mixer_gain, feed_gain, group_gain, w_query, w_key, w_value, w_swish, w_output, w_gelu, w_linear, w_down = params
    normed_in = low(rms_scale(tokens, mixer_gain))
    queries = low(low_back(matmul(normed_in, w_query))).reshape(CAP, H, DK)
    key_rows = low(low_back(matmul(normed_in, w_key))).reshape(CAP, H, DK)
    values = low(low_back(matmul(normed_in, w_value))).reshape(CAP, H, DV)
    gate_pre = low_back(matmul(normed_in, w_swish))
    retained = low_back(retention(queries, key_rows, values, log_keep))
    center = retained - lax.optimization_barrier(jnp.mean(retained, axis=-1, keepdims=True))
    spread = lax.optimization_barrier(jnp.mean(center * center, axis=-1, keepdims=True))
    normed = (center * lax.rsqrt(spread + group_eps)).reshape(CAP, VD)
    mixed_low = low(jax.nn.silu(gate_pre) * normed * group_gain)
    mixer_out = low_back(matmul(mixed_low, w_output))
    middle = tokens + valid_rows * mixer_out
    normed_mid = low(rms_scale(middle, feed_gain))
    gelu_in = low_back(matmul(normed_mid, w_gelu))
    linear_in = low_back(matmul(normed_mid, w_linear))
    hidden = low(jax.nn.gelu(gelu_in, approximate=False) * linear_in)
    feed_out = low_back(matmul(hidden, w_down))
    return middle + valid_rows * feed_out

def reference(tokens, group_length, forget_rate, mixer_gain, feed_gain, group_gain, w_query, w_key, w_value, w_swish, w_output, w_gelu, w_linear, w_down, cotangent):
    params = tuple((weight_arr.astype(jnp.float32) for weight_arr in (mixer_gain, feed_gain, group_gain, w_query, w_key, w_value, w_swish, w_output, w_gelu, w_linear, w_down)))
    log_keep = jnp.log1p(-forget_rate.astype(jnp.float32))
    inputs = tokens.astype(jnp.float32).reshape(GROUPS, CAP, D)
    grads_in = cotangent.astype(jnp.float32).reshape(GROUPS, CAP, D)
    positions = jnp.arange(CAP, dtype=jnp.int32)[:, None]

    def one_group(carried, item_triple):
        group_in, group_grad, length = item_triple
        valid_rows = (positions < length).astype(jnp.float32)

        def apply_layer(layer_in, *layer_params):
            return layer(layer_in, layer_params, log_keep, valid_rows)
        output, pullback = jax.vjp(apply_layer, group_in, *params)
        gradients = pullback(group_grad)
        summed = jax.tree.map(jnp.add, carried, tuple(gradients[1:]))
        return (summed, (output, gradients[0]))
    zero_grads = tuple((jnp.zeros_like(weight_arr) for weight_arr in params))
    totals, (outputs, grad_rows) = lax.scan(one_group, zero_grads, (inputs, grads_in, group_length))
    return (outputs.reshape(TOKENS, D).astype(jnp.bfloat16), grad_rows.reshape(TOKENS, D).astype(jnp.bfloat16), totals[0], totals[1], totals[2], totals[3], totals[4], totals[5], totals[6], totals[7], totals[8], totals[9], totals[10])
```

```python
import jax
import jax.numpy as jnp
from jax import lax
from jax.sharding import PartitionSpec as P

norm_eps = 1e-05
group_eps = 1.0
AXES = ("dp", "tensor")
f32 = jnp.float32
bf16 = jnp.bfloat16
NT = (((1,), (1,)), ((), ()))
TN = (((0,), (0,)), ((), ()))


def device_index(x, z, y, c):
    return ((x * 4 + z) * 2 + y // 2) * 4 + (y % 2) * 2 + c


def xor_pairs(dx=0, dz=0, dy=0, dc=0):
    return [
        (device_index(x, z, y, c), device_index(x ^ dx, z ^ dz, y ^ dy, c ^ dc))
        for x in range(4)
        for z in range(4)
        for y in range(4)
        for c in range(2)
    ]


X1, X2, X3 = (xor_pairs(dx=d) for d in (1, 2, 3))
Z1, Z2, Z3 = (xor_pairs(dz=d) for d in (1, 2, 3))
Y1, Y2, Y3 = (xor_pairs(dy=d) for d in (1, 2, 3))
C1 = xor_pairs(dc=1)
PLANES = [
    [device_index(x, z, y, c) for x in range(4) for z in range(4)]
    for y in range(4)
    for c in range(2)
]


def move(value, pairs):
    return lax.ppermute(value, AXES, pairs)


def tie(*values):
    return lax.optimization_barrier(values)


def gather_plane(shard):
    half = shard.shape[0] // 32 * 16
    a, b = shard[:half], shard[half:]
    ha, hb = a.shape[0] // 32 * 16, b.shape[0] // 32 * 16
    a1, a3, b1, b3 = tie(move(a, X1), move(a, X3), move(b, Z1), move(b, Z3))
    a2p, a2q, b2p, b2q = tie(
        move(a3[:ha], X1), move(a1[ha:], X3), move(b3[:hb], Z1), move(b1[hb:], Z3)
    )
    a2, b2 = jnp.concatenate([a2p, a2q]), jnp.concatenate([b2p, b2q])
    sa, sb = jnp.stack([a, a1, a2, a3]), jnp.stack([b, b1, b2, b3])
    sa, sb = tie(sa, sb)
    sa1, sa3, sb1, sb3 = tie(move(sa, Z1), move(sa, Z3), move(sb, X1), move(sb, X3))
    sa2p, sa2q, sb2p, sb2q = tie(
        move(sa3[:2], Z1), move(sa1[2:], Z3), move(sb3[:2], X1), move(sb1[2:], X3)
    )
    sa2, sb2 = jnp.concatenate([sa2p, sa2q]), jnp.concatenate([sb2p, sb2q])
    va = (sa, sa1, sa2, sa3)
    vb = (sb, sb1, sb2, sb3)
    return [
        jnp.concatenate([va[dz][dx], vb[dx][dz]]) for dx in range(4) for dz in range(4)
    ]


def add_low(*terms):
    total = terms[0].astype(f32)
    for term in terms[1:]:
        total = total + term.astype(f32)
    return total.astype(bf16)


def scatter_plane(grad):
    rows = grad.shape[0]
    half = rows // 32 * 16
    blocks = [grad[:, 128 * j : 128 * j + 128] for j in range(16)]
    a = [jnp.stack([blocks[4 * dx + dz][:half] for dx in range(4)]) for dz in range(4)]
    b = [jnp.stack([blocks[4 * dx + dz][half:] for dz in range(4)]) for dx in range(4)]
    ap, aq, bp, bq = tie(
        move(a[2][:2], Z1), move(a[2][2:], Z3), move(b[2][:2], X1), move(b[2][2:], X3)
    )
    a3 = jnp.concatenate([add_low(a[3][:2], ap), a[3][2:]])
    a1 = jnp.concatenate([a[1][:2], add_low(a[1][2:], aq)])
    b3 = jnp.concatenate([add_low(b[3][:2], bp), b[3][2:]])
    b1 = jnp.concatenate([b[1][:2], add_low(b[1][2:], bq)])
    a3, a1, b3, b1 = tie(a3, a1, b3, b1)
    r3, r1, s3, s1 = tie(move(a3, Z3), move(a1, Z1), move(b3, X3), move(b1, X1))
    a, b = add_low(a[0], r3, r1), add_low(b[0], s3, s1)
    a, b = tie(a, b)
    ha, hb = a.shape[1] // 32 * 16, b.shape[1] // 32 * 16
    ap, aq, bp, bq = tie(
        move(a[2][:ha], X1), move(a[2][ha:], X3), move(b[2][:hb], Z1), move(b[2][hb:], Z3)
    )
    a3 = jnp.concatenate([add_low(a[3][:ha], ap), a[3][ha:]])
    a1 = jnp.concatenate([a[1][:ha], add_low(a[1][ha:], aq)])
    b3 = jnp.concatenate([add_low(b[3][:hb], bp), b[3][hb:]])
    b1 = jnp.concatenate([b[1][:hb], add_low(b[1][hb:], bq)])
    a3, a1, b3, b1 = tie(a3, a1, b3, b1)
    r3, r1, s3, s1 = tie(move(a3, X3), move(a1, X1), move(b3, Z3), move(b1, Z1))
    top = a[0].astype(f32) + r3.astype(f32) + r1.astype(f32)
    low = b[0].astype(f32) + s3.astype(f32) + s1.astype(f32)
    return jnp.concatenate([top, low])


def gather_line(own):
    half = own.shape[0] // 2
    r1, r3 = tie(move(own, Y1), move(own, Y3))
    mine = jnp.concatenate([own, r1])
    mine = jnp.concatenate([mine, move(mine, C1)])
    r2 = jnp.concatenate([move(r3[:half], Y1), move(r1[half:], Y3)])
    other = jnp.concatenate([r2, r3])
    other = jnp.concatenate([other, move(other, C1)])
    return mine, other


def scatter_line(mine, other):
    rows = mine.shape[0] // 4
    half = rows // 2
    o = other[: 2 * rows] + move(other[2 * rows :].astype(bf16), C1).astype(f32)
    s2 = o[:rows].astype(bf16)
    t3, t1 = tie(move(s2[:half], Y1), move(s2[half:], Y3))
    m = mine[: 2 * rows] + move(mine[2 * rows :].astype(bf16), C1).astype(f32)
    s3 = jnp.concatenate([o[rows : rows + half] + t3.astype(f32), o[rows + half :]]).astype(bf16)
    s1 = jnp.concatenate([m[rows : rows + half], m[rows + half :] + t1.astype(f32)]).astype(bf16)
    u3, u1 = tie(move(s3, Y3), move(s1, Y1))
    return m[:rows] + u3.astype(f32) + u1.astype(f32)


def shards(
    tokens,
    group_length,
    forget_rate,
    mixer_gain,
    feed_gain,
    group_gain,
    w_query,
    w_key,
    w_value,
    w_swish,
    w_output,
    w_gelu,
    w_linear,
    w_down,
    cotangent,
):
    rows, width = tokens.shape
    dp = lax.axis_index("dp")
    tensor = lax.axis_index("tensor")
    plane = dp // 2
    high = dp % 2
    is_low = high == 0
    wide = w_value.shape[1] // 2
    kwide = w_query.shape[1] // 2
    score_scale = kwide ** (-0.5)
    log_keep = jnp.log1p(-jnp.where(is_low, forget_rate[0], forget_rate[1]))
    valid_rows = (tensor * rows + lax.broadcasted_iota(jnp.int32, (rows, 1), 0) < group_length[0]).astype(f32)
    relative = jnp.bitwise_xor(plane, jnp.arange(16, dtype=jnp.int32))

    def to_relative(value):
        parts = [lax.dynamic_slice_in_dim(value, relative[j] * 128, 128, value.ndim - 1) for j in range(16)]
        return jnp.concatenate(parts, axis=-1)

    def from_relative(value):
        return to_relative(value)

    def halves(parts):
        return [
            (
                jnp.where(is_low, part[:, : part.shape[1] // 2], part[:, part.shape[1] // 2 :]),
                jnp.where(is_low, part[:, part.shape[1] // 2 :], part[:, : part.shape[1] // 2]),
            )
            for part in parts
        ]

    def padded(parts):
        return jnp.concatenate(
            [jnp.pad(p, ((0, 0), (0, -p.shape[1] % 128))) for p in parts], axis=1
        )

    def trade(parts):
        pairs = halves(parts)
        keep, send = padded([p[0] for p in pairs]), padded([p[1] for p in pairs])
        got = move(send, Y2)
        both = jnp.where(is_low, jnp.concatenate([keep, got]), jnp.concatenate([got, keep])).T
        out, place = [], 0
        for part in parts:
            size = part.shape[1] // 2
            out.append(both[place : place + size])
            place += size + (-size % 128)
        return jnp.concatenate(out)

    first = trade([w_query, w_key, w_value, w_swish])
    second = trade([w_output.T, w_gelu, w_linear, w_down.T])

    token_float = to_relative(tokens).astype(f32)
    grad_result = to_relative(cotangent).astype(f32)
    mixer_rel = to_relative(mixer_gain)
    feed_rel = to_relative(feed_gain)
    group_own = jnp.where(is_low, group_gain[:wide], group_gain[wide:])

    r1 = lax.rsqrt(jnp.mean(token_float * token_float, axis=-1, keepdims=True) + norm_eps)
    normed_in = (token_float * r1 * mixer_rel).astype(bf16)
    normed_group = jnp.concatenate(gather_line(normed_in))

    first_full = jnp.concatenate(gather_plane(first), axis=1)
    wq, wk = first_full[:kwide], first_full[kwide : 2 * kwide]
    wv, ws = first_full[2 * kwide : 2 * kwide + wide], first_full[2 * kwide + wide :]
    second_full = lax.all_gather(second, AXES, axis_index_groups=PLANES, axis=0, tiled=False)
    second_full = jnp.concatenate(
        [lax.dynamic_index_in_dim(second_full, relative[j], 0, keepdims=False) for j in range(16)],
        axis=1,
    )
    wo, wg, wl, wd = (second_full[i * wide : (i + 1) * wide] for i in range(4))

    def dot(left, right, dims=(((1,), (0,)), ((), ()))):
        return lax.dot_general(left, right, dims, preferred_element_type=f32)

    group_rows = 4 * rows
    q = dot(normed_group, wq, NT).astype(bf16).reshape(2, group_rows, kwide)
    k = dot(normed_group, wk, NT).astype(bf16).reshape(2, group_rows, kwide)
    v = dot(normed_group, wv, NT).astype(bf16).reshape(2, group_rows, wide)
    gate_pre = dot(normed_group, ws, NT)

    order = jnp.array([0, 2, 1, 3], jnp.int32)
    starts = jnp.bitwise_xor(tensor, order) * rows
    position = (starts[:, None] + jnp.arange(rows, dtype=jnp.int32)[None]).reshape(-1)
    offset = position[:, None] - position[None]
    decay = jnp.where(
        offset >= 0, jnp.exp(jnp.maximum(offset, 0).astype(f32) * log_keep) * score_scale, 0.0
    )
    scores = jnp.einsum("gid,gjd->gij", q, k, preferred_element_type=f32)
    weights = (scores * decay).astype(bf16)
    retained = jnp.einsum("gij,gje->gie", weights, v, preferred_element_type=f32).reshape(-1, wide)
    center = retained - jnp.mean(retained, axis=-1, keepdims=True)
    rstd = lax.rsqrt(jnp.mean(center * center, axis=-1, keepdims=True) + group_eps)
    normed = center * rstd
    sig = jax.nn.sigmoid(gate_pre)
    silu = gate_pre * sig
    mixed_low = (silu * normed * group_own).astype(bf16)
    mixer_part = dot(mixed_low, wo)
    mixer_out = scatter_line(mixer_part[:group_rows], mixer_part[group_rows:])
    middle = token_float + valid_rows * mixer_out
    r2 = lax.rsqrt(jnp.mean(middle * middle, axis=-1, keepdims=True) + norm_eps)
    normed_mid = (middle * r2 * feed_rel).astype(bf16)
    mid_group = jnp.concatenate(gather_line(normed_mid))
    gelu_in = dot(mid_group, wg, NT)
    linear_in = dot(mid_group, wl, NT)
    cdf = 0.5 * (1.0 + lax.erf(gelu_in * (0.5**0.5)))
    gelu = gelu_in * cdf
    gelu_slope = cdf + gelu_in * jnp.exp(-0.5 * gelu_in * gelu_in) * 0.3989422804014327
    hidden = (gelu * linear_in).astype(bf16)
    feed_part = dot(hidden, wd)

    grad_feed_out = (valid_rows * grad_result).astype(bf16)
    grad_feed_group = jnp.concatenate(gather_line(grad_feed_out))
    grad_hidden = dot(grad_feed_group, wd, NT)
    grad_gelu_in = (grad_hidden * linear_in * gelu_slope).astype(bf16)
    grad_linear_in = (grad_hidden * gelu).astype(bf16)
    mid_part = dot(grad_gelu_in, wg) + dot(grad_linear_in, wl)
    grad_normed_mid = scatter_line(mid_part[:group_rows], mid_part[group_rows:])
    grad_ffn = jnp.concatenate(
        [
            dot(grad_gelu_in, mid_group, TN).astype(bf16),
            dot(grad_linear_in, mid_group, TN).astype(bf16),
            dot(hidden, grad_feed_group, TN).astype(bf16),
        ]
    )
    feed_out = scatter_line(feed_part[:group_rows], feed_part[group_rows:])
    result = (middle + valid_rows * feed_out).astype(bf16)

    part_feed_gain = jnp.sum(grad_normed_mid * middle * r2, axis=0)
    z2 = grad_normed_mid * feed_rel
    grad_middle = (
        grad_result + r2 * z2 - middle * (r2 * r2 * r2) * jnp.mean(z2 * middle, axis=-1, keepdims=True)
    )
    grad_mixer_out = (valid_rows * grad_middle).astype(bf16)
    grad_mixer_group = jnp.concatenate(gather_line(grad_mixer_out))
    grad_mixed = dot(grad_mixer_group, wo, NT)
    grad_output = dot(mixed_low, grad_mixer_group, TN).astype(bf16)
    grad_gate_pre = (
        grad_mixed * normed * group_own * (sig * (1.0 + gate_pre * (1.0 - sig)))
    ).astype(bf16)
    part_group_gain = jnp.sum(grad_mixed * silu * normed, axis=0)
    y = grad_mixed * silu * group_own
    grad_retained = (
        rstd * (y - jnp.mean(y, axis=-1, keepdims=True))
        - center * (rstd * rstd * rstd) * jnp.mean(y * center, axis=-1, keepdims=True)
    ).astype(bf16).reshape(2, group_rows, wide)
    grad_scores = (
        jnp.einsum("gie,gje->gij", grad_retained, v, preferred_element_type=f32) * decay
    ).astype(bf16)
    gq = jnp.einsum("gij,gjd->gid", grad_scores, k, preferred_element_type=f32).astype(bf16)
    gk = jnp.einsum("gij,gid->gjd", grad_scores, q, preferred_element_type=f32).astype(bf16)
    gv = jnp.einsum("gij,gie->gje", weights, grad_retained, preferred_element_type=f32).astype(bf16)
    gq, gk, gv = gq.reshape(-1, kwide), gk.reshape(-1, kwide), gv.reshape(-1, wide)
    in_part = dot(gq, wq) + dot(gk, wk) + dot(gv, wv) + dot(grad_gate_pre, ws)
    grad_normed_in = scatter_line(in_part[:group_rows], in_part[group_rows:])
    grad_attn = jnp.concatenate(
        [
            dot(gq, normed_group, TN).astype(bf16),
            dot(gk, normed_group, TN).astype(bf16),
            dot(gv, normed_group, TN).astype(bf16),
            dot(grad_gate_pre, normed_group, TN).astype(bf16),
        ]
    )
    part_mixer_gain = jnp.sum(grad_normed_in * token_float * r1, axis=0)
    z1 = grad_normed_in * mixer_rel
    grad_tokens = (
        grad_middle + r1 * z1 - token_float * (r1 * r1 * r1) * jnp.mean(z1 * token_float, axis=-1, keepdims=True)
    ).astype(bf16)
    result = from_relative(result)
    grad_tokens = from_relative(grad_tokens)

    late = jnp.concatenate([grad_output, grad_attn])
    late_sum = scatter_plane(late).astype(bf16)
    early = jnp.stack(
        [lax.dynamic_slice_in_dim(grad_ffn, relative[j] * 128, 128, 1) for j in range(16)]
    )
    early_sum = lax.psum_scatter(
        early, AXES, axis_index_groups=PLANES, scatter_dimension=0, tiled=False
    )

    def settle(summed, sizes):
        flat = jnp.concatenate(
            [
                jnp.pad(p, ((0, -p.shape[0] % 128), (0, 0)))
                for p in (summed[a : a + n] for a, n in sizes)
            ]
        ).T
        half = flat.shape[0] // 2
        keep = jnp.where(is_low, flat[:half], flat[half:])
        send = jnp.where(is_low, flat[half:], flat[:half])
        got = move(send, Y2)
        out, place = [], 0
        for _, n in sizes:
            own, far = keep[:, place : place + n], got[:, place : place + n]
            out.append(
                jnp.where(
                    is_low,
                    jnp.concatenate([own, far], axis=1),
                    jnp.concatenate([far, own], axis=1),
                ).astype(f32)
            )
            place += n + (-n % 128)
        return out

    g_gelu, g_linear, g_down = settle(early_sum, [(0, wide), (wide, wide), (2 * wide, wide)])
    g_output, g_query, g_key, g_value, g_swish = settle(
        late_sum,
        [
            (0, wide),
            (wide, kwide),
            (wide + kwide, kwide),
            (wide + 2 * kwide, wide),
            (2 * wide + 2 * kwide, wide),
        ],
    )

    def butterfly(value, *steps):
        for pairs in steps:
            value = value + move(value, pairs)
        return value

    feed_sum = butterfly(from_relative(part_feed_gain), C1, Y1, Y2, X1, X2, Z1, Z2)
    mixer_sum = butterfly(from_relative(part_mixer_gain), C1, Y1, Y2, X1, X2, Z1, Z2)
    group_half = butterfly(part_group_gain, X1, X2, Z1, Z2)
    group_far = move(group_half, Y2)
    group_sum = jnp.where(
        is_low,
        jnp.concatenate([group_half, group_far]),
        jnp.concatenate([group_far, group_half]),
    )
    return (
        result,
        grad_tokens,
        mixer_sum,
        feed_sum,
        group_sum,
        g_query,
        g_key,
        g_value,
        g_swish,
        g_output.T,
        g_gelu,
        g_linear,
        g_down.T,
    )


def solution(mesh):
    return jax.shard_map(
        shards,
        mesh=mesh,
        in_specs=(
            P(("dp", "tensor"), None),
            P("dp"),
            P("tensor"),
            P(),
            P(),
            P("tensor"),
            P("dp", "tensor"),
            P("dp", "tensor"),
            P("dp", "tensor"),
            P("dp", "tensor"),
            P("tensor", "dp"),
            P("dp", "tensor"),
            P("dp", "tensor"),
            P("tensor", "dp"),
            P(("dp", "tensor"), None),
        ),
        out_specs=(
            P(("dp", "tensor"), None),
            P(("dp", "tensor"), None),
            P(),
            P(),
            P("tensor"),
            P("dp", "tensor"),
            P("dp", "tensor"),
            P("dp", "tensor"),
            P("dp", "tensor"),
            P("tensor", "dp"),
            P("dp", "tensor"),
            P("dp", "tensor"),
            P("tensor", "dp"),
        ),
        check_vma=False,
    )
```

```python
import functools

import jax
import jax.numpy as jnp
from jax import lax
from jax.experimental import pallas as pl
from jax.experimental.pallas import tpu as pltpu
from jax.sharding import PartitionSpec as P

norm_eps = 1e-05
group_eps = 1.0
AXES = ("dp", "tensor")
f32 = jnp.float32
bf16 = jnp.bfloat16
NN = (((1,), (0,)), ((), ()))
NT = (((1,), (1,)), ((), ()))
TN = (((0,), (0,)), ((), ()))
MB = 1 << 20
VMEM = pl.BlockSpec(memory_space=pltpu.VMEM)
ANY = pl.BlockSpec(memory_space=pl.ANY)


def device_index(x, z, y, c):
    return ((x * 4 + z) * 2 + y // 2) * 4 + (y % 2) * 2 + c


def xor_pairs(dx=0, dz=0, dy=0, dc=0):
    return [
        (device_index(x, z, y, c), device_index(x ^ dx, z ^ dz, y ^ dy, c ^ dc))
        for x in range(4)
        for z in range(4)
        for y in range(4)
        for c in range(2)
    ]


X1, X2, X3 = (xor_pairs(dx=d) for d in (1, 2, 3))
Z1, Z2, Z3 = (xor_pairs(dz=d) for d in (1, 2, 3))
Y1, Y2, Y3 = (xor_pairs(dy=d) for d in (1, 2, 3))
C1 = xor_pairs(dc=1)
PLANES = [
    [device_index(x, z, y, c) for x in range(4) for z in range(4)]
    for y in range(4)
    for c in range(2)
]


def move(value, pairs):
    return lax.ppermute(value, AXES, pairs)


def tie(*values):
    return lax.optimization_barrier(values)


def dot(left, right, dims=NN):
    return lax.dot_general(left, right, dims, preferred_element_type=f32)


def params(mb):
    return pltpu.CompilerParams(vmem_limit_bytes=mb * MB)


def up128(n):
    return n + (-n % 128)


def stacked(*parts):
    return jnp.concatenate(parts, axis=0)


def split_kernel(q_ref, k_ref, o_ref, v_ref, s_ref, g_ref, l_ref, d_ref, keep_ref, send_ref, pack_ref):
    low = lax.axis_index("dp") % 2 == 0
    place = 0
    for ref in (q_ref, k_ref, o_ref, v_ref, s_ref):
        half = ref.shape[1] // 2
        left, right = ref[:, :half], ref[:, half:]
        keep_ref[:, place : place + half] = jnp.where(low, left, right)
        send_ref[:, place : place + half] = jnp.where(low, right, left)
        place += up128(half)
    place = 0
    for ref in (g_ref, l_ref, d_ref):
        pack_ref[:, place : place + ref.shape[1]] = ref[...]
        place += up128(ref.shape[1])


def split_weights(mixer, feed):
    size = sum(up128(w.shape[1] // 2) for w in mixer)
    pack = sum(up128(w.shape[1]) for w in feed)
    return pl.pallas_call(
        split_kernel,
        out_shape=(
            jax.ShapeDtypeStruct((64, size), bf16),
            jax.ShapeDtypeStruct((64, size), bf16),
            jax.ShapeDtypeStruct((64, pack), bf16),
        ),
        compiler_params=params(48),
    )(*mixer, *feed)


def join_kernel(groups, keep_ref, got_ref, *out_refs):
    low = lax.axis_index("dp") % 2 == 0
    place = 0
    for sizes, out_ref in zip(groups, out_refs):
        row = 0
        for size in sizes:
            wide = up128(size)
            keep, got = keep_ref[:, place : place + wide], got_ref[:, place : place + wide]
            both = stacked(jnp.where(low, keep, got), jnp.where(low, got, keep))
            out_ref[row : row + size, :] = both.T[:size]
            place += wide
            row += size


def join_weights(keep, got, *groups):
    out = pl.pallas_call(
        functools.partial(join_kernel, groups),
        out_shape=tuple(jax.ShapeDtypeStruct((sum(sizes), 128), bf16) for sizes in groups),
        compiler_params=params(16),
    )(keep, got)
    return out


def arrange_kernel(*refs):
    va, vb, out_ref, sems = refs[:4], refs[4:8], refs[8], refs[9]
    plane = lax.axis_index("dp") // 2
    ra, rb = va[0].shape[1], vb[0].shape[1]
    copies = []
    for dx in range(4):
        for dz in range(4):
            j = 4 * dx + dz
            lanes = pl.ds(pl.multiple_of(jnp.bitwise_xor(j, plane) * 128, 128), 128)
            copies.append(
                pltpu.make_async_copy(va[dz].at[dx], out_ref.at[pl.ds(0, ra), lanes], sems.at[2 * j])
            )
            copies.append(
                pltpu.make_async_copy(
                    vb[dx].at[dz], out_ref.at[pl.ds(ra, rb), lanes], sems.at[2 * j + 1]
                )
            )
    for copy in copies:
        copy.start()
    for copy in copies:
        copy.wait()


def gather_plane(a, b, later):
    ha, hb = a.shape[0] // 32 * 16, b.shape[0] // 32 * 16
    a1, a3, b1, b3 = tie(move(a, X1), move(a, X3), move(b, Z1), move(b, Z3))
    a2p, a2q, b2p, b2q = tie(
        move(a3[:ha], X1), move(a1[ha:], X3), move(b3[:hb], Z1), move(b1[hb:], Z3)
    )
    a2, b2 = stacked(a2p, a2q), stacked(b2p, b2q)
    sa, sb, later = tie(jnp.stack([a, a1, a2, a3]), jnp.stack([b, b1, b2, b3]), later)
    sa1, sa3, sb1, sb3 = tie(move(sa, Z1), move(sa, Z3), move(sb, X1), move(sb, X3))
    sa2p, sa2q, sb2p, sb2q = tie(
        move(sa3[:2], Z1), move(sa1[2:], Z3), move(sb3[:2], X1), move(sb1[2:], X3)
    )
    sa2, sb2 = stacked(sa2p, sa2q), stacked(sb2p, sb2q)
    full = pl.pallas_call(
        arrange_kernel,
        out_shape=jax.ShapeDtypeStruct((a.shape[0] + b.shape[0], 2048), bf16),
        in_specs=[ANY] * 8,
        out_specs=ANY,
        scratch_shapes=[pltpu.SemaphoreType.DMA((32,))],
        compiler_params=params(4),
    )(sa, sa1, sa2, sa3, sb, sb1, sb2, sb3)
    return full, later


def widen_kernel(in_ref, out_ref, sems):
    rows = out_ref.shape[0]
    copies = [
        pltpu.make_async_copy(
            in_ref.at[pl.ds(j * rows, rows), :], out_ref.at[:, pl.ds(128 * j, 128)], sems.at[j]
        )
        for j in range(16)
    ]
    for copy in copies:
        copy.start()
    for copy in copies:
        copy.wait()


def widen(blocks):
    rows = blocks.shape[0] // 16
    return pl.pallas_call(
        widen_kernel,
        out_shape=jax.ShapeDtypeStruct((rows, 2048), bf16),
        in_specs=[ANY],
        out_specs=ANY,
        scratch_shapes=[pltpu.SemaphoreType.DMA((16,))],
        compiler_params=params(4),
    )(blocks)


def add_low(*terms):
    total = terms[0].astype(f32)
    for term in terms[1:]:
        total = total + term.astype(f32)
    return total.astype(bf16)


def scatter_plane(a, b):
    ap, aq, bp, bq = tie(
        move(a[2, :2], Z1), move(a[2, 2:], Z3), move(b[2, :2], X1), move(b[2, 2:], X3)
    )
    a3 = stacked(add_low(a[3, :2], ap), a[3, 2:])
    a1 = stacked(a[1, :2], add_low(a[1, 2:], aq))
    b3 = stacked(add_low(b[3, :2], bp), b[3, 2:])
    b1 = stacked(b[1, :2], add_low(b[1, 2:], bq))
    a3, a1, b3, b1 = tie(a3, a1, b3, b1)
    r3, r1, s3, s1 = tie(move(a3, Z3), move(a1, Z1), move(b3, X3), move(b1, X1))
    a, b = add_low(a[0], r3, r1), add_low(b[0], s3, s1)
    a, b = tie(a, b)
    ha, hb = a.shape[1] // 32 * 16, b.shape[1] // 32 * 16
    ap, aq, bp, bq = tie(
        move(a[2, :ha], X1), move(a[2, ha:], X3), move(b[2, :hb], Z1), move(b[2, hb:], Z3)
    )
    a3 = stacked(add_low(a[3, :ha], ap), a[3, ha:])
    a1 = stacked(a[1, :ha], add_low(a[1, ha:], aq))
    b3 = stacked(add_low(b[3, :hb], bp), b[3, hb:])
    b1 = stacked(b[1, :hb], add_low(b[1, hb:], bq))
    a3, a1, b3, b1 = tie(a3, a1, b3, b1)
    r3, r1, s3, s1 = tie(move(a3, X3), move(a1, X1), move(b3, Z3), move(b1, Z1))
    return add_low(a[0], r3, r1), add_low(b[0], s3, s1)


def early_kernel(gelu_ref, linear_ref, hidden_ref, mid_ref, feed_ref, out_ref, left_ref, down_ref):
    wide = gelu_ref.shape[1]

    @pl.when(pl.program_id(0) == 0)
    def _():
        left_ref[:wide, :] = gelu_ref[...].T
        left_ref[wide:, :] = linear_ref[...].T
        down_ref[...] = hidden_ref[...].T

    up = jnp.dot(left_ref[...], mid_ref[...], preferred_element_type=f32).astype(bf16)
    down = jnp.dot(down_ref[...], feed_ref[...], preferred_element_type=f32).astype(bf16)
    for i in range(2):
        lanes = slice(128 * i, 128 * i + 128)
        out_ref[i, : 2 * wide, :] = up[:, lanes]
        out_ref[i, 2 * wide :, :] = down[:, lanes]


def early_gradients(gelu, linear, hidden, mid, feed):
    rows, wide = gelu.shape
    whole = pl.BlockSpec((rows, wide), lambda i: (0, 0))
    block = pl.BlockSpec((rows, 256), lambda i: (0, i))
    return pl.pallas_call(
        early_kernel,
        grid=(8,),
        out_shape=jax.ShapeDtypeStruct((16, 3 * wide, 128), bf16),
        in_specs=[whole, whole, whole, block, block],
        out_specs=pl.BlockSpec((2, 3 * wide, 128), lambda i: (i, 0, 0)),
        scratch_shapes=[pltpu.VMEM((2 * wide, rows), bf16), pltpu.VMEM((wide, rows), bf16)],
        compiler_params=params(32),
    )(gelu, linear, hidden, mid, feed)


def late_kernel(
    plane_ref, q_ref, k_ref, v_ref, s_ref, o_ref, x_ref, m_ref, w_ref, a_ref, b_ref, gain_ref, left_ref, out_left
):
    kwide, wide = q_ref.shape[1], v_ref.shape[1]
    keys = 2 * kwide

    @pl.when(pl.program_id(0) == 0)
    def _():
        left_ref[:kwide, :] = q_ref[...].T
        left_ref[kwide:keys, :] = k_ref[...].T
        left_ref[keys : keys + wide, :] = v_ref[...].T
        left_ref[keys + wide :, :] = s_ref[...].T
        out_left[...] = o_ref[...].T

    odd = plane_ref[0] % 2 == 1
    main = jnp.dot(left_ref[...], x_ref[...], preferred_element_type=f32)
    gain_ref[...] = jnp.sum(
        main[:keys] * w_ref[:keys, :].astype(f32), axis=0, keepdims=True
    ) + jnp.sum(main[keys:] * w_ref[keys + wide :, :].astype(f32), axis=0, keepdims=True)
    main = main.astype(bf16)
    out = jnp.dot(out_left[...], m_ref[...], preferred_element_type=f32).astype(bf16)
    for i in range(2):
        here, there = slice(128 * i, 128 * i + 128), slice(128 - 128 * i, 256 - 128 * i)
        left = jnp.where(odd, main[:, there], main[:, here])
        a_ref[i, 0, :keys, :] = left[:keys]
        a_ref[i, 0, keys:, :] = jnp.where(odd, out[:, there], out[:, here])
        b_ref[0, i, :, :] = left[keys:]


def late_gradients(plane, q, k, v, s, o, x, m, w):
    rows, kwide = q.shape
    wide = v.shape[1]
    ra, rb = 2 * kwide + wide, 2 * wide
    slim = pl.BlockSpec((rows, kwide), lambda i, p: (0, 0))
    whole = pl.BlockSpec((rows, wide), lambda i, p: (0, 0))
    block = pl.BlockSpec((rows, 256), lambda i, p: (0, jnp.bitwise_xor(i, p[0] // 2)))
    return pl.pallas_call(
        late_kernel,
        grid_spec=pltpu.PrefetchScalarGridSpec(
            num_scalar_prefetch=1,
            grid=(8,),
            in_specs=[
                slim,
                slim,
                whole,
                whole,
                whole,
                block,
                block,
                pl.BlockSpec((w.shape[0], 256), lambda i, p: (0, jnp.bitwise_xor(i, p[0] // 2))),
            ],
            out_specs=(
                pl.BlockSpec((2, 1, ra, 128), lambda i, p: (i % 2, i // 2, 0, 0)),
                pl.BlockSpec((1, 2, rb, 128), lambda i, p: (i // 2, i % 2, 0, 0)),
                pl.BlockSpec((1, 256), lambda i, p: (0, jnp.bitwise_xor(i, p[0] // 2))),
            ),
            scratch_shapes=[
                pltpu.VMEM((2 * kwide + 2 * wide, rows), bf16),
                pltpu.VMEM((wide, rows), bf16),
            ],
        ),
        out_shape=(
            jax.ShapeDtypeStruct((4, 4, ra, 128), bf16),
            jax.ShapeDtypeStruct((4, 4, rb, 128), bf16),
            jax.ShapeDtypeStruct((1, 2048), f32),
        ),
        compiler_params=params(48),
    )(plane.reshape(1), q, k, v, s, o, x, m, w)


def early_out_kernel(sum_ref, keep_ref, send_ref):
    low = lax.axis_index("dp") % 2 == 0
    wide = sum_ref.shape[0] // 3
    for i in range(3):
        flat = sum_ref[i * wide : (i + 1) * wide, :].T
        place = slice(i * up128(wide), i * up128(wide) + wide)
        keep_ref[:, place] = jnp.where(low, flat[:64], flat[64:])
        send_ref[:, place] = jnp.where(low, flat[64:], flat[:64])


def early_end_kernel(keep_ref, got_ref, *out_refs):
    wide = out_refs[0].shape[1]
    for i, out_ref in enumerate(out_refs):
        place = slice(i * up128(wide), i * up128(wide) + wide)
        out_ref[...] = keep_ref[:, place].astype(f32) + got_ref[:, place].astype(f32)


def settle_early(summed):
    wide = summed.shape[0] // 3
    flat = jax.ShapeDtypeStruct((64, 3 * up128(wide)), bf16)
    keep, send = pl.pallas_call(
        early_out_kernel, out_shape=(flat, flat), compiler_params=params(16)
    )(summed)
    return pl.pallas_call(
        early_end_kernel,
        out_shape=(jax.ShapeDtypeStruct((64, wide), f32),) * 3,
        compiler_params=params(16),
    )(keep, move(send, Y2))


def late_out_kernel(sizes, a_ref, b_ref, keep_ref, send_ref):
    low = lax.axis_index("dp") % 2 == 0
    place, row, ref = 0, 0, a_ref
    for size in sizes:
        if row == ref.shape[0]:
            row, ref = 0, b_ref
        flat = ref[row : row + size, :].T
        keep_ref[:, place : place + size] = jnp.where(low, flat[:64], flat[64:])
        send_ref[:, place : place + size] = jnp.where(low, flat[64:], flat[:64])
        row += size
        place += up128(size)


def late_end_kernel(keep_ref, got_ref, *out_refs):
    low = lax.axis_index("dp") % 2 == 0
    place = 0
    for out_ref in out_refs:
        size = out_ref.shape[1] // 2
        keep = keep_ref[:, place : place + size].astype(f32)
        got = got_ref[:, place : place + size].astype(f32)
        out_ref[:, :size] = jnp.where(low, keep, got)
        out_ref[:, size:] = jnp.where(low, got, keep)
        place += up128(size)


def settle_late(a, b, sizes):
    flat = jax.ShapeDtypeStruct((64, sum(up128(n) for n in sizes)), bf16)
    keep, send = pl.pallas_call(
        functools.partial(late_out_kernel, sizes), out_shape=(flat, flat), compiler_params=params(16)
    )(a, b)
    return pl.pallas_call(
        late_end_kernel,
        out_shape=tuple(jax.ShapeDtypeStruct((64, 2 * n), f32) for n in sizes),
        compiler_params=params(16),
    )(keep, move(send, Y2))


def gather_line(own):
    half = own.shape[0] // 2
    r1, r3 = tie(move(own, Y1), move(own, Y3))
    mine = stacked(own, r1)
    r2 = stacked(move(r3[:half], Y1), move(r1[half:], Y3))
    other = stacked(r2, r3)
    return stacked(mine, move(mine, C1), other, move(other, C1))


def scatter_line(keep_m, send_m, keep_o, send_o):
    rows = keep_m.shape[0] // 2
    half = rows // 2
    o = keep_o + move(send_o, C1).astype(f32)
    s2 = o[:rows].astype(bf16)
    t3, t1 = tie(move(s2[:half], Y1), move(s2[half:], Y3))
    m = keep_m + move(send_m, C1).astype(f32)
    s3 = stacked(o[rows : rows + half] + t3.astype(f32), o[rows + half :]).astype(bf16)
    s1 = stacked(m[rows : rows + half], m[rows + half :] + t1.astype(f32)).astype(bf16)
    u3, u1 = tie(move(s3, Y3), move(s1, Y1))
    return m[:rows] + u3.astype(f32) + u1.astype(f32)


def gather_pair(own):
    mine = stacked(own, move(own, Y1))
    return stacked(mine, move(mine, C1))


def scatter_pair(keep, send, *later):
    rows = keep.shape[0] // 2
    m = keep + move(send, C1).astype(f32)
    u1, *later = tie(move(m[rows:].astype(bf16), Y1), *later)
    return (m[:rows] + u1.astype(f32), *later)


def mixer_kernel(q_ref, k_ref, v_ref, gate_ref, decay_ref, gain_ref, retained_ref, mixed_ref):
    scores = dot(q_ref[...], k_ref[...], NT)
    weights = (scores * decay_ref[...]).astype(bf16)
    retained = dot(weights, v_ref[...])
    retained_ref[...] = retained
    center = retained - jnp.mean(retained, axis=-1, keepdims=True)
    spread = jnp.mean(center * center, axis=-1, keepdims=True)
    normed = center * lax.rsqrt(spread + group_eps)
    gate = gate_ref[...]
    mixed_ref[...] = (gate * jax.nn.sigmoid(gate) * normed * gain_ref[...]).astype(bf16)


def mixer_forward(q, k, v, gate, decay, gain):
    total, kwide = q.shape
    wide = v.shape[1]
    rows = decay.shape[0]
    slim = pl.BlockSpec((rows, kwide), lambda i: (i, 0))
    whole = pl.BlockSpec((rows, wide), lambda i: (i, 0))
    return pl.pallas_call(
        mixer_kernel,
        grid=(total // rows,),
        out_shape=(
            jax.ShapeDtypeStruct((total, wide), f32),
            jax.ShapeDtypeStruct((total, wide), bf16),
        ),
        in_specs=[
            slim,
            slim,
            whole,
            whole,
            pl.BlockSpec((rows, rows), lambda i: (0, 0)),
            pl.BlockSpec((1, wide), lambda i: (0, 0)),
        ],
        out_specs=(whole, whole),
        compiler_params=params(32),
    )(q, k, v, gate, decay, gain)


def mixer_back_kernel(
    q_ref, k_ref, v_ref, gate_ref, decay_ref, gain_ref, retained_ref, mixed_ref,
    gq_ref, gk_ref, gv_ref, gate_out_ref, gain_out_ref,
):
    q, k, v, decay = q_ref[...], k_ref[...], v_ref[...], decay_ref[...]
    gain = gain_ref[...]
    retained = retained_ref[...]
    center = retained - jnp.mean(retained, axis=-1, keepdims=True)
    rstd = lax.rsqrt(jnp.mean(center * center, axis=-1, keepdims=True) + group_eps)
    normed = center * rstd
    gate = gate_ref[...]
    sig = jax.nn.sigmoid(gate)
    grad = mixed_ref[...]
    grad_normed = grad * normed
    gate_out_ref[...] = (grad_normed * gain * (sig * (1.0 + gate * (1.0 - sig)))).astype(bf16)
    silu = gate * sig

    @pl.when(pl.program_id(0) == 0)
    def _():
        gain_out_ref[...] = jnp.zeros_like(gain_out_ref)

    gain_out_ref[...] += jnp.sum(grad_normed * silu, axis=0, keepdims=True)
    y = grad * silu * gain
    back = rstd * (
        y
        - jnp.mean(y, axis=-1, keepdims=True)
        - normed * jnp.mean(y * normed, axis=-1, keepdims=True)
    )
    back = back.astype(bf16)
    weights = (dot(q, k, NT) * decay).astype(bf16)
    grad_scores = (dot(back, v, NT) * decay).astype(bf16)
    gq_ref[...] = dot(grad_scores, k).astype(bf16)
    gk_ref[...] = dot(grad_scores, q, TN).astype(bf16)
    gv_ref[...] = dot(weights, back, TN).astype(bf16)


def mixer_backward(q, k, v, gate, decay, gain, retained, mixed):
    total, kwide = q.shape
    wide = v.shape[1]
    rows = decay.shape[0]
    slim = pl.BlockSpec((rows, kwide), lambda i: (i, 0))
    whole = pl.BlockSpec((rows, wide), lambda i: (i, 0))
    line = pl.BlockSpec((1, wide), lambda i: (0, 0))
    return pl.pallas_call(
        mixer_back_kernel,
        grid=(total // rows,),
        out_shape=(
            jax.ShapeDtypeStruct((total, kwide), bf16),
            jax.ShapeDtypeStruct((total, kwide), bf16),
            jax.ShapeDtypeStruct((total, wide), bf16),
            jax.ShapeDtypeStruct((total, wide), bf16),
            jax.ShapeDtypeStruct((1, wide), f32),
        ),
        in_specs=[
            slim,
            slim,
            whole,
            whole,
            pl.BlockSpec((rows, rows), lambda i: (0, 0)),
            line,
            whole,
            whole,
        ],
        out_specs=(slim, slim, whole, whole, line),
        compiler_params=params(32),
    )(q, k, v, gate, decay, gain, retained, mixed)


def shards(
    tokens,
    group_length,
    forget_rate,
    mixer_gain,
    feed_gain,
    group_gain,
    w_query,
    w_key,
    w_value,
    w_swish,
    w_output,
    w_gelu,
    w_linear,
    w_down,
    cotangent,
):
    rows, width = tokens.shape
    dp = lax.axis_index("dp")
    tensor = lax.axis_index("tensor")
    plane = dp // 2
    is_low = dp % 2 == 0
    feed_wide = w_gelu.shape[1]
    wide = w_value.shape[1] // 2
    kwide = w_query.shape[1] // 2
    group = 4 * rows
    half = group // 2
    score_scale = kwide ** (-0.5)
    log_keep = jnp.log1p(-jnp.where(is_low, forget_rate[0], forget_rate[1]))
    valid_rows = (tensor * rows + lax.broadcasted_iota(jnp.int32, (rows, 1), 0) < group_length[0]).astype(f32)

    keep, send, pack = split_weights(
        (w_query, w_key, w_output.T, w_value, w_swish), (w_gelu, w_linear, w_down.T)
    )
    first_a, first_b = join_weights(keep, move(send, Y2), (kwide, kwide, wide), (wide, wide))
    (second,) = join_weights(pack, move(pack, Y2), (feed_wide,) * 3)

    token_float = tokens.astype(f32)
    grad_result = cotangent.astype(f32)
    group_own = jnp.where(is_low, group_gain[:wide], group_gain[wide:]).reshape(1, wide)

    r1 = lax.rsqrt(jnp.mean(token_float * token_float, axis=-1, keepdims=True) + norm_eps)
    normed_in = (token_float * r1 * mixer_gain).astype(bf16)
    normed_group = gather_line(normed_in)
    grad_feed_out = (valid_rows * grad_result).astype(bf16)
    grad_feed_group = gather_pair(grad_feed_out)

    first_full, second = gather_plane(first_a, first_b, second)
    second_full = widen(
        lax.all_gather(second, AXES, axis_index_groups=PLANES, axis=0, tiled=True)
    )
    normed_group, grad_feed_group = tie(normed_group, grad_feed_group)
    wqk = first_full[: 2 * kwide]
    wo = first_full[2 * kwide : 2 * kwide + wide]
    wv = first_full[2 * kwide + wide : 2 * kwide + 2 * wide]
    ws = first_full[2 * kwide + 2 * wide :]
    wg, wl, wd = (second_full[i * feed_wide : (i + 1) * feed_wide] for i in range(3))

    def line_dots(pairs):
        def part(a, b, kind):
            return sum(dot(left[a:b], right) for left, right in pairs).astype(kind)

        send_o, keep_o = part(group + half, 2 * group, bf16), part(group, group + half, f32)
        send_m, keep_m = part(half, group, bf16), part(0, half, f32)
        return scatter_line(keep_m, send_m, keep_o, send_o)

    def pair_dots(pairs):
        def part(a, b, kind):
            return sum(dot(left[a:b], right) for left, right in pairs).astype(kind)

        send = part(half, group, bf16)
        return part(0, half, f32), send

    qk = dot(normed_group, wqk, NT).astype(bf16)
    q, k = qk[:, :kwide], qk[:, kwide:]
    v = dot(normed_group, wv, NT).astype(bf16)
    gate_pre = dot(normed_group, ws, NT)

    place = lax.broadcasted_iota(jnp.int32, (group, 1), 0)
    block = place // rows
    order = jnp.where(block == 1, 2, jnp.where(block == 2, 1, block))
    position = jnp.bitwise_xor(tensor, order) * rows + place % rows
    offset = position - position.reshape(1, -1)
    decay = jnp.where(
        offset >= 0, jnp.exp(jnp.maximum(offset, 0).astype(f32) * log_keep) * score_scale, 0.0
    )
    retained, mixed_low = mixer_forward(q, k, v, gate_pre, decay, group_own)
    mixer_out = line_dots([(mixed_low, wo)])
    middle = token_float + valid_rows * mixer_out
    r2 = lax.rsqrt(jnp.mean(middle * middle, axis=-1, keepdims=True) + norm_eps)
    normed_mid = (middle * r2 * feed_gain).astype(bf16)
    mid_group = gather_pair(normed_mid)
    gelu_in = dot(mid_group, wg, NT)
    linear_in = dot(mid_group, wl, NT)
    cdf = 0.5 * (1.0 + lax.erf(gelu_in * (0.5**0.5)))
    gelu = gelu_in * cdf
    gelu_slope = cdf + gelu_in * jnp.exp(-0.5 * gelu_in * gelu_in) * 0.3989422804014327
    grad_hidden = dot(grad_feed_group, wd, NT)
    hidden, grad_gelu_in, grad_linear_in = tie(
        (gelu * linear_in).astype(bf16),
        (grad_hidden * linear_in * gelu_slope).astype(bf16),
        (grad_hidden * gelu).astype(bf16),
    )
    early = early_gradients(grad_gelu_in, grad_linear_in, hidden, mid_group, grad_feed_group)
    keep, send = pair_dots([(grad_gelu_in, wg), (grad_linear_in, wl)])
    grad_normed_mid, early = scatter_pair(keep, send, early)
    early_sum = lax.psum_scatter(
        early.reshape(-1, 128), AXES, axis_index_groups=PLANES, scatter_dimension=0, tiled=True
    )

    part_feed_gain = jnp.sum(grad_normed_mid * middle * r2, axis=0)
    z2 = grad_normed_mid * feed_gain
    grad_middle = (
        grad_result + r2 * z2 - middle * (r2 * r2 * r2) * jnp.mean(z2 * middle, axis=-1, keepdims=True)
    )
    grad_mixer_out = (valid_rows * grad_middle).astype(bf16)
    keep, send = pair_dots([(hidden, wd)])
    grad_mixer_group, keep, send = tie(gather_line(grad_mixer_out), keep, send)
    (feed_out,) = scatter_pair(keep, send)
    result = (middle + valid_rows * feed_out).astype(bf16)

    grad_mixed = dot(grad_mixer_group, wo, NT)
    gq, gk, gv, grad_gate_pre, part_group_gain = mixer_backward(
        q, k, v, gate_pre, decay, group_own, retained, grad_mixed
    )
    late_a, late_b, part_mixer_gain = late_gradients(
        plane, gq, gk, gv, grad_gate_pre, mixed_low, normed_group, grad_mixer_group, first_full
    )
    grad_normed_in = line_dots([(gq, wqk[:kwide]), (gk, wqk[kwide:]), (gv, wv), (grad_gate_pre, ws)])
    sum_a, sum_b = scatter_plane(late_a, late_b)
    z1 = grad_normed_in * mixer_gain
    grad_tokens = (
        grad_middle + r1 * z1 - token_float * (r1 * r1 * r1) * jnp.mean(z1 * token_float, axis=-1, keepdims=True)
    ).astype(bf16)

    g_gelu, g_linear, g_down = settle_early(early_sum)
    g_query, g_key, g_output, g_value, g_swish = settle_late(
        sum_a, sum_b, (kwide, kwide, wide, wide, wide)
    )

    gains = jnp.concatenate(
        [part_mixer_gain.reshape(-1) / mixer_gain, part_feed_gain, part_group_gain.reshape(-1)]
    )
    for pairs in (X1, X2, Z1, Z2):
        gains = gains + move(gains, pairs)
    group_half = gains[2 * width :]
    gains = gains[: 2 * width]
    for pairs in (Y1, Y2, C1):
        gains = gains + move(gains, pairs)
    group_far = move(group_half, Y2)
    group_sum = jnp.where(
        is_low,
        jnp.concatenate([group_half, group_far]),
        jnp.concatenate([group_far, group_half]),
    )
    return (
        result,
        grad_tokens,
        gains[:width],
        gains[width:],
        group_sum,
        g_query,
        g_key,
        g_value,
        g_swish,
        g_output.T,
        g_gelu,
        g_linear,
        g_down.T,
    )


def solution(mesh):
    weight = P("dp", "tensor")
    turned = P("tensor", "dp")
    rows = P(("dp", "tensor"), None)
    return jax.shard_map(
        shards,
        mesh=mesh,
        in_specs=(
            rows,
            P("dp"),
            P("tensor"),
            P(),
            P(),
            P("tensor"),
            weight,
            weight,
            weight,
            weight,
            turned,
            weight,
            weight,
            turned,
            rows,
        ),
        out_specs=(
            rows,
            rows,
            P(),
            P(),
            P("tensor"),
            weight,
            weight,
            weight,
            weight,
            turned,
            weight,
            weight,
            turned,
        ),
        check_vma=False,
    )
```

```python
import functools

import jax
import jax.numpy as jnp
from jax import lax
from jax.experimental import pallas as pl
from jax.experimental.pallas import tpu as pltpu
from jax.sharding import PartitionSpec as P

norm_eps = 1e-05
group_eps = 1.0
AXES = ("dp", "tensor")
f32 = jnp.float32
bf16 = jnp.bfloat16
NN = (((1,), (0,)), ((), ()))
NT = (((1,), (1,)), ((), ()))
TN = (((0,), (0,)), ((), ()))
MB = 1 << 20
VMEM = pl.BlockSpec(memory_space=pltpu.VMEM)
ANY = pl.BlockSpec(memory_space=pl.ANY)


def device_index(x, z, y, c):
    return ((x * 4 + z) * 2 + y // 2) * 4 + (y % 2) * 2 + c


def xor_pairs(dx=0, dz=0, dy=0, dc=0):
    return [
        (device_index(x, z, y, c), device_index(x ^ dx, z ^ dz, y ^ dy, c ^ dc))
        for x in range(4)
        for z in range(4)
        for y in range(4)
        for c in range(2)
    ]


X1, X2, X3 = (xor_pairs(dx=d) for d in (1, 2, 3))
Z1, Z2, Z3 = (xor_pairs(dz=d) for d in (1, 2, 3))
Y1, Y2, Y3 = (xor_pairs(dy=d) for d in (1, 2, 3))
C1 = xor_pairs(dc=1)
LINES = [
    [device_index(x, z, y, c) for y in range(4) for c in range(2)]
    for x in range(4)
    for z in range(4)
]
LINE_ORDER = ((0, 0), (1, 0), (0, 1), (1, 1), (2, 0), (3, 0), (2, 1), (3, 1))
PLANES = [
    [device_index(x, z, y, c) for x in range(4) for z in range(4)]
    for y in range(4)
    for c in range(2)
]


def move(value, pairs):
    return lax.ppermute(value, AXES, pairs)


def tie(*values):
    return lax.optimization_barrier(values)


def dot(left, right, dims=NN):
    return lax.dot_general(left, right, dims, preferred_element_type=f32)


def params(mb):
    return pltpu.CompilerParams(vmem_limit_bytes=mb * MB)


def up128(n):
    return n + (-n % 128)


def stacked(*parts):
    return jnp.concatenate(parts, axis=0)


def split_kernel(*refs):
    ins, held, (keep_ref, send_ref), sems = refs[:8], refs[10:18], refs[8:10], refs[18]
    copies = [pltpu.make_async_copy(i, h, sems.at[n]) for n, (i, h) in enumerate(zip(ins, held))]
    for copy in copies:
        copy.start()
    low = lax.axis_index("dp") % 2 == 0
    place = 0
    for n, ref in enumerate(held):
        copies[n].wait()
        if n < 5:
            half = ref.shape[1] // 2
            left, right = ref[:, :half], ref[:, half:]
            keep_ref[:, place : place + half] = jnp.where(low, left, right)
            send_ref[:, place : place + half] = jnp.where(low, right, left)
        else:
            half = ref.shape[1]
            keep_ref[:, place : place + half] = ref[...]
            send_ref[:, place : place + half] = ref[...]
        place += up128(half)


def split_weights(mixer, feed):
    size = sum(up128(w.shape[1] // 2) for w in mixer) + sum(up128(w.shape[1]) for w in feed)
    return pl.pallas_call(
        split_kernel,
        out_shape=(jax.ShapeDtypeStruct((64, size), bf16),) * 2,
        in_specs=[ANY] * 8,
        scratch_shapes=[pltpu.VMEM(w.shape, bf16) for w in (*mixer, *feed)]
        + [pltpu.SemaphoreType.DMA((8,))],
        compiler_params=params(60),
    )(*mixer, *feed)


def join_kernel(groups, keep_ref, got_ref, *out_refs):
    low = lax.axis_index("dp") % 2 == 0
    place = 0
    for sizes, out_ref in zip(groups, out_refs):
        row = 0
        for size in sizes:
            wide = up128(size)
            keep, got = keep_ref[:, place : place + wide], got_ref[:, place : place + wide]
            both = stacked(jnp.where(low, keep, got), jnp.where(low, got, keep))
            out_ref[row : row + size, :] = both.T[:size]
            place += wide
            row += size


def join_weights(keep, got, *groups):
    out = pl.pallas_call(
        functools.partial(join_kernel, groups),
        out_shape=tuple(jax.ShapeDtypeStruct((sum(sizes), 128), bf16) for sizes in groups),
        compiler_params=params(16),
    )(keep, got)
    return out


def pick_kernel(starts, *refs):
    count = len(starts)
    ins, outs, sems = refs[:count], refs[count : 2 * count], refs[2 * count]
    copies = [
        pltpu.make_async_copy(i.at[pl.ds(start, o.shape[0])], o, sems.at[n])
        for n, (i, o, start) in enumerate(zip(ins, outs, starts))
    ]
    for copy in copies:
        copy.start()
    for copy in copies:
        copy.wait()


def pick(values, starts, sizes):
    return pl.pallas_call(
        functools.partial(pick_kernel, starts),
        out_shape=tuple(
            jax.ShapeDtypeStruct((n, *v.shape[1:]), v.dtype) for v, n in zip(values, sizes)
        ),
        in_specs=[ANY] * len(values),
        out_specs=(ANY,) * len(values),
        scratch_shapes=[pltpu.SemaphoreType.DMA((len(values),))],
        compiler_params=params(4),
    )(*values)


def gather_plane(a, b):
    ha, hb = a.shape[0] // 32 * 16, b.shape[0] // 32 * 16
    a1, a3, b1, b3 = tie(move(a, X1), move(a, X3), move(b, Z1), move(b, Z3))
    a2p, a2q, b2p, b2q = tie(
        move(a3[:ha], X1), move(a1[ha:], X3), move(b3[:hb], Z1), move(b1[hb:], Z3)
    )
    a2, b2 = stacked(a2p, a2q), stacked(b2p, b2q)
    sa, sb = tie(jnp.stack([a, a1, a2, a3]), jnp.stack([b, b1, b2, b3]))
    sa1, sa3, sb1, sb3 = tie(move(sa, Z1), move(sa, Z3), move(sb, X1), move(sb, X3))
    ap, aq, bp, bq = pick((sa3, sa1, sb3, sb1), (0, 2, 0, 2), (2,) * 4)
    sa2p, sa2q, sb2p, sb2q = tie(move(ap, Z1), move(aq, Z3), move(bp, X1), move(bq, X3))
    return sa, sa1, sa2p, sa2q, sa3, sb, sb1, sb2p, sb2q, sb3


def add_low(*terms):
    total = terms[0].astype(f32)
    for term in terms[1:]:
        total = total + term.astype(f32)
    return total.astype(bf16)


def scatter_start(a, b):
    ap, aq, bp, bq = pick(
        (a.reshape(16, *a.shape[2:]),) * 2 + (b.reshape(16, *b.shape[2:]),) * 2, (8, 10, 8, 10), (2,) * 4
    )
    return move(ap, Z1), move(aq, Z3), move(bp, X1), move(bq, X3)


def scatter_add(a, b, moved, half_a, half_b):
    ap, aq, bp, bq = moved
    a3 = stacked(add_low(a[3, :half_a], ap), a[3, half_a:])
    a1 = stacked(a[1, :half_a], add_low(a[1, half_a:], aq))
    b3 = stacked(add_low(b[3, :half_b], bp), b[3, half_b:])
    b1 = stacked(b[1, :half_b], add_low(b[1, half_b:], bq))
    return tie(a3, a1, b3, b1)


def feed_kernel(
    w_ref, x0_ref, x1_ref, g_ref, hidden_ref, gelu_ref, linear_ref, keep_ref, send_ref,
    held_ref, x_ref, grad_ref, sems,
):
    wide = hidden_ref.shape[0]
    half = x0_ref.shape[0]
    given = [
        pltpu.make_async_copy(x0_ref, x_ref.at[pl.ds(0, half), :], sems.at[48]),
        pltpu.make_async_copy(x1_ref, x_ref.at[pl.ds(half, half), :], sems.at[49]),
    ]
    weights = [
        [
            pltpu.make_async_copy(
                w_ref.at[pl.ds((3 * j + i) * wide, wide), :],
                held_ref.at[pl.ds(i * wide, wide), pl.ds(128 * j, 128)],
                sems.at[16 * i + j],
            )
            for j in range(16)
        ]
        for i in range(3)
    ]
    grad = pltpu.make_async_copy(g_ref, grad_ref, sems.at[50])
    for copy in given + weights[0] + weights[1] + [grad] + weights[2]:
        copy.start()
    for copy in given + weights[0]:
        copy.wait()
    step = wide // 2
    for i in range(2):
        a, b, c = (slice(n * wide + i * step, n * wide + (i + 1) * step) for n in range(3))
        gelu_in = dot(held_ref[a, :], x_ref[...], NT)
        if i == 0:
            for copy in weights[1]:
                copy.wait()
        linear_in = dot(held_ref[b, :], x_ref[...], NT)
        if i == 0:
            for copy in [grad] + weights[2]:
                copy.wait()
        back = dot(held_ref[c, :], grad_ref[...], NT)
        cdf = 0.5 * (1.0 + lax.erf(gelu_in * (0.5**0.5)))
        gelu = gelu_in * cdf
        slope = cdf + gelu_in * jnp.exp(-0.5 * gelu_in * gelu_in) * 0.3989422804014327
        hidden_ref[a, :] = (gelu * linear_in).astype(bf16)
        gelu_ref[a, :] = (back * linear_in * slope).astype(bf16)
        linear_ref[a, :] = (back * gelu).astype(bf16)
    up, down = slice(0, wide), slice(wide, 2 * wide)
    for rows, out_ref in ((slice(half, 2 * half), send_ref), (slice(0, half), keep_ref)):
        total = dot(gelu_ref[:, rows], held_ref[up, :], TN)
        total += dot(linear_ref[:, rows], held_ref[down, :], TN)
        out_ref[...] = total.astype(out_ref.dtype)


def feed_forward_back(w, x0, x1, g):
    half, width = x0.shape
    wide = w.shape[0] // 48
    turned = jax.ShapeDtypeStruct((wide, 2 * half), bf16)
    return pl.pallas_call(
        feed_kernel,
        out_shape=(
            turned,
            turned,
            turned,
            jax.ShapeDtypeStruct((half, width), f32),
            jax.ShapeDtypeStruct((half, width), bf16),
        ),
        in_specs=[ANY] * 4,
        scratch_shapes=[
            pltpu.VMEM((3 * wide, width), bf16),
            pltpu.VMEM((2 * half, width), bf16),
            pltpu.VMEM((2 * half, width), bf16),
            pltpu.SemaphoreType.DMA((51,)),
        ],
        compiler_params=params(56),
    )(w, x0, x1, g)


def early_kernel(
    hidden_ref, gelu_ref, linear_ref, x0_ref, x1_ref, g_ref, w_ref, out_ref, keep_ref, send_ref, turn_ref
):
    wide = gelu_ref.shape[0]
    half = x0_ref.shape[0]

    @pl.when(pl.program_id(0) == 0)
    def _():
        turn_ref[...] = hidden_ref[...].T

    x = stacked(x0_ref[...], x1_ref[...])
    for n, (left, right) in enumerate(((gelu_ref, x), (linear_ref, x), (hidden_ref, g_ref[...]))):
        part = dot(left[...], right).astype(bf16)
        for i in range(2):
            out_ref[i, n * wide : (n + 1) * wide, :] = part[:, 128 * i : 128 * i + 128]
    w = jnp.concatenate([w_ref[0], w_ref[1]], axis=1)
    keep_ref[...] = dot(turn_ref[:half, :], w)
    send_ref[...] = dot(turn_ref[half:, :], w).astype(bf16)


def early_gradients(hidden, gelu, linear, x0, x1, g, w):
    wide, rows = gelu.shape
    half, width = x0.shape
    whole = pl.BlockSpec((wide, rows), lambda i: (0, 0))
    block = pl.BlockSpec((half, 256), lambda i: (0, i))
    return pl.pallas_call(
        early_kernel,
        grid=(8,),
        out_shape=(
            jax.ShapeDtypeStruct((16, 3 * wide, 128), bf16),
            jax.ShapeDtypeStruct((half, width), f32),
            jax.ShapeDtypeStruct((half, width), bf16),
        ),
        in_specs=[
            whole,
            whole,
            whole,
            block,
            block,
            pl.BlockSpec((rows, 256), lambda i: (0, i)),
            pl.BlockSpec((2, wide, 128), lambda i: (i, 2, 0)),
        ],
        out_specs=(pl.BlockSpec((2, 3 * wide, 128), lambda i: (i, 0, 0)), block, block),
        scratch_shapes=[pltpu.VMEM((rows, wide), bf16)],
        compiler_params=params(48),
    )(hidden, gelu, linear, x0, x1, g, w.reshape(16, 3 * wide, 128))


def late_kernel(plane_ref, q_ref, k_ref, o_ref, v_ref, s_ref, x_ref, *refs):
    m_refs, (a_ref, b_ref) = refs[:4], refs[4:]
    odd = plane_ref[0] % 2
    x = x_ref[...]
    row = 0
    for n, left in enumerate((q_ref, k_ref, o_ref, v_ref, s_ref)):
        if n == 2:
            step = m_refs[0].shape[0]
            part = sum(
                dot(left[:, i * step : (i + 1) * step], m_ref[...]) for i, m_ref in enumerate(m_refs)
            )
        else:
            part = dot(left[...], x)
        part = part.astype(bf16)
        rows = slice(row, row + left.shape[0])
        for i in range(2):
            there = jnp.bitwise_xor(odd, i)
            if n < 3:
                a_ref[there, 0, rows, :] = part[:, 128 * i : 128 * i + 128]
            else:
                b_ref[0, there, rows, :] = part[:, 128 * i : 128 * i + 128]
        row = 0 if n == 2 else row + left.shape[0]


def late_gradients(plane, q, k, o, v, s, x, m):
    kwide, rows = q.shape
    wide = v.shape[0]
    ra, rb = 2 * kwide + wide, 2 * wide
    slim = pl.BlockSpec((kwide, rows), lambda i, p: (0, 0))
    whole = pl.BlockSpec((wide, rows), lambda i, p: (0, 0))
    lanes = lambda i, p: (0, jnp.bitwise_xor(i, p[0] // 2))
    return pl.pallas_call(
        late_kernel,
        grid_spec=pltpu.PrefetchScalarGridSpec(
            num_scalar_prefetch=1,
            grid=(8,),
            in_specs=[slim, slim, whole, whole, whole, pl.BlockSpec((rows, 256), lanes)]
            + [pl.BlockSpec((rows // 4, 256), lanes)] * 4,
            out_specs=(
                pl.BlockSpec((2, 1, ra, 128), lambda i, p: (i % 2, i // 2, 0, 0)),
                pl.BlockSpec((1, 2, rb, 128), lambda i, p: (i // 2, i % 2, 0, 0)),
            ),
        ),
        out_shape=(
            jax.ShapeDtypeStruct((4, 4, ra, 128), bf16),
            jax.ShapeDtypeStruct((4, 4, rb, 128), bf16),
        ),
        compiler_params=params(40),
    )(plane.reshape(1), q, k, o, v, s, x, *m)


def early_out_kernel(sum_ref, keep_ref, send_ref):
    low = lax.axis_index("dp") % 2 == 0
    wide = sum_ref.shape[0] // 3
    for i in range(3):
        flat = sum_ref[i * wide : (i + 1) * wide, :].T
        place = slice(i * up128(wide), i * up128(wide) + wide)
        keep_ref[:, place] = jnp.where(low, flat[:64], flat[64:])
        send_ref[:, place] = jnp.where(low, flat[64:], flat[:64])


def early_end_kernel(keep_ref, got_ref, *out_refs):
    wide = out_refs[0].shape[1]
    for i, out_ref in enumerate(out_refs):
        place = slice(i * up128(wide), i * up128(wide) + wide)
        out_ref[...] = keep_ref[:, place].astype(f32) + got_ref[:, place].astype(f32)


def settle_early(summed):
    wide = summed.shape[0] // 3
    flat = jax.ShapeDtypeStruct((64, 3 * up128(wide)), bf16)
    keep, send = pl.pallas_call(
        early_out_kernel, out_shape=(flat, flat), compiler_params=params(16)
    )(summed)
    return pl.pallas_call(
        early_end_kernel,
        out_shape=(jax.ShapeDtypeStruct((64, wide), f32),) * 3,
        compiler_params=params(16),
    )(keep, move(send, Y2))


def late_out_kernel(sizes, a_ref, b_ref, keep_ref, send_ref):
    low = lax.axis_index("dp") % 2 == 0
    place, row, ref = 0, 0, a_ref
    for size in sizes:
        if row == ref.shape[0]:
            row, ref = 0, b_ref
        flat = ref[row : row + size, :].T
        keep_ref[:, place : place + size] = jnp.where(low, flat[:64], flat[64:])
        send_ref[:, place : place + size] = jnp.where(low, flat[64:], flat[:64])
        row += size
        place += up128(size)


def late_end_kernel(keep_ref, got_ref, *out_refs):
    low = lax.axis_index("dp") % 2 == 0
    place = 0
    for out_ref in out_refs:
        size = out_ref.shape[1] // 2
        keep = keep_ref[:, place : place + size].astype(f32)
        got = got_ref[:, place : place + size].astype(f32)
        out_ref[:, :size] = jnp.where(low, keep, got)
        out_ref[:, size:] = jnp.where(low, got, keep)
        place += up128(size)


def settle_late(a, b, sizes):
    flat = jax.ShapeDtypeStruct((64, sum(up128(n) for n in sizes)), bf16)
    keep, send = pl.pallas_call(
        functools.partial(late_out_kernel, sizes), out_shape=(flat, flat), compiler_params=params(16)
    )(a, b)
    return pl.pallas_call(
        late_end_kernel,
        out_shape=tuple(jax.ShapeDtypeStruct((64, 2 * n), f32) for n in sizes),
        compiler_params=params(16),
    )(keep, move(send, Y2))


def line_place(block):
    dp, tensor = lax.axis_index("dp"), lax.axis_index("tensor")
    y, c = dp % 2 * 2 + tensor // 2, tensor % 2
    dy, dc = LINE_ORDER[block]
    return jnp.bitwise_xor(y, dy) * 2 + jnp.bitwise_xor(c, dc)


def reorder_kernel(in_ref, out_ref, sems):
    rows = in_ref.shape[0] // 8
    copies = [
        pltpu.make_async_copy(
            in_ref.at[pl.ds(pl.multiple_of(line_place(j) * rows, rows), rows), :],
            out_ref.at[pl.ds(j * rows, rows), :],
            sems.at[j],
        )
        for j in range(8)
    ]
    for copy in copies:
        copy.start()
    for copy in copies:
        copy.wait()


def gather_line_whole(own):
    rows = lax.all_gather(own, AXES, axis_index_groups=LINES, axis=0, tiled=True)
    return pl.pallas_call(
        reorder_kernel,
        out_shape=jax.ShapeDtypeStruct(rows.shape, rows.dtype),
        in_specs=[ANY],
        out_specs=ANY,
        scratch_shapes=[pltpu.SemaphoreType.DMA((8,))],
        compiler_params=params(4),
    )(rows)


def back_kernel(q_ref, k_ref, v_ref, s_ref, w_ref, x_ref, out_ref, gain_ref, held_ref, sems):
    kwide, wide = q_ref.shape[0], v_ref.shape[0]
    rows = q_ref.shape[1] // 4
    step = pl.program_id(0)
    total = dot(q_ref[...], w_ref[:kwide, :], TN)
    total += dot(k_ref[...], w_ref[kwide : 2 * kwide, :], TN)
    total += dot(v_ref[...], w_ref[2 * kwide + wide : 2 * kwide + 2 * wide, :], TN)
    total += dot(s_ref[...], w_ref[2 * kwide + 2 * wide :, :], TN)
    held_ref[...] = total.astype(bf16)
    copies = []
    for j in range(4):
        where = jnp.where(step == 0, line_place(j), line_place(j + 4))
        copies.append(
            pltpu.make_async_copy(
                held_ref.at[pl.ds(j * rows, rows), :],
                out_ref.at[pl.ds(pl.multiple_of(where * rows, rows), rows), :],
                sems.at[j],
            )
        )
    for copy in copies:
        copy.start()
    gain = jnp.sum(total * x_ref[...].astype(f32), axis=0, keepdims=True)

    @pl.when(step == 0)
    def _():
        gain_ref[...] = gain

    @pl.when(step > 0)
    def _():
        gain_ref[...] += gain

    for copy in copies:
        copy.wait()


def input_gradients(q, k, v, s, w, x):
    kwide, total = q.shape
    wide = v.shape[0]
    half = total // 2
    slim = pl.BlockSpec((kwide, half), lambda i: (0, i))
    whole = pl.BlockSpec((wide, half), lambda i: (0, i))
    return pl.pallas_call(
        back_kernel,
        grid=(2,),
        out_shape=(
            jax.ShapeDtypeStruct((total, w.shape[1]), bf16),
            jax.ShapeDtypeStruct((1, w.shape[1]), f32),
        ),
        in_specs=[
            slim,
            slim,
            whole,
            whole,
            pl.BlockSpec(w.shape, lambda i: (0, 0)),
            pl.BlockSpec((half, w.shape[1]), lambda i: (i, 0)),
        ],
        out_specs=(ANY, pl.BlockSpec((1, w.shape[1]), lambda i: (0, 0))),
        scratch_shapes=[pltpu.VMEM((half, w.shape[1]), bf16), pltpu.SemaphoreType.DMA((4,))],
        compiler_params=params(48),
    )(q, k, v, s, w, x)


def gather_line(own):
    half = own.shape[0] // 2
    r1, r3 = tie(move(own, Y1), move(own, Y3))
    mine = stacked(own, r1)
    r2p, r2q = move(r3[:half], Y1), move(r1[half:], Y3)
    other = stacked(r2p, r2q, r3)
    return mine, move(mine, C1), other, move(other, C1)


def scatter_line(keep, send, *beside):
    rows = keep.shape[0] // 4
    half = rows // 2
    keep = keep + move(send, C1).astype(f32)
    m, o = keep[: 2 * rows], keep[2 * rows :]
    s2 = o[:rows].astype(bf16)
    t3, t1 = tie(move(s2[:half], Y1), move(s2[half:], Y3))
    s3 = stacked(o[rows : rows + half] + t3.astype(f32), o[rows + half :]).astype(bf16)
    s1 = stacked(m[rows : rows + half], m[rows + half :] + t1.astype(f32)).astype(bf16)
    u3, u1, *beside = tie(move(s3, Y3), move(s1, Y1), *beside)
    return (m[:rows] + u3.astype(f32) + u1.astype(f32), *beside)


def gather_pair(own):
    mine = stacked(own, move(own, Y1))
    return mine, move(mine, C1)


def scatter_pair(keep, send, *beside):
    rows = keep.shape[0] // 2
    m = keep + move(send, C1).astype(f32)
    u1, *beside = tie(move(m[rows:].astype(bf16), Y1), *beside)
    return (m[:rows] + u1.astype(f32), *beside)


def mixer_kernel(*refs):
    blocks, (x_ref, decay_ref, gain_ref) = refs[:10], refs[10:13]
    w_out, q_ref, k_ref, v_ref, gate_ref, retained_ref, mixed_ref, keep_ref, send_ref = refs[13:22]
    w_ref, sems = refs[22:]
    va, vb = blocks[:5], blocks[5:]
    kwide, wide = q_ref.shape[1], v_ref.shape[1]
    half = keep_ref.shape[0]
    plane = lax.axis_index("dp") // 2
    ra, rb = va[0].shape[1], vb[0].shape[1]
    step = pl.program_id(0)
    copies = []
    for dx in range(4):
        for dz in range(4):
            j = 4 * dx + dz
            lanes = pl.ds(pl.multiple_of(jnp.bitwise_xor(j, plane) * 128, 128), 128)
            for n, (first, then, start, size) in enumerate(((dz, dx, 0, ra), (dx, dz, ra, rb))):
                part = (va, vb)[n]
                if first == 2:
                    source = part[2 + then // 2].at[then % 2]
                else:
                    source = part[(0, 1, None, 4)[first]].at[then]
                copies.append(
                    pltpu.make_async_copy(source, w_ref.at[pl.ds(start, size), lanes], sems.at[2 * j + n])
                )
    back = pltpu.make_async_copy(w_ref, w_out, sems.at[32])

    @pl.when(step == 0)
    def _():
        for copy in copies:
            copy.start()
        for copy in copies:
            copy.wait()
        back.start()

    keys = 2 * kwide
    x = x_ref[...]
    q = dot(x, w_ref[:kwide, :], NT).astype(bf16)
    k = dot(x, w_ref[kwide:keys, :], NT).astype(bf16)
    v = dot(x, w_ref[keys + wide : keys + 2 * wide, :], NT).astype(bf16)
    gate = dot(x, w_ref[keys + 2 * wide :, :], NT)
    q_ref[...], k_ref[...], v_ref[...], gate_ref[...] = q, k, v, gate
    weights = (dot(q, k, NT) * decay_ref[...]).astype(bf16)
    retained = dot(weights, v)
    retained_ref[...] = retained
    center = retained - jnp.mean(retained, axis=-1, keepdims=True)
    spread = jnp.mean(center * center, axis=-1, keepdims=True)
    normed = center * lax.rsqrt(spread + group_eps)
    mixed = (gate * jax.nn.sigmoid(gate) * normed * gain_ref[...]).astype(bf16)
    mixed_ref[...] = mixed.T
    wo = w_ref[keys : keys + wide, :]
    send_ref[...] = dot(mixed[half:], wo).astype(bf16)
    keep_ref[...] = dot(mixed[:half], wo)

    @pl.when(step == 1)
    def _():
        back.wait()


def mixer_forward(blocks, x, decay, gain, kwide):
    total, width = x.shape
    rows = decay.shape[0]
    wide = gain.shape[1]
    size = 2 * kwide + 3 * wide
    slim = pl.BlockSpec((rows, kwide), lambda i: (i, 0))
    whole = pl.BlockSpec((rows, wide), lambda i: (i, 0))
    part = pl.BlockSpec((rows // 2, width), lambda i: (i, 0))
    return pl.pallas_call(
        mixer_kernel,
        grid=(2,),
        out_shape=(
            jax.ShapeDtypeStruct((size, width), bf16),
            jax.ShapeDtypeStruct((total, kwide), bf16),
            jax.ShapeDtypeStruct((total, kwide), bf16),
            jax.ShapeDtypeStruct((total, wide), bf16),
            jax.ShapeDtypeStruct((total, wide), f32),
            jax.ShapeDtypeStruct((total, wide), f32),
            jax.ShapeDtypeStruct((wide, total), bf16),
            jax.ShapeDtypeStruct((rows, width), f32),
            jax.ShapeDtypeStruct((rows, width), bf16),
        ),
        in_specs=[ANY] * 10
        + [
            pl.BlockSpec((rows, width), lambda i: (i, 0)),
            pl.BlockSpec((rows, rows), lambda i: (0, 0)),
            pl.BlockSpec((1, wide), lambda i: (0, 0)),
        ],
        out_specs=(
            ANY,
            slim,
            slim,
            whole,
            whole,
            whole,
            pl.BlockSpec((wide, rows), lambda i: (0, i)),
            part,
            part,
        ),
        scratch_shapes=[pltpu.VMEM((size, width), bf16), pltpu.SemaphoreType.DMA((33,))],
        compiler_params=params(56),
    )(*blocks, x, decay, gain)


def mixer_back_kernel(
    g0_ref, g1_ref, g2_ref, g3_ref, w_ref, q_ref, k_ref, v_ref, gate_ref, decay_ref, gain_ref, retained_ref,
    gq_ref, gk_ref, gv_ref, gate_out_ref, gain_out_ref, grad_ref, wo_ref, sems,
):
    kwide, wide = q_ref.shape[1], v_ref.shape[1]
    rows, half = q_ref.shape[0], g0_ref.shape[0]
    step = pl.program_id(0)
    copies = [
        pltpu.make_async_copy(g_ref, grad_ref.at[pl.ds(i * half, half), :], sems.at[i])
        for i, g_ref in enumerate((g0_ref, g1_ref, g2_ref, g3_ref))
    ]
    weight = pltpu.make_async_copy(w_ref.at[pl.ds(2 * kwide, wide), :], wo_ref, sems.at[4])

    @pl.when(step == 0)
    def _():
        weight.start()
        for copy in copies:
            copy.start()
        weight.wait()
        copies[0].wait()
        copies[1].wait()

    @pl.when(step == 1)
    def _():
        copies[2].wait()
        copies[3].wait()

    grad = dot(grad_ref[pl.ds(pl.multiple_of(step * rows, rows), rows), :], wo_ref[...], NT)
    q, k, v, decay = q_ref[...], k_ref[...], v_ref[...], decay_ref[...]
    gain = gain_ref[...]
    retained = retained_ref[...]
    center = retained - jnp.mean(retained, axis=-1, keepdims=True)
    rstd = lax.rsqrt(jnp.mean(center * center, axis=-1, keepdims=True) + group_eps)
    normed = center * rstd
    gate = gate_ref[...]
    sig = jax.nn.sigmoid(gate)
    grad_normed = grad * normed
    gate_out_ref[...] = (grad_normed * gain * (sig * (1.0 + gate * (1.0 - sig)))).astype(bf16).T
    silu = gate * sig
    gain_part = jnp.sum(grad_normed * silu, axis=0, keepdims=True)

    @pl.when(step == 0)
    def _():
        gain_out_ref[...] = gain_part

    @pl.when(step > 0)
    def _():
        gain_out_ref[...] += gain_part

    y = grad * silu * gain
    back = rstd * (
        y
        - jnp.mean(y, axis=-1, keepdims=True)
        - normed * jnp.mean(y * normed, axis=-1, keepdims=True)
    )
    back = back.astype(bf16)
    weights = (dot(q, k, NT) * decay).astype(bf16)
    grad_scores = (dot(back, v, NT) * decay).astype(bf16)
    gq_ref[...] = dot(grad_scores, k).astype(bf16).T
    gk_ref[...] = dot(q, grad_scores, TN).astype(bf16)
    gv_ref[...] = dot(back, weights, TN).astype(bf16)


def mixer_backward(grads, w, q, k, v, gate, decay, gain, retained):
    total, kwide = q.shape
    wide = v.shape[1]
    rows = decay.shape[0]
    slim = pl.BlockSpec((rows, kwide), lambda i: (i, 0))
    whole = pl.BlockSpec((rows, wide), lambda i: (i, 0))
    line = pl.BlockSpec((1, wide), lambda i: (0, 0))
    slim_turned = pl.BlockSpec((kwide, rows), lambda i: (0, i))
    whole_turned = pl.BlockSpec((wide, rows), lambda i: (0, i))
    return pl.pallas_call(
        mixer_back_kernel,
        grid=(2,),
        out_shape=(
            jax.ShapeDtypeStruct((kwide, total), bf16),
            jax.ShapeDtypeStruct((kwide, total), bf16),
            jax.ShapeDtypeStruct((wide, total), bf16),
            jax.ShapeDtypeStruct((wide, total), bf16),
            jax.ShapeDtypeStruct((1, wide), f32),
        ),
        in_specs=[ANY] * 5
        + [slim, slim, whole, whole, pl.BlockSpec((rows, rows), lambda i: (0, 0)), line, whole],
        out_specs=(slim_turned, slim_turned, whole_turned, whole_turned, line),
        scratch_shapes=[
            pltpu.VMEM((total, w.shape[1]), bf16),
            pltpu.VMEM((wide, w.shape[1]), bf16),
            pltpu.SemaphoreType.DMA((5,)),
        ],
        compiler_params=params(48),
    )(*grads, w, q, k, v, gate, decay, gain, retained)


def shards(
    tokens,
    group_length,
    forget_rate,
    mixer_gain,
    feed_gain,
    group_gain,
    w_query,
    w_key,
    w_value,
    w_swish,
    w_output,
    w_gelu,
    w_linear,
    w_down,
    cotangent,
):
    rows, width = tokens.shape
    dp = lax.axis_index("dp")
    tensor = lax.axis_index("tensor")
    plane = dp // 2
    is_low = dp % 2 == 0
    feed_wide = w_gelu.shape[1]
    wide = w_value.shape[1] // 2
    kwide = w_query.shape[1] // 2
    group = 4 * rows
    score_scale = kwide ** (-0.5)
    log_keep = jnp.log1p(-jnp.where(is_low, forget_rate[0], forget_rate[1]))
    valid_rows = (tensor * rows + lax.broadcasted_iota(jnp.int32, (rows, 1), 0) < group_length[0]).astype(f32)

    keep, send = split_weights(
        (w_query, w_key, w_output.T, w_value, w_swish), (w_gelu, w_linear, w_down.T)
    )
    token_float = tokens.astype(f32)
    grad_result = cotangent.astype(f32)
    group_own = jnp.where(is_low, group_gain[:wide], group_gain[wide:]).reshape(1, wide)

    r1 = lax.rsqrt(jnp.mean(token_float * token_float, axis=-1, keepdims=True) + norm_eps)
    normed_in = (token_float * r1 * mixer_gain).astype(bf16)
    got, normed_in = tie(move(send, Y2), normed_in)
    first_a, first_b, second = join_weights(
        keep, got, (kwide, kwide, wide), (wide, wide), (feed_wide,) * 3
    )
    normed_group = gather_line_whole(normed_in)
    grad_feed_out = (valid_rows * grad_result).astype(bf16)
    grad_feed_group = gather_pair(grad_feed_out)

    first = gather_plane(first_a, first_b)
    second = lax.all_gather(second, AXES, axis_index_groups=PLANES, axis=0, tiled=True)
    normed_group, grad_feed_group = tie(normed_group, stacked(*grad_feed_group))

    place = lax.broadcasted_iota(jnp.int32, (group, 1), 0)
    block = place // rows
    order = jnp.where(block == 1, 2, jnp.where(block == 2, 1, block))
    position = jnp.bitwise_xor(tensor, order) * rows + place % rows
    offset = position - position.reshape(1, -1)
    decay = jnp.where(
        offset >= 0, jnp.exp(jnp.maximum(offset, 0).astype(f32) * log_keep) * score_scale, 0.0
    )
    w_mixer, q, k, v, gate, retained, mixed, keep, send = mixer_forward(
        first, normed_group, decay, group_own, kwide
    )
    (mixer_out,) = scatter_line(keep, send)
    middle = token_float + valid_rows * mixer_out
    r2 = lax.rsqrt(jnp.mean(middle * middle, axis=-1, keepdims=True) + norm_eps)
    normed_mid = (middle * r2 * feed_gain).astype(bf16)
    mid = gather_pair(normed_mid)
    hidden, grad_gelu, grad_linear, keep, send = feed_forward_back(second, *mid, grad_feed_group)
    early, feed_keep, feed_send = early_gradients(
        hidden, grad_gelu, grad_linear, *mid, grad_feed_group, second
    )
    grad_normed_mid, early, feed_keep, feed_send = scatter_pair(keep, send, early, feed_keep, feed_send)
    early_sum = lax.psum_scatter(
        early.reshape(-1, 128), AXES, axis_index_groups=PLANES, scatter_dimension=0, tiled=True
    )

    part_feed_gain = jnp.sum(grad_normed_mid * middle * r2, axis=0)
    z2 = grad_normed_mid * feed_gain
    grad_middle = (
        grad_result + r2 * z2 - middle * (r2 * r2 * r2) * jnp.mean(z2 * middle, axis=-1, keepdims=True)
    )
    grad_mixer_out = (valid_rows * grad_middle).astype(bf16)
    grad_mixer = gather_line(grad_mixer_out)
    *grad_mixer, feed_send = tie(*grad_mixer, feed_send)
    gq, gk, gv, gs, part_group_gain = mixer_backward(
        grad_mixer, w_mixer, q, k, v, gate, decay, group_own, retained
    )
    a, b = late_gradients(plane, gq, gk, mixed, gv, gs, normed_group, grad_mixer)
    a, b, gq, feed_got = tie(a, b, gq, move(feed_send, C1))

    back, part_mixer_gain = input_gradients(gq, gk, gv, gs, w_mixer, normed_group)
    feed_keep = feed_keep + feed_got.astype(f32)
    feed_far = move(feed_keep[rows:].astype(bf16), Y1)
    *moved, back, part_mixer_gain, feed_far = tie(
        *scatter_start(a, b), back, part_mixer_gain, feed_far
    )
    result = (middle + valid_rows * (feed_keep[:rows] + feed_far.astype(f32))).astype(bf16)
    a3, a1, b3, b1 = scatter_add(a, b, moved, 2, 2)
    moved = move(a3, Z3), move(a1, Z1), move(b3, X3), move(b1, X1)
    gains = jnp.concatenate([part_mixer_gain.reshape(-1) / mixer_gain, part_feed_gain])
    for pairs in (C1, Y1, Y2):
        gains = gains + move(gains, pairs)
    part_group_gain = part_group_gain.reshape(-1)
    group_far = move(part_group_gain, Y2)
    gains = jnp.concatenate(
        [
            gains,
            jnp.where(is_low, part_group_gain, group_far),
            jnp.where(is_low, group_far, part_group_gain),
        ]
    )
    gains = gains + move(gains, X1)
    r3, r1_, s3, s1, gains, early_sum, back = tie(*moved, gains, early_sum, back)
    grad_normed_in = lax.psum_scatter(
        back, AXES, axis_index_groups=LINES, scatter_dimension=0, tiled=True
    ).astype(f32)
    a, b = tie(add_low(a[0], r3, r1_), add_low(b[0], s3, s1))
    ha, hb = a.shape[1] // 32 * 16, b.shape[1] // 32 * 16
    *moved, gains = tie(
        move(a[2, :ha], X1),
        move(a[2, ha:], X3),
        move(b[2, :hb], Z1),
        move(b[2, hb:], Z3),
        gains + move(gains, X2),
    )
    a3, a1, b3, b1 = scatter_add(a, b, moved, ha, hb)
    r3, r1_, s3, s1, gains, g_gelu, g_linear, g_down = tie(
        move(a3, X3),
        move(a1, X1),
        move(b3, Z3),
        move(b1, Z1),
        gains + move(gains, Z1),
        *settle_early(early_sum),
    )
    sum_a, sum_b = add_low(a[0], r3, r1_), add_low(b[0], s3, s1)
    gains = gains + move(gains, Z2)
    z1 = grad_normed_in * mixer_gain
    grad_tokens = (
        grad_middle + r1 * z1 - token_float * (r1 * r1 * r1) * jnp.mean(z1 * token_float, axis=-1, keepdims=True)
    ).astype(bf16)

    g_query, g_key, g_output, g_value, g_swish = settle_late(
        sum_a, sum_b, (kwide, kwide, wide, wide, wide)
    )

    return (
        result,
        grad_tokens,
        gains[:width],
        gains[width : 2 * width],
        gains[2 * width :],
        g_query,
        g_key,
        g_value,
        g_swish,
        g_output.T,
        g_gelu,
        g_linear,
        g_down.T,
    )


def solution(mesh):
    weight = P("dp", "tensor")
    turned = P("tensor", "dp")
    rows = P(("dp", "tensor"), None)
    return jax.shard_map(
        shards,
        mesh=mesh,
        in_specs=(
            rows,
            P("dp"),
            P("tensor"),
            P(),
            P(),
            P("tensor"),
            weight,
            weight,
            weight,
            weight,
            turned,
            weight,
            weight,
            turned,
            rows,
        ),
        out_specs=(
            rows,
            rows,
            P(),
            P(),
            P("tensor"),
            weight,
            weight,
            weight,
            weight,
            turned,
            weight,
            weight,
            turned,
        ),
        check_vma=False,
    )
```

```python
import functools

import jax
import jax.numpy as jnp
from jax import lax
from jax.experimental import pallas as pl
from jax.experimental.pallas import tpu as pltpu
from jax.sharding import PartitionSpec as P

norm_eps = 1e-05
group_eps = 1.0
AXES = ("dp", "tensor")
f32 = jnp.float32
bf16 = jnp.bfloat16
NN = (((1,), (0,)), ((), ()))
NT = (((1,), (1,)), ((), ()))
TN = (((0,), (0,)), ((), ()))
MB = 1 << 20
VMEM = pl.BlockSpec(memory_space=pltpu.VMEM)
ANY = pl.BlockSpec(memory_space=pl.ANY)


def device_index(x, z, y, c):
    return ((x * 4 + z) * 2 + y // 2) * 4 + (y % 2) * 2 + c


def xor_pairs(dx=0, dz=0, dy=0, dc=0):
    return [
        (device_index(x, z, y, c), device_index(x ^ dx, z ^ dz, y ^ dy, c ^ dc))
        for x in range(4)
        for z in range(4)
        for y in range(4)
        for c in range(2)
    ]


X1, X2, X3 = (xor_pairs(dx=d) for d in (1, 2, 3))
Z1, Z2, Z3 = (xor_pairs(dz=d) for d in (1, 2, 3))
Y1, Y2, Y3 = (xor_pairs(dy=d) for d in (1, 2, 3))
C1 = xor_pairs(dc=1)
LINES = [
    [device_index(x, z, y, c) for y in range(4) for c in range(2)]
    for x in range(4)
    for z in range(4)
]
LINE_ORDER = ((0, 0), (1, 0), (0, 1), (1, 1), (2, 0), (3, 0), (2, 1), (3, 1))
PLANES = [
    [device_index(x, z, y, c) for x in range(4) for z in range(4)]
    for y in range(4)
    for c in range(2)
]


def move(value, pairs):
    return lax.ppermute(value, AXES, pairs)


def tie(*values):
    return lax.optimization_barrier(values)


def dot(left, right, dims=NN):
    return lax.dot_general(left, right, dims, preferred_element_type=f32)


def params(mb):
    return pltpu.CompilerParams(vmem_limit_bytes=mb * MB)


def cost(flops, moved):
    return pl.CostEstimate(flops=flops, bytes_accessed=moved, transcendentals=0)


def up128(n):
    return n + (-n % 128)


def stacked(*parts):
    return jnp.concatenate(parts, axis=0)


def split_kernel(*refs):
    ins, (keep_ref, send_ref, pack_ref), held, sems = refs[:8], refs[8:11], refs[11:19], refs[19]
    copies = [pltpu.make_async_copy(i, h, sems.at[n]) for n, (i, h) in enumerate(zip(ins, held))]
    for copy in copies:
        copy.start()
    low = lax.axis_index("dp") % 2 == 0
    place = 0
    for n, ref in enumerate(held[:5]):
        copies[n].wait()
        half = ref.shape[1] // 2
        left, right = ref[:, :half], ref[:, half:]
        keep_ref[:, place : place + half] = jnp.where(low, left, right)
        send_ref[:, place : place + half] = jnp.where(low, right, left)
        place += up128(half)
    place = 0
    for n, ref in enumerate(held[5:]):
        copies[5 + n].wait()
        pack_ref[:, place : place + ref.shape[1]] = ref[...]
        place += up128(ref.shape[1])


def split_weights(mixer, feed):
    size = sum(up128(w.shape[1] // 2) for w in mixer)
    pack = sum(up128(w.shape[1]) for w in feed)
    return pl.pallas_call(
        split_kernel,
        out_shape=(
            jax.ShapeDtypeStruct((64, size), bf16),
            jax.ShapeDtypeStruct((64, size), bf16),
            jax.ShapeDtypeStruct((64, pack), bf16),
        ),
        in_specs=[ANY] * 8,
        scratch_shapes=[pltpu.VMEM(w.shape, bf16) for w in (*mixer, *feed)]
        + [pltpu.SemaphoreType.DMA((8,))],
        compiler_params=params(63),
    )(*mixer, *feed)


def join_kernel(groups, keep_ref, got_ref, *out_refs):
    low = lax.axis_index("dp") % 2 == 0
    place = 0
    for sizes, out_ref in zip(groups, out_refs):
        row = 0
        for size in sizes:
            wide = up128(size)
            keep, got = keep_ref[:, place : place + wide], got_ref[:, place : place + wide]
            both = stacked(jnp.where(low, keep, got), jnp.where(low, got, keep))
            out_ref[row : row + size, :] = both.T[:size]
            place += wide
            row += size


def join_weights(keep, got, *groups):
    out = pl.pallas_call(
        functools.partial(join_kernel, groups),
        out_shape=tuple(jax.ShapeDtypeStruct((sum(sizes), 128), bf16) for sizes in groups),
        compiler_params=params(16),
    )(keep, got)
    return out


def pick_kernel(starts, *refs):
    count = len(starts)
    ins, outs, sems = refs[:count], refs[count : 2 * count], refs[2 * count]
    copies = [
        pltpu.make_async_copy(i.at[pl.ds(start, o.shape[0])], o, sems.at[n])
        for n, (i, o, start) in enumerate(zip(ins, outs, starts))
    ]
    for copy in copies:
        copy.start()
    for copy in copies:
        copy.wait()


def pick(values, starts, sizes):
    return pl.pallas_call(
        functools.partial(pick_kernel, starts),
        out_shape=tuple(
            jax.ShapeDtypeStruct((n, *v.shape[1:]), v.dtype) for v, n in zip(values, sizes)
        ),
        in_specs=[ANY] * len(values),
        out_specs=(ANY,) * len(values),
        scratch_shapes=[pltpu.SemaphoreType.DMA((len(values),))],
        compiler_params=params(4),
    )(*values)


def gather_plane(a, b, pack, rows):
    a1, a3, b1, b3, a2, b2 = tie(
        move(a, X1), move(a, X3), move(b, Z1), move(b, Z3), move(a, X2), move(b, Z2)
    )
    sa, sb = tie(jnp.stack([a, a1, a2, a3]), jnp.stack([b, b1, b2, b3]))
    sa1, sa3, sb1, sb3, got = tie(
        move(sa, Z1), move(sa, Z3), move(sb, X1), move(sb, X3), move(pack, Y2)
    )
    ap, aq, bp, bq, rows, got = tie(*pick((sa3, sa1, sb3, sb1), (0, 2, 0, 2), (2,) * 4), rows, got)
    sa2p, sa2q, sb2p, sb2q, far = tie(
        move(ap, Z1), move(aq, Z3), move(bp, X1), move(bq, X3), move(rows, Y1)
    )
    return (sa, sa1, sa2p, sa2q, sa3, sb, sb1, sb2p, sb2q, sb3), got, stacked(rows, far)


def add_low(*terms):
    total = terms[0].astype(f32)
    for term in terms[1:]:
        total = total + term.astype(f32)
    return total.astype(bf16)


def fold_kernel(*refs):
    olds, more, outs = refs[:4], refs[4:8], refs[8:12]
    held, sems = refs[12:20], refs[20]
    loads, stores = [], []
    for n in range(4):
        start = 2 * (n % 2)
        loads.append(pltpu.make_async_copy(olds[n].at[pl.ds(start, 2)], held[n], sems.at[n, 0]))
        loads.append(pltpu.make_async_copy(more[n], held[4 + n], sems.at[n, 1]))
        stores.append(pltpu.make_async_copy(held[n], outs[n].at[pl.ds(start, 2)], sems.at[n, 2]))
    for copy in loads:
        copy.start()
    for n in range(4):
        loads[2 * n].wait()
        loads[2 * n + 1].wait()
        held[n][...] = (held[n][...].astype(f32) + held[4 + n][...].astype(f32)).astype(bf16)
        stores[n].start()
    for copy in stores:
        copy.wait()


def fold(a3, a1, b3, b1, ap, aq, bp, bq):
    values, more = (a3, a1, b3, b1), (ap, aq, bp, bq)
    return pl.pallas_call(
        fold_kernel,
        out_shape=tuple(jax.ShapeDtypeStruct(v.shape, v.dtype) for v in values),
        in_specs=[ANY] * 8,
        out_specs=(ANY,) * 4,
        scratch_shapes=[pltpu.VMEM(v.shape, bf16) for v in more * 2] + [pltpu.SemaphoreType.DMA((4, 3))],
        input_output_aliases={i: i for i in range(4)},
        compiler_params=params(63),
    )(*values, *more)


def add_kernel(*refs):
    ins, outs = refs[:6], refs[6:]
    for j in range(4):

        @pl.when(pl.program_id(0) == j)
        def _():
            for n in range(2):
                total = sum(ref[0].astype(f32) for ref in ins[3 * n : 3 * n + 3])
                outs[4 * n + j][...] = total.astype(bf16)


def add_blocks(a, b):
    blocks = [pl.BlockSpec((1, *v.shape[1:]), lambda i: (i, 0, 0)) for v in (*a, *b)]
    outs = [v.shape[1:] for v in (a[0],) * 4 + (b[0],) * 4]
    out = pl.pallas_call(
        add_kernel,
        grid=(4,),
        out_shape=tuple(jax.ShapeDtypeStruct(shape, bf16) for shape in outs),
        in_specs=blocks,
        out_specs=tuple(pl.BlockSpec(shape, lambda i: (0, 0)) for shape in outs),
        compiler_params=params(32),
    )(*a, *b)
    return out[:4], out[4:]


def feed_kernel(
    w_ref, x0_ref, x1_ref, g0_ref, g1_ref, hidden_ref, grads_ref, keep_ref, send_ref,
    held_ref, x_ref, grad_ref, sems,
):
    wide = hidden_ref.shape[0]
    half = x0_ref.shape[0]
    given = [
        pltpu.make_async_copy(x0_ref, x_ref.at[pl.ds(0, half), :], sems.at[48]),
        pltpu.make_async_copy(x1_ref, x_ref.at[pl.ds(half, half), :], sems.at[49]),
    ]
    weights = [
        [
            pltpu.make_async_copy(
                w_ref.at[pl.ds((3 * j + i) * wide, wide), :],
                held_ref.at[pl.ds(i * wide, wide), pl.ds(128 * j, 128)],
                sems.at[16 * i + j],
            )
            for j in range(16)
        ]
        for i in range(3)
    ]
    grads = [
        pltpu.make_async_copy(g0_ref, grad_ref.at[pl.ds(0, half), :], sems.at[50]),
        pltpu.make_async_copy(g1_ref, grad_ref.at[pl.ds(half, half), :], sems.at[51]),
    ]
    for copy in given + weights[0] + weights[1] + grads + weights[2]:
        copy.start()
    for copy in given + weights[0]:
        copy.wait()
    up, down, last = (slice(n * wide, (n + 1) * wide) for n in range(3))
    gelu_in = dot(held_ref[up, :], x_ref[...], NT)
    for copy in weights[1]:
        copy.wait()
    linear_in = dot(held_ref[down, :], x_ref[...], NT)
    for copy in grads + weights[2]:
        copy.wait()
    back = dot(held_ref[last, :], grad_ref[...], NT)
    cdf = 0.5 * (1.0 + lax.erf(gelu_in * (0.5**0.5)))
    gelu = gelu_in * cdf
    slope = cdf + gelu_in * jnp.exp(-0.5 * gelu_in * gelu_in) * 0.3989422804014327
    hidden_ref[...] = (gelu * linear_in).astype(bf16)
    grads_ref[up, :] = (back * linear_in * slope).astype(bf16)
    grads_ref[down, :] = (back * gelu).astype(bf16)
    for rows, out_ref in ((slice(half, 2 * half), send_ref), (slice(0, half), keep_ref)):
        out_ref[...] = dot(grads_ref[:, rows], held_ref[: 2 * wide, :], TN).astype(out_ref.dtype)


def feed_forward_back(w, x0, x1, g0, g1):
    half, width = x0.shape
    wide = w.shape[0] // 48
    return pl.pallas_call(
        feed_kernel,
        out_shape=(
            jax.ShapeDtypeStruct((wide, 2 * half), bf16),
            jax.ShapeDtypeStruct((2 * wide, 2 * half), bf16),
            jax.ShapeDtypeStruct((half, width), f32),
            jax.ShapeDtypeStruct((half, width), bf16),
        ),
        in_specs=[ANY] * 5,
        scratch_shapes=[
            pltpu.VMEM((3 * wide, width), bf16),
            pltpu.VMEM((2 * half, width), bf16),
            pltpu.VMEM((2 * half, width), bf16),
            pltpu.SemaphoreType.DMA((52,)),
        ],
        cost_estimate=cost(20 * half * wide * width, 10 * wide * width),
        compiler_params=params(63),
    )(w, x0, x1, g0, g1)


def early_kernel(
    hidden_ref, grads_ref, x0_ref, x1_ref, g0_ref, g1_ref, w_ref, out_ref, keep_ref, send_ref, turn_ref
):
    wide = hidden_ref.shape[0]
    half = x0_ref.shape[0]

    @pl.when(pl.program_id(0) == 0)
    def _():
        turn_ref[...] = hidden_ref[...].T

    up = dot(grads_ref[...], stacked(x0_ref[...], x1_ref[...])).astype(bf16)
    down = dot(hidden_ref[...], stacked(g0_ref[...], g1_ref[...])).astype(bf16)
    for i in range(4):
        lanes = slice(128 * i, 128 * i + 128)
        out_ref[i, : 2 * wide, :] = up[:, lanes]
        out_ref[i, 2 * wide :, :] = down[:, lanes]
    w = jnp.concatenate([w_ref[i] for i in range(4)], axis=1)
    keep_ref[...] = dot(turn_ref[:half, :], w).astype(bf16)
    send_ref[...] = dot(turn_ref[half:, :], w).astype(bf16)


def early_gradients(hidden, grads, x0, x1, g0, g1, w):
    wide, rows = hidden.shape
    half, width = x0.shape
    block = pl.BlockSpec((half, 512), lambda i: (0, i))
    return pl.pallas_call(
        early_kernel,
        grid=(4,),
        out_shape=(
            jax.ShapeDtypeStruct((16, 3 * wide, 128), bf16),
            jax.ShapeDtypeStruct((half, width), bf16),
            jax.ShapeDtypeStruct((half, width), bf16),
        ),
        in_specs=[
            pl.BlockSpec((wide, rows), lambda i: (0, 0)),
            pl.BlockSpec((2 * wide, rows), lambda i: (0, 0)),
            block,
            block,
            block,
            block,
            pl.BlockSpec((4, wide, 128), lambda i: (i, 2, 0)),
        ],
        out_specs=(pl.BlockSpec((4, 3 * wide, 128), lambda i: (i, 0, 0)), block, block),
        scratch_shapes=[pltpu.VMEM((rows, wide), bf16)],
        cost_estimate=cost(14 * half * wide * width, 10 * wide * width),
        compiler_params=params(63),
    )(hidden, grads, x0, x1, g0, g1, w.reshape(16, 3 * wide, 128))


def parts_kernel(steps, g_in, o_in, x_in, *refs):
    m_in, refs = refs[:4], refs[4:]
    outs, (g_ref, o_ref, x_ref, m_ref, sems) = refs[:-5], refs[-5:]
    plane = lax.axis_index("dp") // 2
    wide = o_ref.shape[0]
    keys = g_ref.shape[0] - 2 * wide
    size = m_in[0].shape[0]

    def lanes(dx, dz):
        return pl.ds(pl.multiple_of(jnp.bitwise_xor(4 * dx + dz, plane) * 128, 128), 128)

    fixed = [
        pltpu.make_async_copy(g_in.at[pl.ds(0, keys)], g_ref.at[pl.ds(0, keys)], sems.at[0]),
        pltpu.make_async_copy(g_in.at[pl.ds(keys, 2 * wide)], g_ref.at[pl.ds(keys, 2 * wide)], sems.at[1]),
        pltpu.make_async_copy(o_in, o_ref, sems.at[2]),
    ]
    waits = []
    for n, d in enumerate(steps):
        base = 3 + 24 * n
        copies = [[], [], []]
        for i in range(4):
            here = pl.ds(128 * i, 128)
            for k, at in enumerate((lanes(i, d), lanes(d, i))):
                copies[k].append(
                    pltpu.make_async_copy(
                        x_in.at[:, at], x_ref.at[2 * n + k, :, here], sems.at[base + 4 * k + i]
                    )
                )
            for k, m in enumerate(m_in):
                copies[2].append(
                    pltpu.make_async_copy(
                        m.at[:, lanes(i, d)],
                        m_ref.at[n, pl.ds(k * size, size), here],
                        sems.at[base + 8 + 4 * i + k],
                    )
                )
        if n == 0:
            for k in range(3):
                copies[k].append(fixed[k])
        waits.append(copies)
    for copies in waits:
        for part in copies:
            for copy in part:
                copy.start()

    per = len(outs) // len(steps) // 2

    def store(value, refs, rows):
        value = value.astype(bf16)
        for i in range(4):
            refs[i * per // 4][i % (4 // per), rows, :] = value[:, 128 * i : 128 * i + 128]

    for n in range(len(steps)):
        a_refs = outs[2 * per * n : 2 * per * n + per]
        b_refs = outs[2 * per * n + per : 2 * per * (n + 1)]
        for copy in waits[n][0]:
            copy.wait()
        store(dot(g_ref[:keys, :], x_ref[2 * n]), a_refs, slice(wide, wide + keys))
        for copy in waits[n][1]:
            copy.wait()
        store(dot(g_ref[keys:, :], x_ref[2 * n + 1]), b_refs, slice(0, 2 * wide))
        for copy in waits[n][2]:
            copy.wait()
        store(dot(o_ref[...], m_ref[n]), a_refs, slice(0, wide))


def gradient_parts(steps, per, g, o, x, m):
    wide, rows = o.shape
    rb = 2 * wide
    ra = g.shape[0] - rb + wide
    shapes = ([(4 // per, ra, 128)] * per + [(4 // per, rb, 128)] * per) * len(steps)
    return pl.pallas_call(
        functools.partial(parts_kernel, steps),
        grid=(1,),
        out_shape=tuple(jax.ShapeDtypeStruct(shape, bf16) for shape in shapes),
        in_specs=[ANY] * 7,
        out_specs=tuple(pl.BlockSpec(shape, lambda i: (0, 0, 0)) for shape in shapes),
        scratch_shapes=[
            pltpu.VMEM(g.shape, bf16),
            pltpu.VMEM(o.shape, bf16),
            pltpu.VMEM((2 * len(steps), rows, 512), bf16),
            pltpu.VMEM((len(steps), rows, 512), bf16),
            pltpu.SemaphoreType.DMA((3 + 24 * len(steps),)),
        ],
        cost_estimate=cost(rows * 512 * (ra + rb) * 2 * len(steps), 6 * rows * 2048),
        compiler_params=params(63),
    )(g, o, x, *m)


def early_out_kernel(sum_ref, keep_ref, send_ref):
    low = lax.axis_index("dp") % 2 == 0
    wide = sum_ref.shape[0] // 3
    for i in range(3):
        flat = sum_ref[i * wide : (i + 1) * wide, :].T
        place = slice(i * up128(wide), i * up128(wide) + wide)
        keep_ref[:, place] = jnp.where(low, flat[:64], flat[64:])
        send_ref[:, place] = jnp.where(low, flat[64:], flat[:64])


def early_end_kernel(keep_ref, got_ref, *out_refs):
    wide = out_refs[0].shape[1]
    for i, out_ref in enumerate(out_refs):
        place = slice(i * up128(wide), i * up128(wide) + wide)
        out_ref[...] = keep_ref[:, place].astype(f32) + got_ref[:, place].astype(f32)


def settle_early(summed):
    wide = summed.shape[0] // 3
    flat = jax.ShapeDtypeStruct((64, 3 * up128(wide)), bf16)
    keep, send = pl.pallas_call(
        early_out_kernel, out_shape=(flat, flat), compiler_params=params(16)
    )(summed)
    return pl.pallas_call(
        early_end_kernel,
        out_shape=(jax.ShapeDtypeStruct((64, wide), f32),) * 3,
        compiler_params=params(16),
    )(keep, move(send, Y2))


def late_out_kernel(sizes, *refs):
    a_refs, b_refs, (keep_ref, send_ref) = refs[:4], refs[4:8], refs[8:]
    low = lax.axis_index("dp") % 2 == 0
    place, row, parts = 0, 0, a_refs
    for size in sizes:
        if row == parts[0].shape[0]:
            row, parts = 0, b_refs
        total = sum(ref[row : row + size, :].astype(f32) for ref in parts)
        flat = total.astype(bf16).T
        keep_ref[:, place : place + size] = jnp.where(low, flat[:64], flat[64:])
        send_ref[:, place : place + size] = jnp.where(low, flat[64:], flat[:64])
        row += size
        place += up128(size)


def late_end_kernel(keep_ref, got_ref, *out_refs):
    low = lax.axis_index("dp") % 2 == 0
    place = 0
    for out_ref in out_refs:
        size = out_ref.shape[1] // 2
        keep = keep_ref[:, place : place + size].astype(f32)
        got = got_ref[:, place : place + size].astype(f32)
        out_ref[:, :size] = jnp.where(low, keep, got)
        out_ref[:, size:] = jnp.where(low, got, keep)
        place += up128(size)


def settle_late(a, b, sizes):
    flat = jax.ShapeDtypeStruct((64, sum(up128(n) for n in sizes)), bf16)
    keep, send = pl.pallas_call(
        functools.partial(late_out_kernel, sizes), out_shape=(flat, flat), compiler_params=params(16)
    )(*a, *b)
    return pl.pallas_call(
        late_end_kernel,
        out_shape=tuple(jax.ShapeDtypeStruct((64, 2 * n), f32) for n in sizes),
        compiler_params=params(16),
    )(keep, move(send, Y2))


def line_place(block):
    dp, tensor = lax.axis_index("dp"), lax.axis_index("tensor")
    y, c = dp % 2 * 2 + tensor // 2, tensor % 2
    dy, dc = LINE_ORDER[block]
    return jnp.bitwise_xor(y, dy) * 2 + jnp.bitwise_xor(c, dc)


def back_kernel(g_ref, w_ref, x_ref, out_ref, gain_ref, held_ref, sems):
    rows = g_ref.shape[1] // 4
    step = pl.program_id(0)
    total = dot(g_ref[...], w_ref[w_ref.shape[0] - g_ref.shape[0] :, :], TN)
    held_ref[...] = total.astype(bf16)
    copies = []
    for j in range(4):
        where = jnp.where(step == 0, line_place(j), line_place(j + 4))
        copies.append(
            pltpu.make_async_copy(
                held_ref.at[pl.ds(j * rows, rows), :],
                out_ref.at[pl.ds(pl.multiple_of(where * rows, rows), rows), :],
                sems.at[j],
            )
        )
    for copy in copies:
        copy.start()
    gain = jnp.sum(total * x_ref[...].astype(f32), axis=0, keepdims=True)

    @pl.when(step == 0)
    def _():
        gain_ref[...] = gain

    @pl.when(step > 0)
    def _():
        gain_ref[...] += gain

    for copy in copies:
        copy.wait()


def input_gradients(g, w, x):
    size, total = g.shape
    width = w.shape[1]
    half = total // 2
    return pl.pallas_call(
        back_kernel,
        grid=(2,),
        out_shape=(
            jax.ShapeDtypeStruct((total, width), bf16),
            jax.ShapeDtypeStruct((1, width), f32),
        ),
        in_specs=[
            pl.BlockSpec((size, half), lambda i: (0, i)),
            pl.BlockSpec(w.shape, lambda i: (0, 0)),
            pl.BlockSpec((half, width), lambda i: (i, 0)),
        ],
        out_specs=(ANY, pl.BlockSpec((1, width), lambda i: (0, 0))),
        scratch_shapes=[pltpu.VMEM((half, width), bf16), pltpu.SemaphoreType.DMA((4,))],
        cost_estimate=cost(2 * size * total * width, 10 * total * width),
        compiler_params=params(63),
    )(g, w, x)


def gather_line_first(own, *beside):
    r1, r3, *beside = tie(move(own, Y1), move(own, Y3), *beside)
    mine = stacked(own, r1)
    half = own.shape[0] // 2
    return (mine, move(mine, C1)), (move(r3[:half], Y1), move(r1[half:], Y3), r3), beside


def gather_line_last(r2p, r2q, r3):
    other = stacked(r2p, r2q, r3)
    return other, move(other, C1)


def scatter_line(keep_m, send_m, keep_o, send_o):
    rows = keep_m.shape[0] // 2
    half = rows // 2
    o = keep_o.astype(f32) + move(send_o, C1).astype(f32)
    s2 = o[:rows].astype(bf16)
    t3, t1 = tie(move(s2[:half], Y1), move(s2[half:], Y3))
    m = keep_m.astype(f32) + move(send_m, C1).astype(f32)
    s3 = stacked(o[rows : rows + half] + t3.astype(f32), o[rows + half :]).astype(bf16)
    s1 = stacked(m[rows : rows + half], m[rows + half :] + t1.astype(f32)).astype(bf16)
    u3, u1 = tie(move(s3, Y3), move(s1, Y1))
    return m[:rows] + u3.astype(f32) + u1.astype(f32)


def gather_pair(own):
    mine = stacked(own, move(own, Y1))
    return mine, move(mine, C1)


def scatter_pair(keep, send, *beside):
    rows = keep.shape[0] // 2
    m = keep + move(send, C1).astype(f32)
    u1, *beside = tie(move(m[rows:].astype(bf16), Y1), *beside)
    return (m[:rows] + u1.astype(f32), *beside)


def mixer_kernel(*refs):
    blocks, (line_ref, decay_ref, gain_ref) = refs[:10], refs[10:13]
    w_out, x_out, q_ref, k_ref, v_ref, gate_ref, retained_ref, mixed_ref = refs[13:21]
    parts, (w_ref, x_ref, sems) = refs[21:25], refs[25:]
    va, vb = blocks[:5], blocks[5:]
    kwide, wide = q_ref.shape[1], v_ref.shape[1]
    rows, half = q_ref.shape[0], parts[0].shape[0]
    plane = lax.axis_index("dp") // 2
    ra, rb = va[0].shape[1], vb[0].shape[1]
    keys = 2 * kwide
    step = pl.program_id(0)
    copies = []
    for dx in range(4):
        for dz in range(4):
            j = 4 * dx + dz
            lanes = pl.ds(pl.multiple_of(jnp.bitwise_xor(j, plane) * 128, 128), 128)
            for n, (part, first, then, row, size) in enumerate(((va, dz, dx, 0, ra), (vb, dx, dz, ra, rb))):
                if first == 2:
                    source = part[2 + then // 2].at[then % 2]
                else:
                    source = part[(0, 1, None, 4)[first]].at[then]
                copies.append(
                    pltpu.make_async_copy(
                        source, w_ref.at[pl.ds(row, size), lanes], sems.at[2 * j + n]
                    )
                )
    size = rows // 4
    given = [
        pltpu.make_async_copy(
            line_ref.at[pl.ds(pl.multiple_of(line_place(j) * size, size), size), :],
            x_ref.at[pl.ds(j * size, size), :],
            sems.at[32 + j],
        )
        for j in range(8)
    ]
    w_back = pltpu.make_async_copy(w_ref, w_out, sems.at[40])
    x_back = pltpu.make_async_copy(x_ref, x_out, sems.at[41])

    @pl.when(step == 0)
    def _():
        for copy in given[:4] + copies + given[4:]:
            copy.start()
        for copy in given[:4] + copies:
            copy.wait()
        w_back.start()

    @pl.when(step == 1)
    def _():
        for copy in given[4:]:
            copy.wait()
        x_back.start()

    x = x_ref[pl.ds(pl.multiple_of(step * rows, rows), rows), :]
    both = dot(x, w_ref[wide : keys + 2 * wide, :], NT).astype(bf16)
    q, k, v = both[:, :kwide], both[:, kwide:keys], both[:, keys:]
    gate = dot(x, w_ref[keys + 2 * wide :, :], NT)
    q_ref[...], k_ref[...], v_ref[...], gate_ref[...] = q, k, v, gate
    weights = (dot(q, k, NT) * decay_ref[...]).astype(bf16)
    retained = dot(weights, v)
    retained_ref[...] = retained
    center = retained - jnp.mean(retained, axis=-1, keepdims=True)
    spread = jnp.mean(center * center, axis=-1, keepdims=True)
    normed = center * lax.rsqrt(spread + group_eps)
    mixed = (gate * jax.nn.sigmoid(gate) * normed * gain_ref[...]).astype(bf16)
    mixed_ref[...] = mixed.T
    wo = w_ref[:wide, :]
    send, keep = dot(mixed[half:], wo).astype(bf16), dot(mixed[:half], wo).astype(bf16)

    @pl.when(step == 0)
    def _():
        parts[0][...], parts[1][...] = keep, send

    @pl.when(step == 1)
    def _():
        parts[2][...], parts[3][...] = keep, send
        w_back.wait()
        x_back.wait()


def mixer_forward(blocks, line, decay, gain, kwide):
    total, width = line.shape
    rows = decay.shape[0]
    wide = gain.shape[1]
    size = 2 * kwide + 3 * wide
    slim = pl.BlockSpec((rows, kwide), lambda i: (i, 0))
    whole = pl.BlockSpec((rows, wide), lambda i: (i, 0))
    part = pl.BlockSpec((rows // 2, width), lambda i: (0, 0))
    return pl.pallas_call(
        mixer_kernel,
        grid=(2,),
        out_shape=(
            jax.ShapeDtypeStruct((size, width), bf16),
            jax.ShapeDtypeStruct((total, width), bf16),
            jax.ShapeDtypeStruct((total, kwide), bf16),
            jax.ShapeDtypeStruct((total, kwide), bf16),
            jax.ShapeDtypeStruct((total, wide), bf16),
            jax.ShapeDtypeStruct((total, wide), f32),
            jax.ShapeDtypeStruct((total, wide), f32),
            jax.ShapeDtypeStruct((wide, total), bf16),
        )
        + (jax.ShapeDtypeStruct((rows // 2, width), bf16),) * 4,
        in_specs=[ANY] * 11
        + [
            pl.BlockSpec((rows, rows), lambda i: (0, 0)),
            pl.BlockSpec((1, wide), lambda i: (0, 0)),
        ],
        out_specs=(
            ANY,
            ANY,
            slim,
            slim,
            whole,
            whole,
            whole,
            pl.BlockSpec((wide, rows), lambda i: (0, i)),
            part,
            part,
            part,
            part,
        ),
        scratch_shapes=[
            pltpu.VMEM((size, width), bf16),
            pltpu.VMEM((total, width), bf16),
            pltpu.SemaphoreType.DMA((42,)),
        ],
        cost_estimate=cost(2 * size * total * width, 16 * total * width),
        compiler_params=params(63),
    )(*blocks, line, decay, gain)


def mixer_back_kernel(
    g0_ref, g1_ref, w_ref, q_ref, k_ref, v_ref, gate_ref, decay_ref, gain_ref, retained_ref, *refs
):
    out_ref, gain_out_ref, grad_ref, wo_ref, sems = refs[-5:]
    kwide, wide = q_ref.shape[1], v_ref.shape[1]
    keys = 2 * kwide
    half = g0_ref.shape[0]
    copies = [
        pltpu.make_async_copy(w_ref.at[pl.ds(0, wide), :], wo_ref, sems.at[2]),
        pltpu.make_async_copy(g0_ref, grad_ref.at[pl.ds(0, half), :], sems.at[0]),
        pltpu.make_async_copy(g1_ref, grad_ref.at[pl.ds(half, half), :], sems.at[1]),
    ]
    for copy in copies:
        copy.start()
    q, k, v, decay = q_ref[...], k_ref[...], v_ref[...], decay_ref[...]
    weights = (dot(q, k, NT) * decay).astype(bf16)
    gain = gain_ref[...]
    retained = retained_ref[...]
    center = retained - jnp.mean(retained, axis=-1, keepdims=True)
    rstd = lax.rsqrt(jnp.mean(center * center, axis=-1, keepdims=True) + group_eps)
    normed = center * rstd
    gate = gate_ref[...]
    sig = jax.nn.sigmoid(gate)
    silu = gate * sig
    for copy in copies:
        copy.wait()
    grad = dot(grad_ref[...], wo_ref[...], NT)
    grad_normed = grad * normed
    out_ref[keys + wide :, :] = (grad_normed * gain * (sig * (1.0 + gate * (1.0 - sig)))).astype(bf16).T
    gain_out_ref[...] = jnp.sum(grad_normed * silu, axis=0, keepdims=True)
    y = grad * silu * gain
    back = rstd * (
        y
        - jnp.mean(y, axis=-1, keepdims=True)
        - normed * jnp.mean(y * normed, axis=-1, keepdims=True)
    )
    back = back.astype(bf16)
    grad_scores = (dot(back, v, NT) * decay).astype(bf16)
    out_ref[keys : keys + wide, :] = dot(back, weights, TN).astype(bf16)
    out_ref[kwide:keys, :] = dot(q, grad_scores, TN).astype(bf16)
    out_ref[:kwide, :] = dot(grad_scores, k).astype(bf16).T


def mixer_backward(group, grads, w, q, k, v, gate, decay, gain, retained, before=None):
    kwide, wide = q.shape[1], v.shape[1]
    rows = decay.shape[0]
    slim = pl.BlockSpec((rows, kwide), lambda i: (group, 0))
    whole = pl.BlockSpec((rows, wide), lambda i: (group, 0))
    line = pl.BlockSpec((1, wide), lambda i: (0, 0))
    size = 2 * kwide + 2 * wide
    given = [] if before is None else [before]
    return pl.pallas_call(
        mixer_back_kernel,
        grid=(1,),
        out_shape=(
            jax.ShapeDtypeStruct((size, q.shape[0]), bf16),
            jax.ShapeDtypeStruct((1, wide), f32),
        ),
        in_specs=[ANY] * 3
        + [slim, slim, whole, whole, pl.BlockSpec((rows, rows), lambda i: (0, 0)), line, whole]
        + [ANY] * len(given),
        out_specs=(pl.BlockSpec((size, rows), lambda i: (0, group)), line),
        input_output_aliases={10: 0} if given else {},
        scratch_shapes=[
            pltpu.VMEM((rows, w.shape[1]), bf16),
            pltpu.VMEM((wide, w.shape[1]), bf16),
            pltpu.SemaphoreType.DMA((3,)),
        ],
        cost_estimate=cost(2 * rows * (size + wide) * 1024, 8 * rows * 2048),
        compiler_params=params(63),
    )(*grads, w, q, k, v, gate, decay, gain, retained, *given)


def shards(
    tokens,
    group_length,
    forget_rate,
    mixer_gain,
    feed_gain,
    group_gain,
    w_query,
    w_key,
    w_value,
    w_swish,
    w_output,
    w_gelu,
    w_linear,
    w_down,
    cotangent,
):
    rows, width = tokens.shape
    dp = lax.axis_index("dp")
    tensor = lax.axis_index("tensor")
    is_low = dp % 2 == 0
    feed_wide = w_gelu.shape[1]
    wide = w_value.shape[1] // 2
    kwide = w_query.shape[1] // 2
    group = 4 * rows
    score_scale = kwide ** (-0.5)
    log_keep = jnp.log1p(-jnp.where(is_low, forget_rate[0], forget_rate[1]))
    valid_rows = (tensor * rows + lax.broadcasted_iota(jnp.int32, (rows, 1), 0) < group_length[0]).astype(f32)

    keep, send, pack = split_weights(
        (w_output.T, w_query, w_key, w_value, w_swish), (w_gelu, w_linear, w_down.T)
    )

    token_float = tokens.astype(f32)
    grad_result = cotangent.astype(f32)
    group_own = jnp.where(is_low, group_gain[:wide], group_gain[wide:]).reshape(1, wide)

    r1 = lax.rsqrt(jnp.mean(token_float * token_float, axis=-1, keepdims=True) + norm_eps)
    normed_in = (token_float * r1 * mixer_gain).astype(bf16)
    place = lax.broadcasted_iota(jnp.int32, (group, 1), 0)
    block = place // rows
    order = jnp.where(block == 1, 2, jnp.where(block == 2, 1, block))
    position = jnp.bitwise_xor(tensor, order) * rows + place % rows
    offset = position - position.reshape(1, -1)
    decay = jnp.where(
        offset >= 0, jnp.exp(jnp.maximum(offset, 0).astype(f32) * log_keep) * score_scale, 0.0
    )

    got, normed_in, decay = tie(move(send, Y2), normed_in, decay)
    first_a, first_b = join_weights(keep, got, (wide, kwide, kwide), (wide, wide))
    normed_line = lax.all_gather(normed_in, AXES, axis_index_groups=LINES, axis=0, tiled=True)
    grad_feed_out = (valid_rows * grad_result).astype(bf16)
    first, got, grad_feed = gather_plane(first_a, first_b, pack, grad_feed_out)
    (second,) = join_weights(pack, got, (feed_wide,) * 3)
    second = lax.all_gather(second, AXES, axis_index_groups=PLANES, axis=0, tiled=True)

    w_mixer, normed_group, q, k, v, gate, retained, mixed, *parts = mixer_forward(
        first, normed_line, decay, group_own, kwide
    )
    *parts, grad_feed_other = tie(*parts, move(grad_feed, C1))
    grad_feed = grad_feed, grad_feed_other
    mixer_out = scatter_line(*parts)
    middle = token_float + valid_rows * mixer_out
    r2 = lax.rsqrt(jnp.mean(middle * middle, axis=-1, keepdims=True) + norm_eps)
    normed_mid = (middle * r2 * feed_gain).astype(bf16)
    mid = gather_pair(normed_mid)
    hidden, grads, keep, send = feed_forward_back(second, *mid, *grad_feed)
    early, feed_keep, feed_send = early_gradients(
        hidden, grads, *mid, *grad_feed, second
    )
    grad_normed_mid, early, feed_keep, feed_send = scatter_pair(keep, send, early, feed_keep, feed_send)
    early_sum = lax.psum_scatter(
        early.reshape(-1, 128), AXES, axis_index_groups=PLANES, scatter_dimension=0, tiled=True
    )

    part_feed_gain = jnp.sum(grad_normed_mid * middle * r2, axis=0)
    z2 = grad_normed_mid * feed_gain
    grad_middle = (
        grad_result + r2 * z2 - middle * (r2 * r2 * r2) * jnp.mean(z2 * middle, axis=-1, keepdims=True)
    )
    grad_mixer_out = (valid_rows * grad_middle).astype(bf16)
    grad_mixer_out, feed_send = tie(grad_mixer_out, feed_send)
    feed_got = move(feed_send, C1)
    grad_mixer_m, left, (feed_keep, feed_send) = gather_line_first(
        grad_mixer_out,
        feed_keep[:rows].astype(f32) + feed_got[:rows].astype(f32),
        add_low(feed_keep[rows:], feed_got[rows:]),
    )
    grads, gain_m = mixer_backward(
        0, grad_mixer_m, w_mixer, q, k, v, gate, decay, group_own, retained
    )
    left, grads, feed_send = tie(left, grads, feed_send)
    grad_mixer_o = gather_line_last(*left)
    grads, gain_o = mixer_backward(
        1, grad_mixer_o, w_mixer, q, k, v, gate, decay, group_own, retained, grads
    )
    part_group_gain = (gain_m + gain_o).reshape(-1)
    grad_mixer = *grad_mixer_m, *grad_mixer_o
    *sent, grads, feed_far, group_far = tie(
        *gradient_parts((2,), 2, grads, mixed, normed_group, grad_mixer),
        grads,
        move(feed_send, Y1),
        move(part_group_gain, Y2),
    )

    moved = [move(part, pairs) for part, pairs in zip(sent, (Z1, Z3, X1, X3))]
    back, part_mixer_gain = input_gradients(grads, w_mixer, normed_group)
    back, grads = tie(back, grads)
    gains = jnp.concatenate([part_mixer_gain.reshape(-1) / mixer_gain, part_feed_gain])
    *moved, (a1, b1, a3, b3), grads, gains = tie(
        *moved,
        gradient_parts((1, 3), 1, grads, mixed, normed_group, grad_mixer),
        grads,
        gains + move(gains, C1),
    )
    a3, a1, b3, b1, grads, gains = tie(
        *fold(a3, a1, b3, b1, *moved), grads, gains + move(gains, Y1)
    )
    moved = move(a3, Z3), move(a1, Z1), move(b3, X3), move(b1, X1)
    a0, b0 = gradient_parts((0,), 1, grads, mixed, normed_group, grad_mixer)
    result = (middle + valid_rows * (feed_keep + feed_far.astype(f32))).astype(bf16)
    gains = gains + move(gains, Y2)
    gains = jnp.concatenate(
        [
            gains,
            jnp.where(is_low, part_group_gain, group_far),
            jnp.where(is_low, group_far, part_group_gain),
        ]
    )
    back, early_sum, _ = tie(back, early_sum, a3)
    grad_normed_in = lax.psum_scatter(
        back, AXES, axis_index_groups=LINES, scatter_dimension=0, tiled=True
    ).astype(f32)
    gains, a0, b0, result = tie(gains, a0, b0, result)
    r3, r1_, s3, s1, gains = tie(*moved, gains + move(gains, X1))
    a, b = tie(*add_blocks((a0, r3, r1_), (b0, s3, s1)))
    z1 = grad_normed_in * mixer_gain
    grad_tokens = (
        grad_middle + r1 * z1 - token_float * (r1 * r1 * r1) * jnp.mean(z1 * token_float, axis=-1, keepdims=True)
    ).astype(bf16)
    *moved, gains, g_gelu, g_linear, g_down, grad_tokens = tie(
        *(move(a[i], (X1, X2, X3)[i - 1]) for i in (1, 2, 3)),
        *(move(b[i], (Z1, Z2, Z3)[i - 1]) for i in (1, 2, 3)),
        gains + move(gains, X2),
        *settle_early(early_sum),
        grad_tokens,
    )
    for pairs in (Z1, Z2):
        gains = gains + move(gains, pairs)
    sum_a, sum_b = (a[0], *moved[:3]), (b[0], *moved[3:])
    g_output, g_query, g_key, g_value, g_swish = settle_late(
        sum_a, sum_b, (wide, kwide, kwide, wide, wide)
    )

    return (
        result,
        grad_tokens,
        gains[:width],
        gains[width : 2 * width],
        gains[2 * width :],
        g_query,
        g_key,
        g_value,
        g_swish,
        g_output.T,
        g_gelu,
        g_linear,
        g_down.T,
    )


def solution(mesh):
    weight = P("dp", "tensor")
    turned = P("tensor", "dp")
    rows = P(("dp", "tensor"), None)
    return jax.shard_map(
        shards,
        mesh=mesh,
        in_specs=(
            rows,
            P("dp"),
            P("tensor"),
            P(),
            P(),
            P("tensor"),
            weight,
            weight,
            weight,
            weight,
            turned,
            weight,
            weight,
            turned,
            rows,
        ),
        out_specs=(
            rows,
            rows,
            P(),
            P(),
            P("tensor"),
            weight,
            weight,
            weight,
            weight,
            turned,
            weight,
            weight,
            turned,
        ),
        check_vma=False,
    )
```

```python
import functools

import jax
import jax.numpy as jnp
from jax import lax
from jax.experimental import pallas as pl
from jax.experimental.pallas import tpu as pltpu
from jax.sharding import PartitionSpec as P

norm_eps = 1e-05
group_eps = 1.0
AXES = ("dp", "tensor")
f32 = jnp.float32
bf16 = jnp.bfloat16
NN = (((1,), (0,)), ((), ()))
NT = (((1,), (1,)), ((), ()))
TN = (((0,), (0,)), ((), ()))
MB = 1 << 20
VMEM = pl.BlockSpec(memory_space=pltpu.VMEM)
ANY = pl.BlockSpec(memory_space=pl.ANY)


def device_index(x, z, y, c):
    return ((x * 4 + z) * 2 + y // 2) * 4 + (y % 2) * 2 + c


def xor_pairs(dx=0, dz=0, dy=0, dc=0):
    return [
        (device_index(x, z, y, c), device_index(x ^ dx, z ^ dz, y ^ dy, c ^ dc))
        for x in range(4)
        for z in range(4)
        for y in range(4)
        for c in range(2)
    ]


X1, X2, X3 = (xor_pairs(dx=d) for d in (1, 2, 3))
Z1, Z2, Z3 = (xor_pairs(dz=d) for d in (1, 2, 3))
Y1, Y2, Y3 = (xor_pairs(dy=d) for d in (1, 2, 3))
C1 = xor_pairs(dc=1)
LINES = [
    [device_index(x, z, y, c) for y in range(4) for c in range(2)]
    for x in range(4)
    for z in range(4)
]
LINE_ORDER = ((0, 0), (1, 0), (0, 1), (1, 1), (2, 0), (3, 0), (2, 1), (3, 1))
PLANES = [
    [device_index(x, z, y, c) for x in range(4) for z in range(4)]
    for y in range(4)
    for c in range(2)
]


def move(value, pairs):
    return lax.ppermute(value, AXES, pairs)


def tie(*values):
    return lax.optimization_barrier(values)


def dot(left, right, dims=NN):
    return lax.dot_general(left, right, dims, preferred_element_type=f32)


def params(mb):
    return pltpu.CompilerParams(vmem_limit_bytes=mb * MB)


def cost(flops, moved):
    return pl.CostEstimate(flops=flops, bytes_accessed=moved, transcendentals=0)


def up128(n):
    return n + (-n % 128)


def stacked(*parts):
    return jnp.concatenate(parts, axis=0)


def split_kernel(*refs):
    ins, (keep_ref, send_ref, pack_ref), held, sems = refs[:8], refs[8:11], refs[11:19], refs[19]
    copies = [pltpu.make_async_copy(i, h, sems.at[n]) for n, (i, h) in enumerate(zip(ins, held))]
    for copy in copies:
        copy.start()
    low = lax.axis_index("dp") % 2 == 0
    place = 0
    for n, ref in enumerate(held[:5]):
        copies[n].wait()
        half = ref.shape[1] // 2
        left, right = ref[:, :half], ref[:, half:]
        keep_ref[:, place : place + half] = jnp.where(low, left, right)
        send_ref[:, place : place + half] = jnp.where(low, right, left)
        place += up128(half)
    place = 0
    for n, ref in enumerate(held[5:]):
        copies[5 + n].wait()
        pack_ref[:, place : place + ref.shape[1]] = ref[...]
        place += up128(ref.shape[1])


def split_weights(mixer, feed):
    size = sum(up128(w.shape[1] // 2) for w in mixer)
    pack = sum(up128(w.shape[1]) for w in feed)
    return pl.pallas_call(
        split_kernel,
        out_shape=(
            jax.ShapeDtypeStruct((64, size), bf16),
            jax.ShapeDtypeStruct((64, size), bf16),
            jax.ShapeDtypeStruct((64, pack), bf16),
        ),
        in_specs=[ANY] * 8,
        scratch_shapes=[pltpu.VMEM(w.shape, bf16) for w in (*mixer, *feed)]
        + [pltpu.SemaphoreType.DMA((8,))],
        compiler_params=params(58),
    )(*mixer, *feed)


def join_kernel(groups, keep_ref, got_ref, *out_refs):
    low = lax.axis_index("dp") % 2 == 0
    place = 0
    for sizes, out_ref in zip(groups, out_refs):
        row = 0
        for size in sizes:
            wide = up128(size)
            keep, got = keep_ref[:, place : place + wide], got_ref[:, place : place + wide]
            both = stacked(jnp.where(low, keep, got), jnp.where(low, got, keep))
            out_ref[row : row + size, :] = both.T[:size]
            place += wide
            row += size


def join_weights(keep, got, *groups):
    out = pl.pallas_call(
        functools.partial(join_kernel, groups),
        out_shape=tuple(jax.ShapeDtypeStruct((sum(sizes), 128), bf16) for sizes in groups),
        compiler_params=params(16),
    )(keep, got)
    return out


def pick_kernel(starts, *refs):
    count = len(starts)
    ins, outs, sems = refs[:count], refs[count : 2 * count], refs[2 * count]
    copies = [
        pltpu.make_async_copy(i.at[pl.ds(start, o.shape[0])], o, sems.at[n])
        for n, (i, o, start) in enumerate(zip(ins, outs, starts))
    ]
    for copy in copies:
        copy.start()
    for copy in copies:
        copy.wait()


def pick(values, starts, sizes):
    return pl.pallas_call(
        functools.partial(pick_kernel, starts),
        out_shape=tuple(
            jax.ShapeDtypeStruct((n, *v.shape[1:]), v.dtype) for v, n in zip(values, sizes)
        ),
        in_specs=[ANY] * len(values),
        out_specs=(ANY,) * len(values),
        scratch_shapes=[pltpu.SemaphoreType.DMA((len(values),))],
        compiler_params=params(4),
    )(*values)


def gather_plane(a, b, pack, rows):
    a1, a3, b1, b3, a2, b2 = tie(
        move(a, X1), move(a, X3), move(b, Z1), move(b, Z3), move(a, X2), move(b, Z2)
    )
    sa, sb = tie(jnp.stack([a, a1, a2, a3]), jnp.stack([b, b1, b2, b3]))
    sa1, sa3, sb1, sb3, got = tie(
        move(sa, Z1), move(sa, Z3), move(sb, X1), move(sb, X3), move(pack, Y2)
    )
    ap, aq, bp, bq, rows, got = tie(*pick((sa3, sa1, sb3, sb1), (0, 2, 0, 2), (2,) * 4), rows, got)
    sa2p, sa2q, sb2p, sb2q, far = tie(
        move(ap, Z1), move(aq, Z3), move(bp, X1), move(bq, X3), move(rows, Y1)
    )
    return (sa, sa1, sa2p, sa2q, sa3, sb, sb1, sb2p, sb2q, sb3), got, stacked(rows, far)


def add_low(*terms):
    total = terms[0].astype(f32)
    for term in terms[1:]:
        total = total + term.astype(f32)
    return total.astype(bf16)


def fold_kernel(*refs):
    olds, more, outs = refs[:4], refs[4:8], refs[8:12]
    held, sems = refs[12:20], refs[20]
    loads, stores = [], []
    for n in range(4):
        start = 2 * (n % 2)
        loads.append(pltpu.make_async_copy(olds[n].at[pl.ds(start, 2)], held[n], sems.at[n, 0]))
        loads.append(pltpu.make_async_copy(more[n], held[4 + n], sems.at[n, 1]))
        stores.append(pltpu.make_async_copy(held[n], outs[n].at[pl.ds(start, 2)], sems.at[n, 2]))
    for copy in loads:
        copy.start()
    for n in range(4):
        loads[2 * n].wait()
        loads[2 * n + 1].wait()
        held[n][...] = (held[n][...].astype(f32) + held[4 + n][...].astype(f32)).astype(bf16)
        stores[n].start()
    for copy in stores:
        copy.wait()


def fold(a3, a1, b3, b1, ap, aq, bp, bq):
    values, more = (a3, a1, b3, b1), (ap, aq, bp, bq)
    return pl.pallas_call(
        fold_kernel,
        out_shape=tuple(jax.ShapeDtypeStruct(v.shape, v.dtype) for v in values),
        in_specs=[ANY] * 8,
        out_specs=(ANY,) * 4,
        scratch_shapes=[pltpu.VMEM(v.shape, bf16) for v in more * 2] + [pltpu.SemaphoreType.DMA((4, 3))],
        input_output_aliases={i: i for i in range(4)},
        compiler_params=params(58),
    )(*values, *more)


def add_kernel(*refs):
    ins, outs = refs[:6], refs[6:]
    for j in range(4):

        @pl.when(pl.program_id(0) == j)
        def _():
            for n in range(2):
                total = sum(ref[0].astype(f32) for ref in ins[3 * n : 3 * n + 3])
                outs[4 * n + j][...] = total.astype(bf16)


def add_blocks(a, b):
    blocks = [pl.BlockSpec((1, *v.shape[1:]), lambda i: (i, 0, 0)) for v in (*a, *b)]
    outs = [v.shape[1:] for v in (a[0],) * 4 + (b[0],) * 4]
    out = pl.pallas_call(
        add_kernel,
        grid=(4,),
        out_shape=tuple(jax.ShapeDtypeStruct(shape, bf16) for shape in outs),
        in_specs=blocks,
        out_specs=tuple(pl.BlockSpec(shape, lambda i: (0, 0)) for shape in outs),
        compiler_params=params(58),
    )(*a, *b)
    return out[:4], out[4:]


def feed_kernel(
    w_ref, x0_ref, x1_ref, x2_ref, x3_ref, g0_ref, g1_ref, hidden_ref, grads_ref, keep_ref, send_ref,
    held_ref, x_ref, grad_ref, sems,
):
    wide = hidden_ref.shape[0]
    part = x0_ref.shape[0]
    half = 2 * part
    given = [
        pltpu.make_async_copy(ref, x_ref.at[pl.ds(i * part, part), :], sems.at[48 + i])
        for i, ref in enumerate((x0_ref, x1_ref, x2_ref, x3_ref))
    ]
    weights = [
        [
            pltpu.make_async_copy(
                w_ref.at[pl.ds((3 * j + i) * wide, wide), :],
                held_ref.at[pl.ds(i * wide, wide), pl.ds(128 * j, 128)],
                sems.at[16 * i + j],
            )
            for j in range(16)
        ]
        for i in range(3)
    ]
    grads = [
        pltpu.make_async_copy(g0_ref, grad_ref.at[pl.ds(0, half), :], sems.at[52]),
        pltpu.make_async_copy(g1_ref, grad_ref.at[pl.ds(half, half), :], sems.at[53]),
    ]
    for copy in given + weights[0] + weights[1] + grads + weights[2]:
        copy.start()
    for copy in given + weights[0]:
        copy.wait()
    up, down, last = (slice(n * wide, (n + 1) * wide) for n in range(3))
    gelu_in = dot(held_ref[up, :], x_ref[...], NT)
    for copy in weights[1]:
        copy.wait()
    linear_in = dot(held_ref[down, :], x_ref[...], NT)
    for copy in grads + weights[2]:
        copy.wait()
    back = dot(held_ref[last, :], grad_ref[...], NT)
    cdf = 0.5 * (1.0 + lax.erf(gelu_in * (0.5**0.5)))
    gelu = gelu_in * cdf
    slope = cdf + gelu_in * jnp.exp(-0.5 * gelu_in * gelu_in) * 0.3989422804014327
    hidden_ref[...] = (gelu * linear_in).astype(bf16)
    grads_ref[up, :] = (back * linear_in * slope).astype(bf16)
    grads_ref[down, :] = (back * gelu).astype(bf16)
    for rows, out_ref in ((slice(half, 2 * half), send_ref), (slice(0, half), keep_ref)):
        out_ref[...] = dot(grads_ref[:, rows], held_ref[: 2 * wide, :], TN).astype(out_ref.dtype)


def feed_forward_back(w, x, g0, g1):
    half, width = g0.shape
    wide = w.shape[0] // 48
    return pl.pallas_call(
        feed_kernel,
        out_shape=(
            jax.ShapeDtypeStruct((wide, 2 * half), bf16),
            jax.ShapeDtypeStruct((2 * wide, 2 * half), bf16),
            jax.ShapeDtypeStruct((half, width), f32),
            jax.ShapeDtypeStruct((half, width), bf16),
        ),
        in_specs=[ANY] * 7,
        scratch_shapes=[
            pltpu.VMEM((3 * wide, width), bf16),
            pltpu.VMEM((2 * half, width), bf16),
            pltpu.VMEM((2 * half, width), bf16),
            pltpu.SemaphoreType.DMA((54,)),
        ],
        cost_estimate=cost(20 * half * wide * width, 10 * wide * width),
        compiler_params=params(58),
    )(w, *x, g0, g1)


def early_kernel(
    hidden_ref, grads_ref, x0_ref, x1_ref, x2_ref, x3_ref, g0_ref, g1_ref, w_ref,
    out_ref, keep_ref, send_ref, turn_ref,
):
    wide = hidden_ref.shape[0]
    half = g0_ref.shape[0]

    @pl.when(pl.program_id(0) == 0)
    def _():
        turn_ref[...] = hidden_ref[...].T

    up = dot(grads_ref[...], stacked(x0_ref[...], x1_ref[...], x2_ref[...], x3_ref[...])).astype(bf16)
    down = dot(hidden_ref[...], stacked(g0_ref[...], g1_ref[...])).astype(bf16)
    for i in range(4):
        lanes = slice(128 * i, 128 * i + 128)
        out_ref[i, : 2 * wide, :] = up[:, lanes]
        out_ref[i, 2 * wide :, :] = down[:, lanes]
    w = jnp.concatenate([w_ref[i] for i in range(4)], axis=1)
    keep_ref[...] = dot(turn_ref[:half, :], w).astype(bf16)
    send_ref[...] = dot(turn_ref[half:, :], w).astype(bf16)


def early_gradients(hidden, grads, x, g0, g1, w):
    wide, rows = hidden.shape
    half, width = g0.shape
    block = pl.BlockSpec((half, 512), lambda i: (0, i))
    return pl.pallas_call(
        early_kernel,
        grid=(4,),
        out_shape=(
            jax.ShapeDtypeStruct((16, 3 * wide, 128), bf16),
            jax.ShapeDtypeStruct((half, width), bf16),
            jax.ShapeDtypeStruct((half, width), bf16),
        ),
        in_specs=[
            pl.BlockSpec((wide, rows), lambda i: (0, 0)),
            pl.BlockSpec((2 * wide, rows), lambda i: (0, 0)),
        ]
        + [pl.BlockSpec((half // 2, 512), lambda i: (0, i))] * 4
        + [block, block, pl.BlockSpec((4, wide, 128), lambda i: (i, 2, 0))],
        out_specs=(pl.BlockSpec((4, 3 * wide, 128), lambda i: (i, 0, 0)), block, block),
        scratch_shapes=[pltpu.VMEM((rows, wide), bf16)],
        cost_estimate=cost(14 * half * wide * width, 10 * wide * width),
        compiler_params=params(58),
    )(hidden, grads, *x, g0, g1, w.reshape(16, 3 * wide, 128))


def parts_kernel(steps, g_in, o_in, x_in, m_in, *refs):
    outs, (g_ref, o_ref, x_ref, m_ref, sems) = refs[:-5], refs[-5:]
    plane = lax.axis_index("dp") // 2
    wide = o_ref.shape[0]
    keys = g_ref.shape[0] - 2 * wide

    def lanes(dx, dz):
        return pl.ds(pl.multiple_of(jnp.bitwise_xor(4 * dx + dz, plane) * 128, 128), 128)

    fixed = [
        pltpu.make_async_copy(g_in.at[pl.ds(0, keys)], g_ref.at[pl.ds(0, keys)], sems.at[0]),
        pltpu.make_async_copy(g_in.at[pl.ds(keys, 2 * wide)], g_ref.at[pl.ds(keys, 2 * wide)], sems.at[1]),
        pltpu.make_async_copy(o_in, o_ref, sems.at[2]),
    ]
    waits = []
    for n, d in enumerate(steps):
        base = 3 + 12 * n
        copies = [[], [], []]
        for i in range(4):
            here = pl.ds(128 * i, 128)
            for k, at in enumerate((lanes(i, d), lanes(d, i))):
                copies[k].append(
                    pltpu.make_async_copy(
                        x_in.at[:, at], x_ref.at[2 * n + k, :, here], sems.at[base + 4 * k + i]
                    )
                )
            copies[2].append(
                pltpu.make_async_copy(
                    m_in.at[:, lanes(i, d)], m_ref.at[n, :, here], sems.at[base + 8 + i]
                )
            )
        if n == 0:
            for k in range(3):
                copies[k].append(fixed[k])
        waits.append(copies)
    for copies in waits:
        for part in copies:
            for copy in part:
                copy.start()

    per = len(outs) // len(steps) // 2

    def store(value, refs, rows):
        value = value.astype(bf16)
        for i in range(4):
            refs[i * per // 4][i % (4 // per), rows, :] = value[:, 128 * i : 128 * i + 128]

    for n in range(len(steps)):
        a_refs = outs[2 * per * n : 2 * per * n + per]
        b_refs = outs[2 * per * n + per : 2 * per * (n + 1)]
        for copy in waits[n][0]:
            copy.wait()
        store(dot(g_ref[:keys, :], x_ref[2 * n]), a_refs, slice(wide, wide + keys))
        for copy in waits[n][1]:
            copy.wait()
        store(dot(g_ref[keys:, :], x_ref[2 * n + 1]), b_refs, slice(0, 2 * wide))
        for copy in waits[n][2]:
            copy.wait()
        store(dot(o_ref[...], m_ref[n]), a_refs, slice(0, wide))


def gradient_parts(steps, per, g, o, x, m):
    wide, rows = o.shape
    rb = 2 * wide
    ra = g.shape[0] - rb + wide
    shapes = ([(4 // per, ra, 128)] * per + [(4 // per, rb, 128)] * per) * len(steps)
    return pl.pallas_call(
        functools.partial(parts_kernel, steps),
        grid=(1,),
        out_shape=tuple(jax.ShapeDtypeStruct(shape, bf16) for shape in shapes),
        in_specs=[ANY] * 4,
        out_specs=tuple(pl.BlockSpec(shape, lambda i: (0, 0, 0)) for shape in shapes),
        scratch_shapes=[
            pltpu.VMEM(g.shape, bf16),
            pltpu.VMEM(o.shape, bf16),
            pltpu.VMEM((2 * len(steps), rows, 512), bf16),
            pltpu.VMEM((len(steps), rows, 512), bf16),
            pltpu.SemaphoreType.DMA((3 + 12 * len(steps),)),
        ],
        cost_estimate=cost(rows * 512 * (ra + rb) * 2 * len(steps), 6 * rows * 2048),
        compiler_params=params(58),
    )(g, o, x, m)


def early_out_kernel(sum_ref, keep_ref, send_ref):
    low = lax.axis_index("dp") % 2 == 0
    wide = sum_ref.shape[0] // 3
    for i in range(3):
        flat = sum_ref[i * wide : (i + 1) * wide, :].T
        place = slice(i * up128(wide), i * up128(wide) + wide)
        keep_ref[:, place] = jnp.where(low, flat[:64], flat[64:])
        send_ref[:, place] = jnp.where(low, flat[64:], flat[:64])


def early_end_kernel(keep_ref, got_ref, *out_refs):
    wide = out_refs[0].shape[1]
    for i, out_ref in enumerate(out_refs):
        place = slice(i * up128(wide), i * up128(wide) + wide)
        out_ref[...] = keep_ref[:, place].astype(f32) + got_ref[:, place].astype(f32)


def settle_early(summed):
    wide = summed.shape[0] // 3
    flat = jax.ShapeDtypeStruct((64, 3 * up128(wide)), bf16)
    keep, send = pl.pallas_call(
        early_out_kernel, out_shape=(flat, flat), compiler_params=params(16)
    )(summed)
    return pl.pallas_call(
        early_end_kernel,
        out_shape=(jax.ShapeDtypeStruct((64, wide), f32),) * 3,
        compiler_params=params(16),
    )(keep, move(send, Y2))


def late_out_kernel(sizes, *refs):
    a_refs, b_refs, (keep_ref, send_ref) = refs[:4], refs[4:8], refs[8:]
    low = lax.axis_index("dp") % 2 == 0
    place, row, parts = 0, 0, a_refs
    for size in sizes:
        if row == parts[0].shape[0]:
            row, parts = 0, b_refs
        total = sum(ref[row : row + size, :].astype(f32) for ref in parts)
        flat = total.astype(bf16).T
        keep_ref[:, place : place + size] = jnp.where(low, flat[:64], flat[64:])
        send_ref[:, place : place + size] = jnp.where(low, flat[64:], flat[:64])
        row += size
        place += up128(size)


def late_end_kernel(keep_ref, got_ref, *out_refs):
    low = lax.axis_index("dp") % 2 == 0
    place = 0
    for out_ref in out_refs:
        size = out_ref.shape[1] // 2
        keep = keep_ref[:, place : place + size].astype(f32)
        got = got_ref[:, place : place + size].astype(f32)
        out_ref[:, :size] = jnp.where(low, keep, got)
        out_ref[:, size:] = jnp.where(low, got, keep)
        place += up128(size)


def settle_late(a, b, sizes):
    flat = jax.ShapeDtypeStruct((64, sum(up128(n) for n in sizes)), bf16)
    keep, send = pl.pallas_call(
        functools.partial(late_out_kernel, sizes), out_shape=(flat, flat), compiler_params=params(16)
    )(*a, *b)
    return pl.pallas_call(
        late_end_kernel,
        out_shape=tuple(jax.ShapeDtypeStruct((64, 2 * n), f32) for n in sizes),
        compiler_params=params(16),
    )(keep, move(send, Y2))


def line_place(block):
    dp, tensor = lax.axis_index("dp"), lax.axis_index("tensor")
    y, c = dp % 2 * 2 + tensor // 2, tensor % 2
    dy, dc = LINE_ORDER[block]
    return jnp.bitwise_xor(y, dy) * 2 + jnp.bitwise_xor(c, dc)


def back_kernel(g_ref, w_ref, x_ref, out_ref, gain_ref, held_ref, sems):
    rows = g_ref.shape[1] // 4
    step = pl.program_id(0)
    total = dot(g_ref[...], w_ref[w_ref.shape[0] - g_ref.shape[0] :, :], TN)
    held_ref[...] = total.astype(bf16)
    copies = []
    for j in range(4):
        where = jnp.where(step == 0, line_place(j), line_place(j + 4))
        copies.append(
            pltpu.make_async_copy(
                held_ref.at[pl.ds(j * rows, rows), :],
                out_ref.at[pl.ds(pl.multiple_of(where * rows, rows), rows), :],
                sems.at[j],
            )
        )
    for copy in copies:
        copy.start()
    gain = jnp.sum(total * x_ref[...].astype(f32), axis=0, keepdims=True)

    @pl.when(step == 0)
    def _():
        gain_ref[...] = gain

    @pl.when(step > 0)
    def _():
        gain_ref[...] += gain

    for copy in copies:
        copy.wait()


def input_gradients(g, w, x):
    size, total = g.shape
    width = w.shape[1]
    half = total // 2
    return pl.pallas_call(
        back_kernel,
        grid=(2,),
        out_shape=(
            jax.ShapeDtypeStruct((total, width), bf16),
            jax.ShapeDtypeStruct((1, width), f32),
        ),
        in_specs=[
            pl.BlockSpec((size, half), lambda i: (0, i)),
            pl.BlockSpec(w.shape, lambda i: (0, 0)),
            pl.BlockSpec((half, width), lambda i: (i, 0)),
        ],
        out_specs=(ANY, pl.BlockSpec((1, width), lambda i: (0, 0))),
        scratch_shapes=[pltpu.VMEM((half, width), bf16), pltpu.SemaphoreType.DMA((4,))],
        cost_estimate=cost(2 * size * total * width, 10 * total * width),
        compiler_params=params(58),
    )(g, w, x)


def gather_line_first(own, *beside):
    r1, r3, core, *beside = tie(move(own, Y1), move(own, Y3), move(own, C1), *beside)
    half = own.shape[0] // 2
    left = move(r3[:half], Y1), move(r1[half:], Y3), r3, move(r3, C1)
    return (own, r1, core, move(r1, C1)), left, beside


def gather_line_last(r2p, r2q, r3, core):
    r2 = stacked(r2p, r2q)
    return r2, r3, move(r2, C1), core


def scatter_line(keep_m, send_m, keep_o, send_o):
    rows = keep_m.shape[0] // 2
    half = rows // 2
    o = keep_o.astype(f32) + move(send_o, C1).astype(f32)
    s2 = o[:rows].astype(bf16)
    t3, t1 = tie(move(s2[:half], Y1), move(s2[half:], Y3))
    m = keep_m.astype(f32) + move(send_m, C1).astype(f32)
    s3 = stacked(o[rows : rows + half] + t3.astype(f32), o[rows + half :]).astype(bf16)
    s1 = stacked(m[rows : rows + half], m[rows + half :] + t1.astype(f32)).astype(bf16)
    u3, u1 = tie(move(s3, Y3), move(s1, Y1))
    return m[:rows] + u3.astype(f32) + u1.astype(f32)


def gather_pair(own):
    far, core = tie(move(own, Y1), move(own, C1))
    return own, far, core, move(far, C1)


def scatter_pair(keep, send, *beside):
    rows = keep.shape[0] // 2
    m = keep + move(send, C1).astype(f32)
    u1, *beside = tie(move(m[rows:].astype(bf16), Y1), *beside)
    return (m[:rows] + u1.astype(f32), *beside)


def mixer_kernel(*refs):
    blocks, (line_ref, decay_ref, gain_ref) = refs[:10], refs[10:13]
    w_out, x_out, q_ref, k_ref, v_ref, gate_ref, retained_ref, mixed_ref = refs[13:21]
    parts, (w_ref, x_ref, sems) = refs[21:25], refs[25:]
    va, vb = blocks[:5], blocks[5:]
    kwide, wide = q_ref.shape[1], v_ref.shape[1]
    rows, half = q_ref.shape[0], parts[0].shape[0]
    plane = lax.axis_index("dp") // 2
    ra, rb = va[0].shape[1], vb[0].shape[1]
    keys = 2 * kwide
    step = pl.program_id(0)
    copies = []
    for dx in range(4):
        for dz in range(4):
            j = 4 * dx + dz
            lanes = pl.ds(pl.multiple_of(jnp.bitwise_xor(j, plane) * 128, 128), 128)
            for n, (part, first, then, row, size) in enumerate(((va, dz, dx, 0, ra), (vb, dx, dz, ra, rb))):
                if first == 2:
                    source = part[2 + then // 2].at[then % 2]
                else:
                    source = part[(0, 1, None, 4)[first]].at[then]
                copies.append(
                    pltpu.make_async_copy(
                        source, w_ref.at[pl.ds(row, size), lanes], sems.at[2 * j + n]
                    )
                )
    size = rows // 4
    given = [
        pltpu.make_async_copy(
            line_ref.at[pl.ds(pl.multiple_of(line_place(j) * size, size), size), :],
            x_ref.at[pl.ds(j * size, size), :],
            sems.at[32 + j],
        )
        for j in range(8)
    ]
    w_back = pltpu.make_async_copy(w_ref, w_out, sems.at[40])
    x_back = pltpu.make_async_copy(x_ref, x_out, sems.at[41])

    @pl.when(step == 0)
    def _():
        for copy in given[:4] + copies + given[4:]:
            copy.start()
        for copy in given[:4] + copies:
            copy.wait()
        w_back.start()

    @pl.when(step == 1)
    def _():
        for copy in given[4:]:
            copy.wait()
        x_back.start()

    x = x_ref[pl.ds(pl.multiple_of(step * rows, rows), rows), :]
    both = dot(x, w_ref[wide : keys + 2 * wide, :], NT).astype(bf16)
    q, k, v = both[:, :kwide], both[:, kwide:keys], both[:, keys:]
    gate = dot(x, w_ref[keys + 2 * wide :, :], NT)
    q_ref[...], k_ref[...], v_ref[...], gate_ref[...] = q, k, v, gate
    weights = (dot(q, k, NT) * decay_ref[...]).astype(bf16)
    retained = dot(weights, v)
    retained_ref[...] = retained
    center = retained - jnp.mean(retained, axis=-1, keepdims=True)
    spread = jnp.mean(center * center, axis=-1, keepdims=True)
    normed = center * lax.rsqrt(spread + group_eps)
    mixed = (gate * jax.nn.sigmoid(gate) * normed * gain_ref[...]).astype(bf16)
    mixed_ref[...] = mixed.T
    wo = w_ref[:wide, :]
    send, keep = dot(mixed[half:], wo).astype(bf16), dot(mixed[:half], wo).astype(bf16)

    @pl.when(step == 0)
    def _():
        parts[0][...], parts[1][...] = keep, send

    @pl.when(step == 1)
    def _():
        parts[2][...], parts[3][...] = keep, send
        w_back.wait()
        x_back.wait()


def mixer_forward(blocks, line, decay, gain, kwide):
    total, width = line.shape
    rows = decay.shape[0]
    wide = gain.shape[1]
    size = 2 * kwide + 3 * wide
    slim = pl.BlockSpec((rows, kwide), lambda i: (i, 0))
    whole = pl.BlockSpec((rows, wide), lambda i: (i, 0))
    part = pl.BlockSpec((rows // 2, width), lambda i: (0, 0))
    return pl.pallas_call(
        mixer_kernel,
        grid=(2,),
        out_shape=(
            jax.ShapeDtypeStruct((size, width), bf16),
            jax.ShapeDtypeStruct((total, width), bf16),
            jax.ShapeDtypeStruct((total, kwide), bf16),
            jax.ShapeDtypeStruct((total, kwide), bf16),
            jax.ShapeDtypeStruct((total, wide), bf16),
            jax.ShapeDtypeStruct((total, wide), f32),
            jax.ShapeDtypeStruct((total, wide), f32),
            jax.ShapeDtypeStruct((wide, total), bf16),
        )
        + (jax.ShapeDtypeStruct((rows // 2, width), bf16),) * 4,
        in_specs=[ANY] * 11
        + [
            pl.BlockSpec((rows, rows), lambda i: (0, 0)),
            pl.BlockSpec((1, wide), lambda i: (0, 0)),
        ],
        out_specs=(
            ANY,
            ANY,
            slim,
            slim,
            whole,
            whole,
            whole,
            pl.BlockSpec((wide, rows), lambda i: (0, i)),
            part,
            part,
            part,
            part,
        ),
        scratch_shapes=[
            pltpu.VMEM((size, width), bf16),
            pltpu.VMEM((total, width), bf16),
            pltpu.SemaphoreType.DMA((42,)),
        ],
        cost_estimate=cost(2 * size * total * width, 16 * total * width),
        compiler_params=params(58),
    )(*blocks, line, decay, gain)


def mixer_back_kernel(
    group, g0_ref, g1_ref, g2_ref, g3_ref, w_ref, q_ref, k_ref, v_ref, gate_ref, decay_ref, gain_ref,
    retained_ref, *refs,
):
    out_ref, gain_out_ref, all_ref, grad_ref, wo_ref, sems = refs[-6:]
    kwide, wide = q_ref.shape[1], v_ref.shape[1]
    keys = 2 * kwide
    part = g0_ref.shape[0]
    rows = 4 * part
    copies = [pltpu.make_async_copy(w_ref.at[pl.ds(0, wide), :], wo_ref, sems.at[4])] + [
        pltpu.make_async_copy(ref, grad_ref.at[pl.ds(i * part, part), :], sems.at[i])
        for i, ref in enumerate((g0_ref, g1_ref, g2_ref, g3_ref))
    ]
    back_copy = pltpu.make_async_copy(grad_ref, all_ref.at[pl.ds(group * rows, rows), :], sems.at[5])
    for copy in copies:
        copy.start()
    q, k, v, decay = q_ref[...], k_ref[...], v_ref[...], decay_ref[...]
    weights = (dot(q, k, NT) * decay).astype(bf16)
    gain = gain_ref[...]
    retained = retained_ref[...]
    center = retained - jnp.mean(retained, axis=-1, keepdims=True)
    rstd = lax.rsqrt(jnp.mean(center * center, axis=-1, keepdims=True) + group_eps)
    normed = center * rstd
    gate = gate_ref[...]
    sig = jax.nn.sigmoid(gate)
    silu = gate * sig
    for copy in copies:
        copy.wait()
    back_copy.start()
    grad = dot(grad_ref[...], wo_ref[...], NT)
    grad_normed = grad * normed
    out_ref[keys + wide :, :] = (grad_normed * gain * (sig * (1.0 + gate * (1.0 - sig)))).astype(bf16).T
    gain_out_ref[...] = jnp.sum(grad_normed * silu, axis=0, keepdims=True)
    y = grad * silu * gain
    back = rstd * (
        y
        - jnp.mean(y, axis=-1, keepdims=True)
        - normed * jnp.mean(y * normed, axis=-1, keepdims=True)
    )
    back = back.astype(bf16)
    grad_scores = (dot(back, v, NT) * decay).astype(bf16)
    out_ref[keys : keys + wide, :] = dot(back, weights, TN).astype(bf16)
    out_ref[kwide:keys, :] = dot(q, grad_scores, TN).astype(bf16)
    out_ref[:kwide, :] = dot(grad_scores, k).astype(bf16).T
    back_copy.wait()


def mixer_backward(group, grads, w, q, k, v, gate, decay, gain, retained, before=()):
    kwide, wide = q.shape[1], v.shape[1]
    rows = decay.shape[0]
    slim = pl.BlockSpec((rows, kwide), lambda i: (group, 0))
    whole = pl.BlockSpec((rows, wide), lambda i: (group, 0))
    line = pl.BlockSpec((1, wide), lambda i: (0, 0))
    size = 2 * kwide + 2 * wide
    return pl.pallas_call(
        functools.partial(mixer_back_kernel, group),
        grid=(1,),
        out_shape=(
            jax.ShapeDtypeStruct((size, q.shape[0]), bf16),
            jax.ShapeDtypeStruct((1, wide), f32),
            jax.ShapeDtypeStruct((q.shape[0], w.shape[1]), bf16),
        ),
        in_specs=[ANY] * 5
        + [slim, slim, whole, whole, pl.BlockSpec((rows, rows), lambda i: (0, 0)), line, whole]
        + [ANY] * len(before),
        out_specs=(pl.BlockSpec((size, rows), lambda i: (0, group)), line, ANY),
        input_output_aliases={12: 0, 13: 2} if before else {},
        scratch_shapes=[
            pltpu.VMEM((rows, w.shape[1]), bf16),
            pltpu.VMEM((wide, w.shape[1]), bf16),
            pltpu.SemaphoreType.DMA((6,)),
        ],
        cost_estimate=cost(2 * rows * (size + wide) * 1024, 8 * rows * 2048),
        compiler_params=params(58),
    )(*grads, w, q, k, v, gate, decay, gain, retained, *before)


def shards(
    tokens,
    group_length,
    forget_rate,
    mixer_gain,
    feed_gain,
    group_gain,
    w_query,
    w_key,
    w_value,
    w_swish,
    w_output,
    w_gelu,
    w_linear,
    w_down,
    cotangent,
):
    rows, width = tokens.shape
    dp = lax.axis_index("dp")
    tensor = lax.axis_index("tensor")
    is_low = dp % 2 == 0
    feed_wide = w_gelu.shape[1]
    wide = w_value.shape[1] // 2
    kwide = w_query.shape[1] // 2
    group = 4 * rows
    score_scale = kwide ** (-0.5)
    log_keep = jnp.log1p(-jnp.where(is_low, forget_rate[0], forget_rate[1]))
    valid_rows = (tensor * rows + lax.broadcasted_iota(jnp.int32, (rows, 1), 0) < group_length[0]).astype(f32)

    keep, send, pack = split_weights(
        (w_output.T, w_query, w_key, w_value, w_swish), (w_gelu, w_linear, w_down.T)
    )

    token_float = tokens.astype(f32)
    grad_result = cotangent.astype(f32)
    group_own = jnp.where(is_low, group_gain[:wide], group_gain[wide:]).reshape(1, wide)

    r1 = lax.rsqrt(jnp.mean(token_float * token_float, axis=-1, keepdims=True) + norm_eps)
    normed_in = (token_float * r1 * mixer_gain).astype(bf16)
    place = lax.broadcasted_iota(jnp.int32, (group, 1), 0)
    block = place // rows
    order = jnp.where(block == 1, 2, jnp.where(block == 2, 1, block))
    position = jnp.bitwise_xor(tensor, order) * rows + place % rows
    offset = position - position.reshape(1, -1)
    decay = jnp.where(
        offset >= 0, jnp.exp(jnp.maximum(offset, 0).astype(f32) * log_keep) * score_scale, 0.0
    )

    got, normed_in, decay = tie(move(send, Y2), normed_in, decay)
    first_a, first_b = join_weights(keep, got, (wide, kwide, kwide), (wide, wide))
    normed_line = lax.all_gather(normed_in, AXES, axis_index_groups=LINES, axis=0, tiled=True)
    grad_feed_out = (valid_rows * grad_result).astype(bf16)
    first, got, grad_feed = gather_plane(first_a, first_b, pack, grad_feed_out)
    (second,) = join_weights(pack, got, (feed_wide,) * 3)
    second = lax.all_gather(second, AXES, axis_index_groups=PLANES, axis=0, tiled=True)

    w_mixer, normed_group, q, k, v, gate, retained, mixed, *parts = mixer_forward(
        first, normed_line, decay, group_own, kwide
    )
    *parts, grad_feed_other = tie(*parts, move(grad_feed, C1))
    grad_feed = grad_feed, grad_feed_other
    mixer_out = scatter_line(*parts)
    middle = token_float + valid_rows * mixer_out
    r2 = lax.rsqrt(jnp.mean(middle * middle, axis=-1, keepdims=True) + norm_eps)
    normed_mid = (middle * r2 * feed_gain).astype(bf16)
    mid = gather_pair(normed_mid)
    hidden, grads, keep, send = feed_forward_back(second, mid, *grad_feed)
    early, feed_keep, feed_send = early_gradients(
        hidden, grads, mid, *grad_feed, second
    )
    grad_normed_mid, early, feed_keep, feed_send = scatter_pair(keep, send, early, feed_keep, feed_send)
    early_sum = lax.psum_scatter(
        early.reshape(-1, 128), AXES, axis_index_groups=PLANES, scatter_dimension=0, tiled=True
    )

    part_feed_gain = jnp.sum(grad_normed_mid * middle * r2, axis=0)
    z2 = grad_normed_mid * feed_gain
    grad_middle = (
        grad_result + r2 * z2 - middle * (r2 * r2 * r2) * jnp.mean(z2 * middle, axis=-1, keepdims=True)
    )
    grad_mixer_out = (valid_rows * grad_middle).astype(bf16)
    grad_mixer_out, feed_send = tie(grad_mixer_out, feed_send)
    feed_got = move(feed_send, C1)
    grad_mixer_m, left, (feed_keep, feed_send) = gather_line_first(
        grad_mixer_out,
        feed_keep[:rows].astype(f32) + feed_got[:rows].astype(f32),
        add_low(feed_keep[rows:], feed_got[rows:]),
    )
    grads, gain_m, grad_mixer = mixer_backward(
        0, grad_mixer_m, w_mixer, q, k, v, gate, decay, group_own, retained
    )
    left, grads, grad_mixer, feed_send = tie(left, grads, grad_mixer, feed_send)
    grad_mixer_o = gather_line_last(*left)
    grads, gain_o, grad_mixer = mixer_backward(
        1, grad_mixer_o, w_mixer, q, k, v, gate, decay, group_own, retained, (grads, grad_mixer)
    )
    part_group_gain = (gain_m + gain_o).reshape(-1)
    *sent, grads, feed_far = tie(
        *gradient_parts((2,), 2, grads, mixed, normed_group, grad_mixer), grads, move(feed_send, Y1)
    )

    moved = [move(part, pairs) for part, pairs in zip(sent, (Z1, Z3, X1, X3))]
    back, part_mixer_gain = input_gradients(grads, w_mixer, normed_group)
    back, grads = tie(back, grads)
    gains = jnp.concatenate([part_mixer_gain.reshape(-1) / mixer_gain, part_feed_gain])
    *moved, (a1, b1, a3, b3), grads, gains = tie(
        *moved,
        gradient_parts((1, 3), 1, grads, mixed, normed_group, grad_mixer),
        grads,
        gains + move(gains, C1),
    )
    a3, a1, b3, b1, grads, gains = tie(
        *fold(a3, a1, b3, b1, *moved), grads, gains + move(gains, Y1)
    )
    moved = move(a3, Z3), move(a1, Z1), move(b3, X3), move(b1, X1)
    a0, b0 = gradient_parts((0,), 1, grads, mixed, normed_group, grad_mixer)
    result = (middle + valid_rows * (feed_keep + feed_far.astype(f32))).astype(bf16)
    gains = jnp.concatenate([gains, part_group_gain])
    far = move(gains, Y2)
    group_far = far[2 * width :]
    gains = jnp.concatenate(
        [
            gains[: 2 * width] + far[: 2 * width],
            jnp.where(is_low, part_group_gain, group_far),
            jnp.where(is_low, group_far, part_group_gain),
        ]
    )
    back, early_sum, _ = tie(back, early_sum, a0)
    grad_normed_in = lax.psum_scatter(
        back, AXES, axis_index_groups=LINES, scatter_dimension=0, tiled=True
    ).astype(f32)
    r3, r1_, s3, s1, gains, a0, b0 = tie(*moved, gains, a0, b0)
    a, b, gains = tie(*add_blocks((a0, r3, r1_), (b0, s3, s1)), gains + move(gains, X1))
    *moved, gains, g_gelu, g_linear, g_down, result = tie(
        *(move(a[i], (X1, X2, X3)[i - 1]) for i in (1, 2, 3)),
        *(move(b[i], (Z1, Z2, Z3)[i - 1]) for i in (1, 2, 3)),
        gains + move(gains, X2),
        *settle_early(early_sum),
        result,
    )
    for pairs in (Z1, Z2):
        gains = gains + move(gains, pairs)
    z1 = grad_normed_in * mixer_gain
    grad_tokens = (
        grad_middle + r1 * z1 - token_float * (r1 * r1 * r1) * jnp.mean(z1 * token_float, axis=-1, keepdims=True)
    ).astype(bf16)
    sum_a, sum_b = (a[0], *moved[:3]), (b[0], *moved[3:])
    g_output, g_query, g_key, g_value, g_swish = settle_late(
        sum_a, sum_b, (wide, kwide, kwide, wide, wide)
    )

    return (
        result,
        grad_tokens,
        gains[:width],
        gains[width : 2 * width],
        gains[2 * width :],
        g_query,
        g_key,
        g_value,
        g_swish,
        g_output.T,
        g_gelu,
        g_linear,
        g_down.T,
    )


def solution(mesh):
    weight = P("dp", "tensor")
    turned = P("tensor", "dp")
    rows = P(("dp", "tensor"), None)
    return jax.shard_map(
        shards,
        mesh=mesh,
        in_specs=(
            rows,
            P("dp"),
            P("tensor"),
            P(),
            P(),
            P("tensor"),
            weight,
            weight,
            weight,
            weight,
            turned,
            weight,
            weight,
            turned,
            rows,
        ),
        out_specs=(
            rows,
            rows,
            P(),
            P(),
            P("tensor"),
            weight,
            weight,
            weight,
            weight,
            turned,
            weight,
            weight,
            turned,
        ),
        check_vma=False,
    )
```

```python
import functools

import jax
import jax.numpy as jnp
from jax import lax
from jax.experimental import pallas as pl
from jax.experimental.pallas import tpu as pltpu
from jax.sharding import PartitionSpec as P

norm_eps = 1e-05
group_eps = 1.0
AXES = ("dp", "tensor")
f32 = jnp.float32
bf16 = jnp.bfloat16
NN = (((1,), (0,)), ((), ()))
NT = (((1,), (1,)), ((), ()))
TN = (((0,), (0,)), ((), ()))
MB = 1 << 20
VMEM = pl.BlockSpec(memory_space=pltpu.VMEM)
ANY = pl.BlockSpec(memory_space=pl.ANY)


def device_index(x, z, y, c):
    return ((x * 4 + z) * 2 + y // 2) * 4 + (y % 2) * 2 + c


def xor_pairs(dx=0, dz=0, dy=0, dc=0):
    return [
        (device_index(x, z, y, c), device_index(x ^ dx, z ^ dz, y ^ dy, c ^ dc))
        for x in range(4)
        for z in range(4)
        for y in range(4)
        for c in range(2)
    ]


X1, X2, X3 = (xor_pairs(dx=d) for d in (1, 2, 3))
Z1, Z2, Z3 = (xor_pairs(dz=d) for d in (1, 2, 3))
Y1, Y2, Y3 = (xor_pairs(dy=d) for d in (1, 2, 3))
C1 = xor_pairs(dc=1)
LINES = [
    [device_index(x, z, y, c) for y in range(4) for c in range(2)]
    for x in range(4)
    for z in range(4)
]
LINE_ORDER = ((0, 0), (1, 0), (0, 1), (1, 1), (2, 0), (3, 0), (2, 1), (3, 1))
PLANES = [
    [device_index(x, z, y, c) for x in range(4) for z in range(4)]
    for y in range(4)
    for c in range(2)
]


def move(value, pairs):
    return lax.ppermute(value, AXES, pairs)


def tie(*values):
    return lax.optimization_barrier(values)


def dot(left, right, dims=NN):
    return lax.dot_general(left, right, dims, preferred_element_type=f32)


def params(mb):
    return pltpu.CompilerParams(vmem_limit_bytes=mb * MB)


def cost(flops, moved):
    return pl.CostEstimate(flops=flops, bytes_accessed=moved, transcendentals=0)


def up128(n):
    return n + (-n % 128)


def stacked(*parts):
    return jnp.concatenate(parts, axis=0)


def split_kernel(*refs):
    ins, (keep_ref, send_ref, pack_ref), held, sems = refs[:8], refs[8:11], refs[11:19], refs[19]
    copies = [pltpu.make_async_copy(i, h, sems.at[n]) for n, (i, h) in enumerate(zip(ins, held))]
    for copy in copies:
        copy.start()
    low = lax.axis_index("dp") % 2 == 0
    place = 0
    for n, ref in enumerate(held[:5]):
        copies[n].wait()
        half = ref.shape[1] // 2
        left, right = ref[:, :half], ref[:, half:]
        keep_ref[:, place : place + half] = jnp.where(low, left, right)
        send_ref[:, place : place + half] = jnp.where(low, right, left)
        place += up128(half)
    place = 0
    for n, ref in enumerate(held[5:]):
        copies[5 + n].wait()
        pack_ref[:, place : place + ref.shape[1]] = ref[...]
        place += up128(ref.shape[1])


def split_weights(mixer, feed):
    size = sum(up128(w.shape[1] // 2) for w in mixer)
    pack = sum(up128(w.shape[1]) for w in feed)
    return pl.pallas_call(
        split_kernel,
        out_shape=(
            jax.ShapeDtypeStruct((64, size), bf16),
            jax.ShapeDtypeStruct((64, size), bf16),
            jax.ShapeDtypeStruct((64, pack), bf16),
        ),
        in_specs=[ANY] * 8,
        scratch_shapes=[pltpu.VMEM(w.shape, bf16) for w in (*mixer, *feed)]
        + [pltpu.SemaphoreType.DMA((8,))],
        compiler_params=params(58),
    )(*mixer, *feed)


def join_kernel(groups, keep_ref, got_ref, *out_refs):
    low = lax.axis_index("dp") % 2 == 0
    place = 0
    for sizes, out_ref in zip(groups, out_refs):
        row = 0
        for size in sizes:
            wide = up128(size)
            keep, got = keep_ref[:, place : place + wide], got_ref[:, place : place + wide]
            both = stacked(jnp.where(low, keep, got), jnp.where(low, got, keep))
            out_ref[row : row + size, :] = both.T[:size]
            place += wide
            row += size


def join_weights(keep, got, *groups):
    out = pl.pallas_call(
        functools.partial(join_kernel, groups),
        out_shape=tuple(jax.ShapeDtypeStruct((sum(sizes), 128), bf16) for sizes in groups),
        compiler_params=params(16),
    )(keep, got)
    return out


def pick_kernel(starts, *refs):
    count = len(starts)
    ins, outs, sems = refs[:count], refs[count : 2 * count], refs[2 * count]
    copies = [
        pltpu.make_async_copy(i.at[pl.ds(start, o.shape[0])], o, sems.at[n])
        for n, (i, o, start) in enumerate(zip(ins, outs, starts))
    ]
    for copy in copies:
        copy.start()
    for copy in copies:
        copy.wait()


def pick(values, starts, sizes):
    return pl.pallas_call(
        functools.partial(pick_kernel, starts),
        out_shape=tuple(
            jax.ShapeDtypeStruct((n, *v.shape[1:]), v.dtype) for v, n in zip(values, sizes)
        ),
        in_specs=[ANY] * len(values),
        out_specs=(ANY,) * len(values),
        scratch_shapes=[pltpu.SemaphoreType.DMA((len(values),))],
        compiler_params=params(4),
    )(*values)


def gather_plane(a, b, pack, rows):
    a1, a3, b1, b3, a2, b2 = tie(
        move(a, X1), move(a, X3), move(b, Z1), move(b, Z3), move(a, X2), move(b, Z2)
    )
    sa, sb = tie(jnp.stack([a, a1, a2, a3]), jnp.stack([b, b1, b2, b3]))
    sa1, sa3, sb1, sb3, got = tie(
        move(sa, Z1), move(sa, Z3), move(sb, X1), move(sb, X3), move(pack, Y2)
    )
    ap, aq, bp, bq, rows, got = tie(*pick((sa3, sa1, sb3, sb1), (0, 2, 0, 2), (2,) * 4), rows, got)
    sa2p, sa2q, sb2p, sb2q, far = tie(
        move(ap, Z1), move(aq, Z3), move(bp, X1), move(bq, X3), move(rows, Y1)
    )
    return (sa, sa1, sa2p, sa2q, sa3, sb, sb1, sb2p, sb2q, sb3), got, stacked(rows, far)


def add_low(*terms):
    total = terms[0].astype(f32)
    for term in terms[1:]:
        total = total + term.astype(f32)
    return total.astype(bf16)


def fold_kernel(*refs):
    olds, more, outs = refs[:4], refs[4:8], refs[8:12]
    held, sems = refs[12:20], refs[20]
    loads, stores = [], []
    for n in range(4):
        start = 2 * (n % 2)
        loads.append(pltpu.make_async_copy(olds[n].at[pl.ds(start, 2)], held[n], sems.at[n, 0]))
        loads.append(pltpu.make_async_copy(more[n], held[4 + n], sems.at[n, 1]))
        stores.append(pltpu.make_async_copy(held[n], outs[n].at[pl.ds(start, 2)], sems.at[n, 2]))
    for copy in loads:
        copy.start()
    for n in range(4):
        loads[2 * n].wait()
        loads[2 * n + 1].wait()
        held[n][...] = (held[n][...].astype(f32) + held[4 + n][...].astype(f32)).astype(bf16)
        stores[n].start()
    for copy in stores:
        copy.wait()


def fold(a3, a1, b3, b1, ap, aq, bp, bq):
    values, more = (a3, a1, b3, b1), (ap, aq, bp, bq)
    return pl.pallas_call(
        fold_kernel,
        out_shape=tuple(jax.ShapeDtypeStruct(v.shape, v.dtype) for v in values),
        in_specs=[ANY] * 8,
        out_specs=(ANY,) * 4,
        scratch_shapes=[pltpu.VMEM(v.shape, bf16) for v in more * 2] + [pltpu.SemaphoreType.DMA((4, 3))],
        input_output_aliases={i: i for i in range(4)},
        compiler_params=params(50),
    )(*values, *more)


def add_kernel(*refs):
    ins, outs = refs[:6], refs[6:]
    for j in range(4):

        @pl.when(pl.program_id(0) == j)
        def _():
            for n in range(2):
                total = sum(ref[0].astype(f32) for ref in ins[3 * n : 3 * n + 3])
                outs[4 * n + j][...] = total.astype(bf16)


def add_blocks(a, b):
    blocks = [pl.BlockSpec((1, *v.shape[1:]), lambda i: (i, 0, 0)) for v in (*a, *b)]
    outs = [v.shape[1:] for v in (a[0],) * 4 + (b[0],) * 4]
    out = pl.pallas_call(
        add_kernel,
        grid=(4,),
        out_shape=tuple(jax.ShapeDtypeStruct(shape, bf16) for shape in outs),
        in_specs=blocks,
        out_specs=tuple(pl.BlockSpec(shape, lambda i: (0, 0)) for shape in outs),
        compiler_params=params(50),
    )(*a, *b)
    return out[:4], out[4:]


def feed_kernel(
    w_ref, x0_ref, x1_ref, x2_ref, x3_ref, g0_ref, g1_ref, hidden_ref, grads_ref, keep_ref, send_ref,
    held_ref, x_ref, grad_ref, sems,
):
    wide = hidden_ref.shape[0]
    part = x0_ref.shape[0]
    half = 2 * part
    given = [
        pltpu.make_async_copy(ref, x_ref.at[pl.ds(i * part, part), :], sems.at[48 + i])
        for i, ref in enumerate((x0_ref, x1_ref, x2_ref, x3_ref))
    ]
    weights = [
        [
            pltpu.make_async_copy(
                w_ref.at[pl.ds((3 * j + i) * wide, wide), :],
                held_ref.at[pl.ds(i * wide, wide), pl.ds(128 * j, 128)],
                sems.at[16 * i + j],
            )
            for j in range(16)
        ]
        for i in range(3)
    ]
    grads = [
        pltpu.make_async_copy(g0_ref, grad_ref.at[pl.ds(0, half), :], sems.at[52]),
        pltpu.make_async_copy(g1_ref, grad_ref.at[pl.ds(half, half), :], sems.at[53]),
    ]
    for copy in given + weights[0] + weights[1] + grads + weights[2]:
        copy.start()
    for copy in given + weights[0]:
        copy.wait()
    up, down, last = (slice(n * wide, (n + 1) * wide) for n in range(3))
    gelu_in = dot(held_ref[up, :], x_ref[...], NT)
    for copy in weights[1]:
        copy.wait()
    linear_in = dot(held_ref[down, :], x_ref[...], NT)
    for copy in grads + weights[2]:
        copy.wait()
    back = dot(held_ref[last, :], grad_ref[...], NT)
    cdf = 0.5 * (1.0 + lax.erf(gelu_in * (0.5**0.5)))
    gelu = gelu_in * cdf
    slope = cdf + gelu_in * jnp.exp(-0.5 * gelu_in * gelu_in) * 0.3989422804014327
    hidden_ref[...] = (gelu * linear_in).astype(bf16)
    grads_ref[up, :] = (back * linear_in * slope).astype(bf16)
    grads_ref[down, :] = (back * gelu).astype(bf16)
    for rows, out_ref in ((slice(half, 2 * half), send_ref), (slice(0, half), keep_ref)):
        out_ref[...] = dot(grads_ref[:, rows], held_ref[: 2 * wide, :], TN).astype(out_ref.dtype)


def feed_forward_back(w, x, g0, g1):
    half, width = g0.shape
    wide = w.shape[0] // 48
    return pl.pallas_call(
        feed_kernel,
        out_shape=(
            jax.ShapeDtypeStruct((wide, 2 * half), bf16),
            jax.ShapeDtypeStruct((2 * wide, 2 * half), bf16),
            jax.ShapeDtypeStruct((half, width), f32),
            jax.ShapeDtypeStruct((half, width), bf16),
        ),
        in_specs=[ANY] * 7,
        scratch_shapes=[
            pltpu.VMEM((3 * wide, width), bf16),
            pltpu.VMEM((2 * half, width), bf16),
            pltpu.VMEM((2 * half, width), bf16),
            pltpu.SemaphoreType.DMA((54,)),
        ],
        cost_estimate=cost(20 * half * wide * width, 10 * wide * width),
        compiler_params=params(50),
    )(w, *x, g0, g1)


def early_kernel(
    hidden_ref, grads_ref, x0_ref, x1_ref, x2_ref, x3_ref, g0_ref, g1_ref, w_ref,
    out_ref, keep_ref, send_ref, turn_ref,
):
    wide = hidden_ref.shape[0]
    half = g0_ref.shape[0]

    @pl.when(pl.program_id(0) == 0)
    def _():
        turn_ref[...] = hidden_ref[...].T

    up = dot(grads_ref[...], stacked(x0_ref[...], x1_ref[...], x2_ref[...], x3_ref[...])).astype(bf16)
    down = dot(hidden_ref[...], stacked(g0_ref[...], g1_ref[...])).astype(bf16)
    for i in range(4):
        lanes = slice(128 * i, 128 * i + 128)
        out_ref[i, : 2 * wide, :] = up[:, lanes]
        out_ref[i, 2 * wide :, :] = down[:, lanes]
    w = jnp.concatenate([w_ref[i] for i in range(4)], axis=1)
    keep_ref[...] = dot(turn_ref[:half, :], w).astype(bf16)
    send_ref[...] = dot(turn_ref[half:, :], w).astype(bf16)


def early_gradients(hidden, grads, x, g0, g1, w):
    wide, rows = hidden.shape
    half, width = g0.shape
    block = pl.BlockSpec((half, 512), lambda i: (0, i))
    return pl.pallas_call(
        early_kernel,
        grid=(4,),
        out_shape=(
            jax.ShapeDtypeStruct((16, 3 * wide, 128), bf16),
            jax.ShapeDtypeStruct((half, width), bf16),
            jax.ShapeDtypeStruct((half, width), bf16),
        ),
        in_specs=[
            pl.BlockSpec((wide, rows), lambda i: (0, 0)),
            pl.BlockSpec((2 * wide, rows), lambda i: (0, 0)),
        ]
        + [pl.BlockSpec((half // 2, 512), lambda i: (0, i))] * 4
        + [block, block, pl.BlockSpec((4, wide, 128), lambda i: (i, 2, 0))],
        out_specs=(pl.BlockSpec((4, 3 * wide, 128), lambda i: (i, 0, 0)), block, block),
        scratch_shapes=[pltpu.VMEM((rows, wide), bf16)],
        cost_estimate=cost(14 * half * wide * width, 10 * wide * width),
        compiler_params=params(50),
    )(hidden, grads, *x, g0, g1, w.reshape(16, 3 * wide, 128))


def parts_kernel(steps, g_in, o_in, x_in, m_in, *refs):
    outs, (g_ref, o_ref, x_ref, m_ref, sems) = refs[:-5], refs[-5:]
    plane = lax.axis_index("dp") // 2
    wide = o_ref.shape[0]
    keys = g_ref.shape[0] - 2 * wide

    def lanes(dx, dz):
        return pl.ds(pl.multiple_of(jnp.bitwise_xor(4 * dx + dz, plane) * 128, 128), 128)

    fixed = [
        pltpu.make_async_copy(g_in.at[pl.ds(0, keys)], g_ref.at[pl.ds(0, keys)], sems.at[0]),
        pltpu.make_async_copy(g_in.at[pl.ds(keys, 2 * wide)], g_ref.at[pl.ds(keys, 2 * wide)], sems.at[1]),
        pltpu.make_async_copy(o_in, o_ref, sems.at[2]),
    ]
    waits = []
    for n, d in enumerate(steps):
        base = 3 + 12 * n
        copies = [[], [], []]
        for i in range(4):
            here = pl.ds(128 * i, 128)
            for k, at in enumerate((lanes(i, d), lanes(d, i))):
                copies[k].append(
                    pltpu.make_async_copy(
                        x_in.at[:, at], x_ref.at[2 * n + k, :, here], sems.at[base + 4 * k + i]
                    )
                )
            copies[2].append(
                pltpu.make_async_copy(
                    m_in.at[:, lanes(i, d)], m_ref.at[n, :, here], sems.at[base + 8 + i]
                )
            )
        if n == 0:
            for k in range(3):
                copies[k].append(fixed[k])
        waits.append(copies)
    for copies in waits:
        for part in copies:
            for copy in part:
                copy.start()

    per = len(outs) // len(steps) // 2

    def store(value, refs, rows):
        value = value.astype(bf16)
        for i in range(4):
            refs[i * per // 4][i % (4 // per), rows, :] = value[:, 128 * i : 128 * i + 128]

    for n in range(len(steps)):
        a_refs = outs[2 * per * n : 2 * per * n + per]
        b_refs = outs[2 * per * n + per : 2 * per * (n + 1)]
        for copy in waits[n][0]:
            copy.wait()
        store(dot(g_ref[:keys, :], x_ref[2 * n]), a_refs, slice(wide, wide + keys))
        for copy in waits[n][1]:
            copy.wait()
        store(dot(g_ref[keys:, :], x_ref[2 * n + 1]), b_refs, slice(0, 2 * wide))
        for copy in waits[n][2]:
            copy.wait()
        store(dot(o_ref[...], m_ref[n]), a_refs, slice(0, wide))


def gradient_parts(steps, per, g, o, x, m):
    wide, rows = o.shape
    rb = 2 * wide
    ra = g.shape[0] - rb + wide
    shapes = ([(4 // per, ra, 128)] * per + [(4 // per, rb, 128)] * per) * len(steps)
    return pl.pallas_call(
        functools.partial(parts_kernel, steps),
        grid=(1,),
        out_shape=tuple(jax.ShapeDtypeStruct(shape, bf16) for shape in shapes),
        in_specs=[ANY] * 4,
        out_specs=tuple(pl.BlockSpec(shape, lambda i: (0, 0, 0)) for shape in shapes),
        scratch_shapes=[
            pltpu.VMEM(g.shape, bf16),
            pltpu.VMEM(o.shape, bf16),
            pltpu.VMEM((2 * len(steps), rows, 512), bf16),
            pltpu.VMEM((len(steps), rows, 512), bf16),
            pltpu.SemaphoreType.DMA((3 + 12 * len(steps),)),
        ],
        cost_estimate=cost(rows * 512 * (ra + rb) * 2 * len(steps), 6 * rows * 2048),
        compiler_params=params(50),
    )(g, o, x, m)


def early_out_kernel(sum_ref, keep_ref, send_ref):
    low = lax.axis_index("dp") % 2 == 0
    wide = sum_ref.shape[0] // 3
    for i in range(3):
        flat = sum_ref[i * wide : (i + 1) * wide, :].T
        place = slice(i * up128(wide), i * up128(wide) + wide)
        keep_ref[:, place] = jnp.where(low, flat[:64], flat[64:])
        send_ref[:, place] = jnp.where(low, flat[64:], flat[:64])


def early_end_kernel(keep_ref, got_ref, *out_refs):
    wide = out_refs[0].shape[1]
    for i, out_ref in enumerate(out_refs):
        place = slice(i * up128(wide), i * up128(wide) + wide)
        out_ref[...] = keep_ref[:, place].astype(f32) + got_ref[:, place].astype(f32)


def settle_early(summed):
    wide = summed.shape[0] // 3
    flat = jax.ShapeDtypeStruct((64, 3 * up128(wide)), bf16)
    keep, send = pl.pallas_call(
        early_out_kernel, out_shape=(flat, flat), compiler_params=params(16)
    )(summed)
    return pl.pallas_call(
        early_end_kernel,
        out_shape=(jax.ShapeDtypeStruct((64, wide), f32),) * 3,
        compiler_params=params(16),
    )(keep, move(send, Y2))


def late_out_kernel(sizes, *refs):
    a_refs, b_refs, (keep_ref, send_ref) = refs[:4], refs[4:8], refs[8:]
    low = lax.axis_index("dp") % 2 == 0
    place, row, parts = 0, 0, a_refs
    for size in sizes:
        if row == parts[0].shape[0]:
            row, parts = 0, b_refs
        total = sum(ref[row : row + size, :].astype(f32) for ref in parts)
        flat = total.astype(bf16).T
        keep_ref[:, place : place + size] = jnp.where(low, flat[:64], flat[64:])
        send_ref[:, place : place + size] = jnp.where(low, flat[64:], flat[:64])
        row += size
        place += up128(size)


def late_end_kernel(keep_ref, got_ref, *out_refs):
    low = lax.axis_index("dp") % 2 == 0
    place = 0
    for out_ref in out_refs:
        size = out_ref.shape[1] // 2
        keep = keep_ref[:, place : place + size].astype(f32)
        got = got_ref[:, place : place + size].astype(f32)
        out_ref[:, :size] = jnp.where(low, keep, got)
        out_ref[:, size:] = jnp.where(low, got, keep)
        place += up128(size)


def settle_late(a, b, sizes):
    flat = jax.ShapeDtypeStruct((64, sum(up128(n) for n in sizes)), bf16)
    keep, send = pl.pallas_call(
        functools.partial(late_out_kernel, sizes), out_shape=(flat, flat), compiler_params=params(16)
    )(*a, *b)
    return pl.pallas_call(
        late_end_kernel,
        out_shape=tuple(jax.ShapeDtypeStruct((64, 2 * n), f32) for n in sizes),
        compiler_params=params(16),
    )(keep, move(send, Y2))


def line_place(block):
    dp, tensor = lax.axis_index("dp"), lax.axis_index("tensor")
    y, c = dp % 2 * 2 + tensor // 2, tensor % 2
    dy, dc = LINE_ORDER[block]
    return jnp.bitwise_xor(y, dy) * 2 + jnp.bitwise_xor(c, dc)


def back_kernel(g_ref, w_ref, x_ref, out_ref, gain_ref, held_ref, sems):
    rows = g_ref.shape[1] // 4
    step = pl.program_id(0)
    total = dot(g_ref[...], w_ref[w_ref.shape[0] - g_ref.shape[0] :, :], TN)
    held_ref[...] = total.astype(bf16)
    copies = []
    for j in range(4):
        where = jnp.where(step == 0, line_place(j), line_place(j + 4))
        copies.append(
            pltpu.make_async_copy(
                held_ref.at[pl.ds(j * rows, rows), :],
                out_ref.at[pl.ds(pl.multiple_of(where * rows, rows), rows), :],
                sems.at[j],
            )
        )
    for copy in copies:
        copy.start()
    gain = jnp.sum(total * x_ref[...].astype(f32), axis=0, keepdims=True)

    @pl.when(step == 0)
    def _():
        gain_ref[...] = gain

    @pl.when(step > 0)
    def _():
        gain_ref[...] += gain

    for copy in copies:
        copy.wait()


def input_gradients(g, w, x):
    size, total = g.shape
    width = w.shape[1]
    half = total // 2
    return pl.pallas_call(
        back_kernel,
        grid=(2,),
        out_shape=(
            jax.ShapeDtypeStruct((total, width), bf16),
            jax.ShapeDtypeStruct((1, width), f32),
        ),
        in_specs=[
            pl.BlockSpec((size, half), lambda i: (0, i)),
            pl.BlockSpec(w.shape, lambda i: (0, 0)),
            pl.BlockSpec((half, width), lambda i: (i, 0)),
        ],
        out_specs=(ANY, pl.BlockSpec((1, width), lambda i: (0, 0))),
        scratch_shapes=[pltpu.VMEM((half, width), bf16), pltpu.SemaphoreType.DMA((4,))],
        cost_estimate=cost(2 * size * total * width, 10 * total * width),
        compiler_params=params(50),
    )(g, w, x)


def gather_line_first(own, *beside):
    r1, r3, core, *beside = tie(move(own, Y1), move(own, Y3), move(own, C1), *beside)
    half = own.shape[0] // 2
    left = move(r3[:half], Y1), move(r1[half:], Y3), r3, move(r3, C1)
    return (own, r1, core, move(r1, C1)), left, beside


def gather_line_last(r2p, r2q, r3, core):
    r2 = stacked(r2p, r2q)
    return r2, r3, move(r2, C1), core


def scatter_line(keep_m, send_m, keep_o, send_o):
    rows = keep_m.shape[0] // 2
    half = rows // 2
    o = keep_o.astype(f32) + move(send_o, C1).astype(f32)
    s2 = o[:rows].astype(bf16)
    t3, t1 = tie(move(s2[:half], Y1), move(s2[half:], Y3))
    m = keep_m.astype(f32) + move(send_m, C1).astype(f32)
    s3 = stacked(o[rows : rows + half] + t3.astype(f32), o[rows + half :]).astype(bf16)
    s1 = stacked(m[rows : rows + half], m[rows + half :] + t1.astype(f32)).astype(bf16)
    u3, u1 = tie(move(s3, Y3), move(s1, Y1))
    return m[:rows] + u3.astype(f32) + u1.astype(f32)


def gather_pair(own):
    far, core = tie(move(own, Y1), move(own, C1))
    return own, far, core, move(far, C1)


def scatter_pair(keep, send, *beside):
    rows = keep.shape[0] // 2
    m = keep + move(send, C1).astype(f32)
    u1, *beside = tie(move(m[rows:].astype(bf16), Y1), *beside)
    return (m[:rows] + u1.astype(f32), *beside)


def mixer_kernel(*refs):
    blocks, (line_ref, decay_ref, gain_ref) = refs[:10], refs[10:13]
    w_out, x_out, q_ref, k_ref, v_ref, gate_ref, retained_ref, mixed_ref = refs[13:21]
    parts, (w_ref, x_ref, sems) = refs[21:25], refs[25:]
    va, vb = blocks[:5], blocks[5:]
    kwide, wide = q_ref.shape[1], v_ref.shape[1]
    rows, half = q_ref.shape[0], parts[0].shape[0]
    plane = lax.axis_index("dp") // 2
    ra, rb = va[0].shape[1], vb[0].shape[1]
    keys = 2 * kwide
    step = pl.program_id(0)
    copies = []
    for dx in range(4):
        for dz in range(4):
            j = 4 * dx + dz
            lanes = pl.ds(pl.multiple_of(jnp.bitwise_xor(j, plane) * 128, 128), 128)
            for n, (part, first, then, row, size) in enumerate(((va, dz, dx, 0, ra), (vb, dx, dz, ra, rb))):
                if first == 2:
                    source = part[2 + then // 2].at[then % 2]
                else:
                    source = part[(0, 1, None, 4)[first]].at[then]
                copies.append(
                    pltpu.make_async_copy(
                        source, w_ref.at[pl.ds(row, size), lanes], sems.at[2 * j + n]
                    )
                )
    size = rows // 4
    given = [
        pltpu.make_async_copy(
            line_ref.at[pl.ds(pl.multiple_of(line_place(j) * size, size), size), :],
            x_ref.at[pl.ds(j * size, size), :],
            sems.at[32 + j],
        )
        for j in range(8)
    ]
    w_back = pltpu.make_async_copy(w_ref, w_out, sems.at[40])
    x_back = pltpu.make_async_copy(x_ref, x_out, sems.at[41])

    @pl.when(step == 0)
    def _():
        for copy in given[:4] + copies + given[4:]:
            copy.start()
        for copy in given[:4] + copies:
            copy.wait()
        w_back.start()

    @pl.when(step == 1)
    def _():
        for copy in given[4:]:
            copy.wait()
        x_back.start()

    x = x_ref[pl.ds(pl.multiple_of(step * rows, rows), rows), :]
    both = dot(x, w_ref[wide : keys + 2 * wide, :], NT).astype(bf16)
    q, k, v = both[:, :kwide], both[:, kwide:keys], both[:, keys:]
    gate = dot(x, w_ref[keys + 2 * wide :, :], NT)
    q_ref[...], k_ref[...], v_ref[...], gate_ref[...] = q, k, v, gate
    weights = (dot(q, k, NT) * decay_ref[...]).astype(bf16)
    retained = dot(weights, v)
    retained_ref[...] = retained
    center = retained - jnp.mean(retained, axis=-1, keepdims=True)
    spread = jnp.mean(center * center, axis=-1, keepdims=True)
    normed = center * lax.rsqrt(spread + group_eps)
    mixed = (gate * jax.nn.sigmoid(gate) * normed * gain_ref[...]).astype(bf16)
    mixed_ref[...] = mixed.T
    wo = w_ref[:wide, :]
    send, keep = dot(mixed[half:], wo).astype(bf16), dot(mixed[:half], wo).astype(bf16)

    @pl.when(step == 0)
    def _():
        parts[0][...], parts[1][...] = keep, send

    @pl.when(step == 1)
    def _():
        parts[2][...], parts[3][...] = keep, send
        w_back.wait()
        x_back.wait()


def mixer_forward(blocks, line, decay, gain, kwide):
    total, width = line.shape
    rows = decay.shape[0]
    wide = gain.shape[1]
    size = 2 * kwide + 3 * wide
    slim = pl.BlockSpec((rows, kwide), lambda i: (i, 0))
    whole = pl.BlockSpec((rows, wide), lambda i: (i, 0))
    part = pl.BlockSpec((rows // 2, width), lambda i: (0, 0))
    return pl.pallas_call(
        mixer_kernel,
        grid=(2,),
        out_shape=(
            jax.ShapeDtypeStruct((size, width), bf16),
            jax.ShapeDtypeStruct((total, width), bf16),
            jax.ShapeDtypeStruct((total, kwide), bf16),
            jax.ShapeDtypeStruct((total, kwide), bf16),
            jax.ShapeDtypeStruct((total, wide), bf16),
            jax.ShapeDtypeStruct((total, wide), f32),
            jax.ShapeDtypeStruct((total, wide), f32),
            jax.ShapeDtypeStruct((wide, total), bf16),
        )
        + (jax.ShapeDtypeStruct((rows // 2, width), bf16),) * 4,
        in_specs=[ANY] * 11
        + [
            pl.BlockSpec((rows, rows), lambda i: (0, 0)),
            pl.BlockSpec((1, wide), lambda i: (0, 0)),
        ],
        out_specs=(
            ANY,
            ANY,
            slim,
            slim,
            whole,
            whole,
            whole,
            pl.BlockSpec((wide, rows), lambda i: (0, i)),
            part,
            part,
            part,
            part,
        ),
        scratch_shapes=[
            pltpu.VMEM((size, width), bf16),
            pltpu.VMEM((total, width), bf16),
            pltpu.SemaphoreType.DMA((42,)),
        ],
        cost_estimate=cost(2 * size * total * width, 16 * total * width),
        compiler_params=params(50),
    )(*blocks, line, decay, gain)


def mixer_back_kernel(
    group, g0_ref, g1_ref, g2_ref, g3_ref, w_ref, q_ref, k_ref, v_ref, gate_ref, decay_ref, gain_ref,
    retained_ref, *refs,
):
    out_ref, gain_out_ref, all_ref, grad_ref, wo_ref, sems = refs[-6:]
    kwide, wide = q_ref.shape[1], v_ref.shape[1]
    keys = 2 * kwide
    part = g0_ref.shape[0]
    rows = 4 * part
    copies = [pltpu.make_async_copy(w_ref.at[pl.ds(0, wide), :], wo_ref, sems.at[4])] + [
        pltpu.make_async_copy(ref, grad_ref.at[pl.ds(i * part, part), :], sems.at[i])
        for i, ref in enumerate((g0_ref, g1_ref, g2_ref, g3_ref))
    ]
    back_copy = pltpu.make_async_copy(grad_ref, all_ref.at[pl.ds(group * rows, rows), :], sems.at[5])
    for copy in copies:
        copy.start()
    q, k, v, decay = q_ref[...], k_ref[...], v_ref[...], decay_ref[...]
    weights = (dot(q, k, NT) * decay).astype(bf16)
    gain = gain_ref[...]
    retained = retained_ref[...]
    center = retained - jnp.mean(retained, axis=-1, keepdims=True)
    rstd = lax.rsqrt(jnp.mean(center * center, axis=-1, keepdims=True) + group_eps)
    normed = center * rstd
    gate = gate_ref[...]
    sig = jax.nn.sigmoid(gate)
    silu = gate * sig
    for copy in copies:
        copy.wait()
    back_copy.start()
    grad = dot(grad_ref[...], wo_ref[...], NT)
    grad_normed = grad * normed
    out_ref[keys + wide :, :] = (grad_normed * gain * (sig * (1.0 + gate * (1.0 - sig)))).astype(bf16).T
    gain_out_ref[...] = jnp.sum(grad_normed * silu, axis=0, keepdims=True)
    y = grad * silu * gain
    back = rstd * (
        y
        - jnp.mean(y, axis=-1, keepdims=True)
        - normed * jnp.mean(y * normed, axis=-1, keepdims=True)
    )
    back = back.astype(bf16)
    grad_scores = (dot(back, v, NT) * decay).astype(bf16)
    out_ref[keys : keys + wide, :] = dot(back, weights, TN).astype(bf16)
    out_ref[kwide:keys, :] = dot(q, grad_scores, TN).astype(bf16)
    out_ref[:kwide, :] = dot(grad_scores, k).astype(bf16).T
    back_copy.wait()


def mixer_backward(group, grads, w, q, k, v, gate, decay, gain, retained, before=()):
    kwide, wide = q.shape[1], v.shape[1]
    rows = decay.shape[0]
    slim = pl.BlockSpec((rows, kwide), lambda i: (group, 0))
    whole = pl.BlockSpec((rows, wide), lambda i: (group, 0))
    line = pl.BlockSpec((1, wide), lambda i: (0, 0))
    size = 2 * kwide + 2 * wide
    return pl.pallas_call(
        functools.partial(mixer_back_kernel, group),
        grid=(1,),
        out_shape=(
            jax.ShapeDtypeStruct((size, q.shape[0]), bf16),
            jax.ShapeDtypeStruct((1, wide), f32),
            jax.ShapeDtypeStruct((q.shape[0], w.shape[1]), bf16),
        ),
        in_specs=[ANY] * 5
        + [slim, slim, whole, whole, pl.BlockSpec((rows, rows), lambda i: (0, 0)), line, whole]
        + [ANY] * len(before),
        out_specs=(pl.BlockSpec((size, rows), lambda i: (0, group)), line, ANY),
        input_output_aliases={12: 0, 13: 2} if before else {},
        scratch_shapes=[
            pltpu.VMEM((rows, w.shape[1]), bf16),
            pltpu.VMEM((wide, w.shape[1]), bf16),
            pltpu.SemaphoreType.DMA((6,)),
        ],
        cost_estimate=cost(2 * rows * (size + wide) * 1024, 8 * rows * 2048),
        compiler_params=params(50),
    )(*grads, w, q, k, v, gate, decay, gain, retained, *before)


def shards(
    tokens,
    group_length,
    forget_rate,
    mixer_gain,
    feed_gain,
    group_gain,
    w_query,
    w_key,
    w_value,
    w_swish,
    w_output,
    w_gelu,
    w_linear,
    w_down,
    cotangent,
):
    rows, width = tokens.shape
    dp = lax.axis_index("dp")
    tensor = lax.axis_index("tensor")
    is_low = dp % 2 == 0
    feed_wide = w_gelu.shape[1]
    wide = w_value.shape[1] // 2
    kwide = w_query.shape[1] // 2
    group = 4 * rows
    score_scale = kwide ** (-0.5)
    log_keep = jnp.log1p(-jnp.where(is_low, forget_rate[0], forget_rate[1]))
    valid_rows = (tensor * rows + lax.broadcasted_iota(jnp.int32, (rows, 1), 0) < group_length[0]).astype(f32)

    keep, send, pack = split_weights(
        (w_output.T, w_query, w_key, w_value, w_swish), (w_gelu, w_linear, w_down.T)
    )

    token_float = tokens.astype(f32)
    grad_result = cotangent.astype(f32)
    group_own = jnp.where(is_low, group_gain[:wide], group_gain[wide:]).reshape(1, wide)

    r1 = lax.rsqrt(jnp.mean(token_float * token_float, axis=-1, keepdims=True) + norm_eps)
    normed_in = (token_float * r1 * mixer_gain).astype(bf16)
    place = lax.broadcasted_iota(jnp.int32, (group, 1), 0)
    block = place // rows
    order = jnp.where(block == 1, 2, jnp.where(block == 2, 1, block))
    position = jnp.bitwise_xor(tensor, order) * rows + place % rows
    offset = position - position.reshape(1, -1)
    decay = jnp.where(
        offset >= 0, jnp.exp(jnp.maximum(offset, 0).astype(f32) * log_keep) * score_scale, 0.0
    )

    got, normed_in, decay = tie(move(send, Y2), normed_in, decay)
    first_a, first_b = join_weights(keep, got, (wide, kwide, kwide), (wide, wide))
    normed_line = lax.all_gather(normed_in, AXES, axis_index_groups=LINES, axis=0, tiled=True)
    grad_feed_out = (valid_rows * grad_result).astype(bf16)
    first, got, grad_feed = gather_plane(first_a, first_b, pack, grad_feed_out)
    (second,) = join_weights(pack, got, (feed_wide,) * 3)
    second = lax.all_gather(second, AXES, axis_index_groups=PLANES, axis=0, tiled=True)

    w_mixer, normed_group, q, k, v, gate, retained, mixed, *parts = mixer_forward(
        first, normed_line, decay, group_own, kwide
    )
    *parts, grad_feed_other = tie(*parts, move(grad_feed, C1))
    grad_feed = grad_feed, grad_feed_other
    mixer_out = scatter_line(*parts)
    middle = token_float + valid_rows * mixer_out
    r2 = lax.rsqrt(jnp.mean(middle * middle, axis=-1, keepdims=True) + norm_eps)
    normed_mid = (middle * r2 * feed_gain).astype(bf16)
    mid = gather_pair(normed_mid)
    hidden, grads, keep, send = feed_forward_back(second, mid, *grad_feed)
    early, feed_keep, feed_send = early_gradients(
        hidden, grads, mid, *grad_feed, second
    )
    grad_normed_mid, early, feed_keep, feed_send = scatter_pair(keep, send, early, feed_keep, feed_send)
    early_sum = lax.psum_scatter(
        early.reshape(-1, 128), AXES, axis_index_groups=PLANES, scatter_dimension=0, tiled=True
    )

    part_feed_gain = jnp.sum(grad_normed_mid * middle * r2, axis=0)
    z2 = grad_normed_mid * feed_gain
    grad_middle = (
        grad_result + r2 * z2 - middle * (r2 * r2 * r2) * jnp.mean(z2 * middle, axis=-1, keepdims=True)
    )
    grad_mixer_out = (valid_rows * grad_middle).astype(bf16)
    grad_mixer_out, feed_send = tie(grad_mixer_out, feed_send)
    feed_got = move(feed_send, C1)
    grad_mixer_m, left, (feed_keep, feed_send) = gather_line_first(
        grad_mixer_out,
        feed_keep[:rows].astype(f32) + feed_got[:rows].astype(f32),
        add_low(feed_keep[rows:], feed_got[rows:]),
    )
    grads, gain_m, grad_mixer = mixer_backward(
        0, grad_mixer_m, w_mixer, q, k, v, gate, decay, group_own, retained
    )
    left, grads, grad_mixer, feed_send = tie(left, grads, grad_mixer, feed_send)
    grad_mixer_o = gather_line_last(*left)
    grads, gain_o, grad_mixer = mixer_backward(
        1, grad_mixer_o, w_mixer, q, k, v, gate, decay, group_own, retained, (grads, grad_mixer)
    )
    part_group_gain = (gain_m + gain_o).reshape(-1)
    *sent, grads, feed_far = tie(
        *gradient_parts((2,), 2, grads, mixed, normed_group, grad_mixer), grads, move(feed_send, Y1)
    )

    moved = [move(part, pairs) for part, pairs in zip(sent, (Z1, Z3, X1, X3))]
    back, part_mixer_gain = input_gradients(grads, w_mixer, normed_group)
    back, grads = tie(back, grads)
    gains = jnp.concatenate([part_mixer_gain.reshape(-1) / mixer_gain, part_feed_gain])
    *moved, (a1, b1, a3, b3), grads, gains = tie(
        *moved,
        gradient_parts((1, 3), 1, grads, mixed, normed_group, grad_mixer),
        grads,
        gains + move(gains, C1),
    )
    a3, a1, b3, b1, grads, gains = tie(
        *fold(a3, a1, b3, b1, *moved), grads, gains + move(gains, Y1)
    )
    moved = move(a3, Z3), move(a1, Z1), move(b3, X3), move(b1, X1)
    a0, b0 = gradient_parts((0,), 1, grads, mixed, normed_group, grad_mixer)
    result = (middle + valid_rows * (feed_keep + feed_far.astype(f32))).astype(bf16)
    gains = jnp.concatenate([gains, part_group_gain])
    far = move(gains, Y2)
    group_far = far[2 * width :]
    gains = jnp.concatenate(
        [
            gains[: 2 * width] + far[: 2 * width],
            jnp.where(is_low, part_group_gain, group_far),
            jnp.where(is_low, group_far, part_group_gain),
        ]
    )
    back, early_sum, _ = tie(back, early_sum, a0)
    grad_normed_in = lax.psum_scatter(
        back, AXES, axis_index_groups=LINES, scatter_dimension=0, tiled=True
    ).astype(f32)
    r3, r1_, s3, s1, gains, a0, b0 = tie(*moved, gains, a0, b0)
    a, b, gains = tie(*add_blocks((a0, r3, r1_), (b0, s3, s1)), gains + move(gains, X1))
    *moved, gains, g_gelu, g_linear, g_down, result = tie(
        *(move(a[i], (X1, X2, X3)[i - 1]) for i in (1, 2, 3)),
        *(move(b[i], (Z1, Z2, Z3)[i - 1]) for i in (1, 2, 3)),
        gains + move(gains, X2),
        *settle_early(early_sum),
        result,
    )
    for pairs in (Z1, Z2):
        gains = gains + move(gains, pairs)
    z1 = grad_normed_in * mixer_gain
    grad_tokens = (
        grad_middle + r1 * z1 - token_float * (r1 * r1 * r1) * jnp.mean(z1 * token_float, axis=-1, keepdims=True)
    ).astype(bf16)
    sum_a, sum_b = (a[0], *moved[:3]), (b[0], *moved[3:])
    g_output, g_query, g_key, g_value, g_swish = settle_late(
        sum_a, sum_b, (wide, kwide, kwide, wide, wide)
    )

    return (
        result,
        grad_tokens,
        gains[:width],
        gains[width : 2 * width],
        gains[2 * width :],
        g_query,
        g_key,
        g_value,
        g_swish,
        g_output.T,
        g_gelu,
        g_linear,
        g_down.T,
    )


def solution(mesh):
    weight = P("dp", "tensor")
    turned = P("tensor", "dp")
    rows = P(("dp", "tensor"), None)
    return jax.shard_map(
        shards,
        mesh=mesh,
        in_specs=(
            rows,
            P("dp"),
            P("tensor"),
            P(),
            P(),
            P("tensor"),
            weight,
            weight,
            weight,
            weight,
            turned,
            weight,
            weight,
            turned,
            rows,
        ),
        out_specs=(
            rows,
            rows,
            P(),
            P(),
            P("tensor"),
            weight,
            weight,
            weight,
            weight,
            turned,
            weight,
            weight,
            turned,
        ),
        check_vma=False,
    )
```
